32 devices in a mesh: seq: 4 (over y, x), fsdp: 8 (over z, core).
Axes of the slice: x: 2, y: 2, z: 4, core: 2. Of those that a mesh axis runs over, the one named last changes fastest.
Arguments:
- block_input: bfloat16 [8, 1024, 1536], P('fsdp', 'seq'), may hold values from -6 to 6
- cotangent: bfloat16 [8, 1024, 1536], P('fsdp', 'seq'), may hold values from -6 to 6
- routes: int32 [8, 1024, 2], P('fsdp', 'seq'), may hold values from 0 to 3, all different within a row; in each aligned block of 256 rows (0 to 255, 256 to 511, ..., all dimensions but the last counted through in order) at most 192 rows name the same one
- gain_attn: bfloat16 [1536], P(('seq', 'fsdp')), may hold values from 0.099609375 to 1.8984375
- w_query: bfloat16 [1536, 1536], P(('seq', 'fsdp')), may hold values from -0.15625 to 0.15625
- w_key: bfloat16 [1536, 512], P(('seq', 'fsdp')), may hold values from -0.15625 to 0.15625
- w_value: bfloat16 [1536, 512], P(('seq', 'fsdp')), may hold values from -0.15625 to 0.15625
- w_out: bfloat16 [1536, 1536], P(('seq', 'fsdp')), may hold values from -1.75 to 1.75
- gain_ffn: bfloat16 [1536], P(('seq', 'fsdp')), may hold values from 0.099609375 to 1.8984375
- router: bfloat16 [1536, 4], P(('seq', 'fsdp')), may hold values from -0.119628906 to 0.119628906
- w_gate: bfloat16 [4, 1536, 1024], P(None, ('seq', 'fsdp')), may hold values from -0.15625 to 0.15625
- w_up: bfloat16 [4, 1536, 1024], P(None, ('seq', 'fsdp')), may hold values from -0.15625 to 0.15625
- w_down: bfloat16 [4, 1024, 1536], P(None, ('seq', 'fsdp')), may hold values from -0.1875 to 0.1875
Outputs:
- output: bfloat16 [8, 1024, 1536], P('fsdp', 'seq')
- grad_input: bfloat16 [8, 1024, 1536], P('fsdp', 'seq')
- grad_gain_attn: float32 [1536], P(('seq', 'fsdp'))
- grad_w_query: float32 [1536, 1536], P(('seq', 'fsdp'))
- grad_w_key: float32 [1536, 512], P(('seq', 'fsdp'))
- grad_w_value: float32 [1536, 512], P(('seq', 'fsdp'))
- grad_w_out: float32 [1536, 1536], P(('seq', 'fsdp'))
- grad_gain_ffn: float32 [1536], P(('seq', 'fsdp'))
- grad_router: float32 [1536, 4], P(('seq', 'fsdp'))
- grad_w_gate: float32 [4, 1536, 1024], P(None, ('seq', 'fsdp'))
- grad_w_up: float32 [4, 1536, 1024], P(None, ('seq', 'fsdp'))
- grad_w_down: float32 [4, 1024, 1536], P(None, ('seq', 'fsdp'))
The draws below stay inside these ranges and needn't reach their ends.
Inputs may be any that keep to these rules, and one draw needn't show every extreme that they name: `routes`: each row names two different experts. Among the 256 rows of one device (aligned blocks of the sequence and position dimensions taken in order), no expert is named more than 192 times, and in some block one expert is named exactly 192 times.
All inputs are finite; a program needn't handle non-finite values.
Results may differ from the reference program's by a relative error of at most 0.014.
The reference program's roundings to bfloat16 on the way count: a program that leaves them out, or rounds other values in their place, can miss the bound.
Values may be sent and summed in bfloat16 or wider, within the bound.
A program may use at most 256 MiB of HBM per device.

```python
import math
import jax
import jax.numpy as jnp
import numpy as np
from jax import lax

D = 1536
HEADS = 24
KV_HEADS = 8
HEAD_DIM = 64
FF = 1024
EXPERTS = 4
TOK_DEV = 256
LENGTH = 1024
SEQS = 8
CAP = 192


def levels(own_key, shape, pieces, smallest, largest):
    factor_of = 1.0
    for dim, blocks in pieces:
        steps = jax.random.uniform(jax.random.fold_in(jax.random.fold_in(own_key, 6), dim), (blocks,), jnp.float32, smallest / len(pieces), largest / len(pieces))
        factor_of = factor_of * jnp.repeat(jnp.exp(steps), shape[dim] // blocks).reshape((-1,) + (1,) * (len(shape) - 1 - dim))
    return factor_of


def shared_out(key, own, number, rows, count, top, most, slope):
    order = jax.random.permutation(key, count)
    packed, common = load_shares(count, rows * top, most, slope, True), load_shares(count, rows * top, most, slope, False)
    places = jnp.arange(count)

    def named(tallies, offset_by):
        used = int((tallies > 0).sum())
        fixed = max(1, used // 4)
        shifted = fixed + (places - fixed + offset_by * (used - fixed)) % max(1, count - fixed)
        return jnp.zeros((count,), jnp.int32).at[order[jnp.where(places < fixed, places, shifted)]].set(jnp.asarray(tallies, jnp.int32))

    tallies = jnp.where(number % 4 == 0, named(packed, number // 4), named(common, number - number // 4 - 1))
    mixed = jax.random.permutation(jax.random.fold_in(own, 3), count)
    giver, sink = mixed[0:count // 2 * 2:2], mixed[1:count // 2 * 2:2]
    room = jnp.minimum(tallies[giver] - 1, most - tallies[sink]) // 2
    room = jnp.where((giver == order[0]) | (sink == order[0]) | (tallies[sink] == 0), 0, jnp.maximum(room, 0))
    shifted = jax.random.randint(jax.random.fold_in(own, 4), (count // 2,), 0, 1 << 20) % (room + 1)
    tallies = tallies.at[giver].add(-shifted).at[sink].add(shifted)
    items = jnp.searchsorted(jnp.cumsum(tallies), jnp.arange(rows * top), side="right").astype(jnp.int32)
    listing = items.reshape(top, rows).T
    listing = listing[jax.random.permutation(jax.random.fold_in(own, 1), rows)]
    offset_by = jax.random.randint(jax.random.fold_in(own, 2), (rows, 1), 0, top)
    return jnp.take_along_axis(listing, (jnp.arange(top)[None, :] + offset_by) % top, axis=1)


def load_shares(amount, total, reach, slope, full):
    portions = [(1 << 20) // math.isqrt(rank ** slope) + 1 for rank in range(1, amount + 1)]
    largest = reach if full else min(reach, max(-(-total // amount), total * portions[0] // sum(portions)))
    least = 1 if total - largest >= amount - 1 else 0
    holding, spare = [largest] + [least] * (amount - 1), total - largest - least * (amount - 1)
    while spare > 0:
        candidates = [i for i in range(1, amount) if holding[i] < largest] or [i for i in range(1, amount) if holding[i] < reach]
        pool, budget = sum([portions[i] for i in candidates]), spare
        for i in candidates:
            addition = min(reach - holding[i], max(1, budget * portions[i] // pool), spare)
            holding[i] = holding[i] + addition
            spare = spare - addition
    return np.array(holding)


def normal_values(key, extent, scale, limit, split=(), kind=jnp.bfloat16):
    drawn = jax.random.normal(key, extent, jnp.float32) * scale
    if len(split) > 0:
        drawn = levels(key, extent, split, -0.22, 0.18) * drawn
    return jnp.clip(drawn, min=-limit, max=limit).astype(kind)


def setup_inputs(seed: int = 0) -> dict:
    splits = jax.random.split(jax.random.key(seed), 14)
    block_input = normal_values(splits[0], (SEQS, LENGTH, D), 1.0, 6.0, ((0, 8), (1, 4)))
    cotangent = normal_values(splits[1], (SEQS, LENGTH, D), 1.0, 6.0, ((0, 8), (1, 4)))
    routes_keys = jax.random.split(jax.random.fold_in(splits[2], 1), SEQS * LENGTH // TOK_DEV)
    routes_turns = jax.random.permutation(jax.random.fold_in(splits[2], 3), SEQS * LENGTH // TOK_DEV)
    routes = jax.vmap(lambda own, number: shared_out(jax.random.fold_in(splits[2], 2), own, number, TOK_DEV, EXPERTS, 2, CAP, 1))(routes_keys, routes_turns).reshape((SEQS, LENGTH, 2))
    gain_attn = jnp.clip(1.0 + 0.18 * jax.random.normal(splits[3], (D,), jnp.float32), 0.099609375, 1.8984375).astype(jnp.bfloat16)
    w_query = normal_values(splits[4], (D, HEADS * HEAD_DIM), D ** -0.5, 0.15625, ((0, 32),))
    w_key = normal_values(splits[5], (D, KV_HEADS * HEAD_DIM), D ** -0.5, 0.15625, ((0, 32),))
    w_value = normal_values(splits[6], (D, KV_HEADS * HEAD_DIM), D ** -0.5, 0.15625, ((0, 32),))
    w_out = normal_values(splits[7], (HEADS * HEAD_DIM, D), (HEADS * HEAD_DIM // 128) ** -0.5, 1.75, ((0, 32),))
    gain_ffn = jnp.clip(1.0 + 0.18 * jax.random.normal(splits[8], (D,), jnp.float32), 0.099609375, 1.8984375).astype(jnp.bfloat16)
    router = normal_values(splits[9], (D, EXPERTS), 0.02, 0.119628906, ((0, 32),))
    w_gate = normal_values(splits[10], (EXPERTS, D, FF), D ** -0.5, 0.15625, ((1, 32),))
    w_up = normal_values(splits[11], (EXPERTS, D, FF), D ** -0.5, 0.15625, ((1, 32),))
    w_down = normal_values(splits[12], (EXPERTS, FF, D), FF ** -0.5, 0.1875, ((1, 32),))
    return dict(block_input=block_input, cotangent=cotangent, routes=routes, gain_attn=gain_attn, w_query=w_query, w_key=w_key, w_value=w_value, w_out=w_out, gain_ffn=gain_ffn, router=router, w_gate=w_gate, w_up=w_up, w_down=w_down)


eps = 1e-06
exact_precision = lax.Precision.HIGHEST

@jax.custom_vjp
def low(v):
    return lax.optimization_barrier(v.astype(jnp.bfloat16)).astype(jnp.float32)

@jax.custom_vjp
def low_back(v):
    return v

def low_keep(v):
    return (low(v), None)

def low_pass(kept, grad):
    return (grad,)

def back_keep(v):
    return (v, None)

def back_low(kept, grad):
    return (low(grad),)
low.defvjp(low_keep, low_pass)
low_back.defvjp(back_keep, back_low)

def matmul(left, right):
    return jnp.dot(left, right, precision=exact_precision)

def rms_norm(rows, gain):
    factor = lax.rsqrt(lax.optimization_barrier(jnp.mean(rows * rows, axis=-1, keepdims=True)) + eps)
    return rows * factor * gain

def attend(queries, keys, values):
    length = queries.shape[0]
    block_rows = min(512, length)
    block_count = length // block_rows
    score_scale = HEAD_DIM ** (-0.5)
    grouped = queries.reshape(block_count, block_rows, queries.shape[1], queries.shape[2], queries.shape[3])
    positions = jnp.arange(length).astype(jnp.int32)

    def one_block(block_args):
        query_block, first_row = block_args
        scores = low_back(score_scale * jnp.einsum('qgrd,kgd->grqk', query_block, keys, precision=exact_precision))
        row_index = first_row + jnp.arange(block_rows).astype(jnp.int32)
        allowed = positions[None, :] <= row_index[:, None]
        scores = jnp.where(allowed, scores, -1e+30)
        row_max = lax.optimization_barrier(jnp.max(scores, axis=-1, keepdims=True))
        exponent = jnp.exp(scores - row_max)
        probability = exponent / lax.optimization_barrier(jnp.sum(exponent, axis=-1, keepdims=True))
        return jnp.einsum('grqk,kgd->qgrd', low(probability), values, precision=exact_precision)
    starts = (jnp.arange(block_count) * block_rows).astype(jnp.int32)
    result = lax.map(jax.checkpoint(one_block), (grouped, starts))
    return result.reshape(length, -1)

def block_layer(inputs, expert_ids, gain_attn, w_query, w_key, w_value, w_out, gain_ffn, router, w_gate, w_up, w_down):
    length = inputs.shape[0]
    heads_ratio = HEADS // KV_HEADS
    normed1 = low(rms_norm(inputs, gain_attn))
    queries = low_back(low(matmul(normed1, w_query))).reshape(length, KV_HEADS, heads_ratio, HEAD_DIM)
    keys = low_back(low(matmul(normed1, w_key))).reshape(length, KV_HEADS, HEAD_DIM)
    values = low_back(low(matmul(normed1, w_value))).reshape(length, KV_HEADS, HEAD_DIM)
    attn = low_back(low(attend(queries, keys, values)))
    mixed = inputs + low_back(matmul(attn, w_out))
    normed2 = low(rms_norm(mixed, gain_ffn))
    logits = low_back(matmul(normed2, router))
    choose = (expert_ids[:, :, None] == jnp.arange(EXPERTS).astype(jnp.int32)[None, None, :]).astype(inputs.dtype)
    picked = lax.optimization_barrier(jnp.sum(choose * logits[:, None, :], axis=-1))
    gate_values = jax.nn.softmax(picked, axis=-1)
    weighting = lax.optimization_barrier(jnp.sum(choose * gate_values[:, :, None], axis=1))
    mixture = jnp.zeros_like(mixed)
    for expert in range(EXPERTS):
        gate_pre = low_back(matmul(normed2, w_gate[expert]))
        up_pre = low_back(matmul(normed2, w_up[expert]))
        hidden = low(jax.nn.silu(gate_pre) * up_pre)
        expert_out = low_back(matmul(hidden, w_down[expert]))
        mixture = mixture + weighting[:, expert:expert + 1] * expert_out
    return mixed + mixture

def reference(block_input, cotangent, routes, gain_attn, w_query, w_key, w_value, w_out, gain_ffn, router, w_gate, w_up, w_down):
    floats = [item.astype(jnp.float32) for item in (block_input, gain_attn, w_query, w_key, w_value, w_out, gain_ffn, router, w_gate, w_up, w_down)]

    def forward(inputs, *params):
        return lax.map(lambda pair: block_layer(pair[0], pair[1], *params), (inputs, routes))
    output, pullback = jax.vjp(forward, *floats)
    grads = pullback(cotangent.astype(jnp.float32))
    return (output.astype(jnp.bfloat16), grads[0].astype(jnp.bfloat16), grads[1], grads[2], grads[3], grads[4], grads[5], grads[6], grads[7], grads[8], grads[9], grads[10])
```

```python
import jax
import jax.numpy as jnp
from jax import lax
from jax.sharding import PartitionSpec as P

HEADS = 24
KV_HEADS = 8
HEAD_DIM = 64
EPS = 1e-06
SCALE = HEAD_DIM ** (-0.5)
BF = jnp.bfloat16
F32 = jnp.float32


def dot(a, b):
    return jnp.dot(a, b, preferred_element_type=F32)


def dot_t(a, b):
    return lax.dot_general(a, b, (((1,), (1,)), ((), ())), preferred_element_type=F32)


def t_dot(a, b):
    return lax.dot_general(a, b, (((0,), (0,)), ((), ())), preferred_element_type=F32)


def rms_factor(rows):
    return lax.rsqrt(jnp.mean(rows * rows, axis=-1, keepdims=True) + EPS)


def scores_of(q, k):
    length = q.shape[0]
    sc = SCALE * jnp.einsum("qgrd,kgd->grqk", q, k, preferred_element_type=F32)
    pos = jnp.arange(length)
    return jnp.where(pos[None, :] <= pos[:, None], sc, -1e30)


def shards(x, cot, routes, gain_attn, w_query, w_key, w_value, w_out, gain_ffn, router, w_gate, w_up, w_down):
    n_seq = lax.axis_size("seq")
    n_fsdp = lax.axis_size("fsdp")
    rows, d = w_query.shape
    experts, ff_rows, _ = w_down.shape
    ff = w_gate.shape[2]
    fc = ff // n_seq
    toks = x.shape[1]

    extra = jnp.concatenate(
        [gain_attn[:, None], gain_ffn[:, None], router, jnp.zeros((rows, 128 - 2 - experts), BF)], axis=1
    )
    qkv = jnp.concatenate(
        [w_query.reshape(rows, n_seq, -1), w_key.reshape(rows, n_seq, -1), w_value.reshape(rows, n_seq, -1),
         jnp.broadcast_to(extra[:, None], (rows, n_seq, 128))], axis=2,
    )
    gu = jnp.stack([w_gate, w_up]).reshape(2, experts, rows, n_seq, fc).transpose(3, 2, 0, 1, 4)
    gu = gu.reshape(n_seq, rows, 2 * experts * fc)
    qkv = qkv.transpose(1, 0, 2)
    qkv = lax.all_to_all(qkv, "seq", split_axis=0, concat_axis=0, tiled=True)
    gu = lax.all_to_all(gu, "seq", split_axis=0, concat_axis=0, tiled=True)
    do = jnp.concatenate([w_down.reshape(experts * ff_rows, d), w_out], axis=0)
    qkv = lax.all_gather(qkv, "fsdp", axis=1).reshape(d, -1)
    do = lax.all_gather(do, "fsdp", axis=0)
    wo = do[:, experts * ff_rows:].reshape(-1, d)
    wd = do[:, : experts * ff_rows].reshape(n_fsdp, experts, ff_rows, d).transpose(1, 0, 2, 3).reshape(-1, d)
    gu = lax.all_gather(gu, "fsdp", axis=1).reshape(d, -1)

    nq, nk = w_query.shape[1] // n_seq, w_key.shape[1] // n_seq
    nqkv = nq + 2 * nk
    gain_one = qkv[:, nqkv].astype(F32)
    gain_two = qkv[:, nqkv + 1].astype(F32)
    wr = qkv[:, nqkv + 2: nqkv + 2 + experts]
    wqkv = qkv[:, :nqkv]

    xs = lax.all_gather(x[0], "seq", axis=0, tiled=True)
    gs = lax.all_gather(cot[0], "seq", axis=0, tiled=True)
    ids = lax.all_gather(routes[0], "seq", axis=0, tiled=True)
    xf = xs.astype(F32)
    n1 = (xf * rms_factor(xf) * gain_one).astype(BF)
    length = xs.shape[0]
    proj = dot(n1, wqkv).astype(BF)
    q = proj[:, :nq].reshape(length, nk // HEAD_DIM, -1, HEAD_DIM)
    k = proj[:, nq: nq + nk].reshape(length, -1, HEAD_DIM)
    v = proj[:, nq + nk:].reshape(length, -1, HEAD_DIM)
    sc = scores_of(q, k)
    m = jnp.max(sc, axis=-1, keepdims=True)
    e = jnp.exp(sc - m)
    tot = jnp.sum(e, axis=-1, keepdims=True)
    prob = (e / tot).astype(BF)
    lse = m + jnp.log(tot)
    attn = jnp.einsum("grqk,kgd->qgrd", prob, v, preferred_element_type=F32).astype(BF).reshape(length, nq)
    part = dot(attn, wo).astype(BF)
    mine = lax.psum_scatter(part, "seq", scatter_dimension=0, tiled=True)
    xo = x[0].astype(F32)
    mixed = xo + mine.astype(F32)
    r2 = rms_factor(mixed)
    n2o = (mixed * r2 * gain_two).astype(BF)

    n2 = lax.all_gather(n2o, "seq", axis=0, tiled=True)
    logits = dot(n2, wr)
    hot = ids[:, :, None] == jnp.arange(experts)[None, None, :]
    named = jnp.any(hot, axis=1)
    lm = jnp.max(jnp.where(named, logits, -1e30), axis=-1, keepdims=True)
    le = jnp.where(named, jnp.exp(logits - lm), 0.0)
    gates = le / jnp.sum(le, axis=-1, keepdims=True)
    pre = dot(n2, gu)
    gp, up = pre[:, : experts * fc], pre[:, experts * fc:]
    dh0 = dot_t(gs, wd)
    sig = jax.nn.sigmoid(gp)
    act = gp * sig
    hid = (act * up).astype(BF).astype(F32)
    gw = jnp.repeat(gates, fc, axis=1)
    hg = (gw * hid).astype(BF)
    dgate = jnp.sum((hid * dh0).reshape(length, experts, fc), axis=-1)
    dh = gw * dh0
    dgp = (dh * up * sig * (1.0 + gp * (1.0 - sig))).astype(BF)
    dup = (dh * act).astype(BF)
    dpre = jnp.concatenate([dgp, dup], axis=1)
    outp = dot(hg, wd).astype(BF)
    dn2p = dot_t(dpre, gu).astype(BF)
    ggu = t_dot(n2, dpre).astype(BF)
    gwd = t_dot(hg, gs).astype(BF)
    gwd = gwd.reshape(experts, n_fsdp, ff_rows, d).transpose(1, 0, 2, 3).reshape(-1, d)
    gwd = lax.psum_scatter(gwd, "fsdp", scatter_dimension=0, tiled=True)
    ggu = ggu.reshape(n_seq, n_fsdp, rows, -1).transpose(1, 0, 2, 3).reshape(n_fsdp * n_seq * rows, -1)
    ggu = lax.psum_scatter(ggu, "fsdp", scatter_dimension=0, tiled=True).reshape(n_seq, rows, -1)
    ggu = lax.all_to_all(ggu, "seq", split_axis=0, concat_axis=0, tiled=True)

    out = lax.psum_scatter(outp, "seq", scatter_dimension=0, tiled=True)
    output = (mixed + out.astype(F32)).astype(BF)
    dn2 = lax.psum_scatter(dn2p, "seq", scatter_dimension=0, tiled=True).astype(F32)
    dgate = lax.psum_scatter(dgate, "seq", scatter_dimension=0, tiled=True)
    go = lax.dynamic_slice_in_dim(gates, lax.axis_index("seq") * toks, toks, 0)
    dlog = (go * (dgate - jnp.sum(go * dgate, axis=-1, keepdims=True))).astype(BF)
    grouter = t_dot(n2o, dlog)
    dn2 = dn2 + dot_t(dlog, wr)
    up_g = cot[0].astype(F32)
    dn = dn2 * gain_two
    dmixed = up_g + r2 * dn - mixed * r2**3 * jnp.mean(dn * mixed, axis=-1, keepdims=True)
    dprojo = dmixed.astype(BF)

    dproj = lax.all_gather(dprojo, "seq", axis=0, tiled=True)
    gwo = t_dot(attn, dproj).astype(BF)
    gwo = lax.psum_scatter(gwo, "fsdp", scatter_dimension=0, tiled=True)
    dattn = dot_t(dproj, wo).astype(BF).reshape(q.shape)
    prob = jnp.exp(scores_of(q, k) - lse)
    dprob = jnp.einsum("qgrd,kgd->grqk", dattn, v, preferred_element_type=F32)
    delta = jnp.sum(prob * dprob, axis=-1, keepdims=True)
    dsc = (prob * (dprob - delta)).astype(BF)
    dq = SCALE * jnp.einsum("grqk,kgd->qgrd", dsc, k, preferred_element_type=F32)
    dk = SCALE * jnp.einsum("grqk,qgrd->kgd", dsc, q, preferred_element_type=F32)
    dv = jnp.einsum("grqk,qgrd->kgd", prob.astype(BF), dattn, preferred_element_type=F32)
    dqkv = jnp.concatenate(
        [dq.astype(BF).reshape(length, -1), dk.astype(BF).reshape(length, -1), dv.astype(BF).reshape(length, -1)], axis=1
    )
    dn1p = dot_t(dqkv, wqkv).astype(BF)
    gqkv = t_dot(n1, dqkv).astype(BF)
    ghi = grouter.astype(BF)
    glo = (grouter - ghi.astype(F32)).astype(BF)
    gqkv = jnp.concatenate([gqkv, ghi, glo, jnp.zeros((d, 128 - 2 * experts), BF)], axis=1)
    gqkv = gqkv.reshape(n_seq, n_fsdp, rows, -1).transpose(1, 0, 2, 3).reshape(n_fsdp * n_seq * rows, -1)
    gqkv = lax.psum_scatter(gqkv, "fsdp", scatter_dimension=0, tiled=True).reshape(n_seq, rows, -1)
    gqkv = lax.all_to_all(gqkv, "seq", split_axis=0, concat_axis=0, tiled=True)
    dn1 = lax.psum_scatter(dn1p, "seq", scatter_dimension=0, tiled=True).astype(F32)
    r1 = rms_factor(xo)
    dg1 = dn1 * gain_one
    gin = dmixed + r1 * dg1 - xo * r1**3 * jnp.mean(dg1 * xo, axis=-1, keepdims=True)

    gqkv = gqkv.astype(F32)
    g_query = gqkv[:, :, :nq].transpose(1, 0, 2).reshape(rows, -1)
    g_key = gqkv[:, :, nq: nq + nk].transpose(1, 0, 2).reshape(rows, -1)
    g_value = gqkv[:, :, nq + nk: nqkv].transpose(1, 0, 2).reshape(rows, -1)
    g_router = jnp.sum(gqkv[:, :, nqkv: nqkv + experts] + gqkv[:, :, nqkv + experts: nqkv + 2 * experts], axis=0)
    ggu = ggu.astype(F32).reshape(n_seq, rows, 2, experts, fc).transpose(2, 3, 1, 0, 4).reshape(2, experts, rows, ff)
    g_gate, g_up = ggu[0], ggu[1]
    g_gain_one = (
        jnp.sum(w_query.astype(F32) * g_query, axis=1) + jnp.sum(w_key.astype(F32) * g_key, axis=1)
        + jnp.sum(w_value.astype(F32) * g_value, axis=1)
    ) / gain_attn.astype(F32)
    g_gain_two = (
        jnp.sum(w_gate.astype(F32) * g_gate + w_up.astype(F32) * g_up, axis=(0, 2))
        + jnp.sum(router.astype(F32) * g_router, axis=1)
    ) / gain_ffn.astype(F32)
    return (
        output[None], gin.astype(BF)[None], g_gain_one, g_query, g_key, g_value, gwo.astype(F32), g_gain_two, g_router,
        g_gate, g_up, gwd.astype(F32).reshape(experts, ff_rows, d),
    )


def solution(mesh):
    tok = P("fsdp", "seq", None)
    vec = P(("seq", "fsdp"))
    mat = P(("seq", "fsdp"), None)
    exp = P(None, ("seq", "fsdp"), None)
    return jax.shard_map(
        shards,
        mesh=mesh,
        in_specs=(tok, tok, tok, vec, mat, mat, mat, mat, vec, mat, exp, exp, exp),
        out_specs=(tok, tok, vec, mat, mat, mat, mat, vec, mat, exp, exp, exp),
        check_vma=False,
    )
```

```python
import functools

import jax
import jax.numpy as jnp
from jax import lax
from jax.experimental import pallas as pl
from jax.experimental.pallas import tpu as pltpu
from jax.sharding import PartitionSpec as P

HEAD_DIM = 64
EPS = 1e-06
SCALE = HEAD_DIM ** (-0.5)
BF = jnp.bfloat16
F32 = jnp.float32
MESH = pl.DeviceIdType.MESH
ANY = pl.BlockSpec(memory_space=pl.ANY)
VM = pl.BlockSpec(memory_space=pltpu.VMEM)
MIB = 2**20


def dot(a, b):
    return jnp.dot(a, b, preferred_element_type=F32)


def dot_t(a, b):
    return lax.dot_general(a, b, (((1,), (1,)), ((), ())), preferred_element_type=F32)


def t_dot(a, b):
    return lax.dot_general(a, b, (((0,), (0,)), ((), ())), preferred_element_type=F32)


def rms_factor(rows):
    return lax.rsqrt(jnp.mean(rows * rows, axis=-1, keepdims=True) + EPS)


def partner(me, step):
    return ((me // 2 + step // 2) % 2) * 2 + (me % 2 + step % 2) % 2


def send(src, dst, sems, slot, peer):
    return pltpu.make_async_remote_copy(
        src_ref=src, dst_ref=dst, send_sem=sems.at[0, slot], recv_sem=sems.at[1, slot],
        device_id={"seq": peer}, device_id_type=MESH,
    )


def greet(me):
    barrier = pltpu.get_barrier_semaphore()
    for step in (1, 2, 3):
        pl.semaphore_signal(barrier, inc=1, device_id={"seq": partner(me, step)}, device_id_type=MESH)
    pl.semaphore_wait(barrier, 3)


class Gather:
    def __init__(self, me, own, buf, sems, base=0):
        rows = own.shape[0]
        half = rows // 2
        one, two = partner(me, 1), partner(me, 2)

        def part(owner, start, size):
            return buf.at[pl.ds(pl.multiple_of(owner * rows + start, half), size)]

        mine = part(me, 0, rows)
        self.first = send(own, mine, sems, base, one)
        self.second = send(own, mine, sems, base + 1, two)
        onward = part(one, 0, half)
        self.third = send(onward, onward, sems, base + 2, two)
        onward = part(two, half, half)
        self.fourth = send(onward, onward, sems, base + 3, one)

    def start(self):
        self.first.start()
        self.second.start()

    def got_one(self):
        self.first.wait_recv()
        self.third.start()

    def got_two(self):
        self.second.wait_recv()
        self.fourth.start()

    def got_three(self):
        self.third.wait_recv()
        self.fourth.wait_recv()

    def finish(self):
        for copy in (self.first, self.second, self.third, self.fourth):
            copy.wait_send()


def lanes(shape):
    return lax.broadcasted_iota(jnp.int32, shape, len(shape) - 1)


def pack_two(value, experts):
    high = value.astype(BF).astype(F32)
    low = value - high
    return jnp.where(lanes(value.shape) < experts, high, pltpu.roll(low, experts, 1)).astype(BF)


def front_kernel(
    nq, nk, experts, x_ref, g_ref, gain_ref, named_ref, wqkv_ref, wo_ref, wr_ref,
    n1_ref, qkv_ref, attn_ref, lse_ref, mixed_ref, n2_ref, gate_ref, gs_ref,
    xs_ref, send_ref, recv_ref, xsem, gsem, asem, lsem,
):
    me = lax.axis_index("seq")
    toks = x_ref.shape[0]
    group = nq // nk
    greet(me)
    xg = Gather(me, x_ref, xs_ref, xsem)
    xg.start()
    keep = pltpu.make_async_copy(g_ref, gs_ref.at[pl.ds(pl.multiple_of(me * toks, toks), toks)], lsem)
    keep.start()
    gg = Gather(me, g_ref, gs_ref, gsem)
    gain1 = gain_ref[0:1, :]

    @pl.loop(0, 4)
    def _(step):
        block = partner(me, step)
        rows = pl.ds(pl.multiple_of(block * toks, toks), toks)

        @pl.when(step == 0)
        def _():
            xs_ref[rows, :] = x_ref[...]

        @pl.when(step == 1)
        def _():
            xg.got_one()

        @pl.when(step == 2)
        def _():
            xg.got_two()

        @pl.when(step == 3)
        def _():
            xg.got_three()
            gg.start()

        xf = xs_ref[rows, :].astype(F32)
        n1_ref[rows, :] = (xf * rms_factor(xf) * gain1).astype(BF)
        proj = dot(n1_ref[rows, :], wqkv_ref[...]).astype(BF)
        qkv_ref[rows, :] = proj

    @pl.loop(0, 4)
    def _(turn):
        step = 3 - turn
        block = partner(me, step)
        rows = pl.ds(pl.multiple_of(block * toks, toks), toks)

        @pl.when(turn == 2)
        def _():
            gg.got_one()
            gg.got_two()

        for b in range(4):

            @pl.when(block == b)
            def _(b=b):
                upto = b * toks
                qrows = slice(upto, upto + toks)
                inside = lanes((toks, toks)) <= lax.broadcasted_iota(jnp.int32, (toks, toks), 0)
                for h in range(nq // HEAD_DIM):
                    g = h // group
                    q = qkv_ref[qrows, h * HEAD_DIM:(h + 1) * HEAD_DIM] * SCALE
                    kc = slice(nq + g * HEAD_DIM, nq + (g + 1) * HEAD_DIM)
                    vc = slice(nq + nk + g * HEAD_DIM, nq + nk + (g + 1) * HEAD_DIM)
                    near = jnp.where(inside, dot_t(q, qkv_ref[qrows, kc]), -1e30)
                    top = jnp.max(near, axis=-1, keepdims=True)
                    if b:
                        far = dot_t(q, qkv_ref[0:upto, kc])
                        top = jnp.maximum(top, jnp.max(far, axis=-1, keepdims=True))
                    near = jnp.exp(near - top)
                    total = jnp.sum(near, axis=-1, keepdims=True)
                    if b:
                        far = jnp.exp(far - top)
                        total = total + jnp.sum(far, axis=-1, keepdims=True)
                    inv = 1.0 / total
                    res = dot((near * inv).astype(BF), qkv_ref[qrows, vc])
                    if b:
                        res = res + dot((far * inv).astype(BF), qkv_ref[0:upto, vc])
                    attn_ref[qrows, h * HEAD_DIM:(h + 1) * HEAD_DIM] = res.astype(BF)
                    lse_ref[qrows, h:h + 1] = top + jnp.log(total)

        send_ref[step] = dot(attn_ref[rows, :], wo_ref[...]).astype(BF)

        @pl.when(step > 0)
        def _():
            send(send_ref.at[step], recv_ref.at[step], asem, step, block).start()

    mixed = x_ref[...].astype(F32) + send_ref[0].astype(F32)
    for step in (1, 2, 3):
        send(send_ref.at[step], recv_ref.at[step], asem, step, partner(me, step)).wait_recv()
        mixed = mixed + recv_ref[step].astype(F32)
    mixed_ref[...] = mixed
    n2 = (mixed * rms_factor(mixed) * gain_ref[1:2, :]).astype(BF)
    n2_ref[:, 0:n2.shape[1]] = n2
    logits = dot(n2, wr_ref[...])
    named = named_ref[...] > 0.0
    top = jnp.max(jnp.where(named, logits, -1e30), axis=-1, keepdims=True)
    weight = jnp.where(named, jnp.exp(jnp.minimum(logits - top, 0.0)), 0.0)
    gates = weight / jnp.sum(weight, axis=-1, keepdims=True)
    gate_ref[...] = gates
    n2_ref[:, n2.shape[1]:] = pack_two(gates, experts)
    gg.got_three()
    gg.finish()
    xg.finish()
    keep.wait()
    for step in (1, 2, 3):
        send(send_ref.at[step], recv_ref.at[step], asem, step, partner(me, step)).wait_send()


def front(nq, nk, experts, x, g, gains, named, wqkv, wo, wr):
    toks, d = x.shape
    length = 4 * toks
    sds = jax.ShapeDtypeStruct
    return pl.pallas_call(
        functools.partial(front_kernel, nq, nk, experts),
        name="front",
        out_shape=(
            sds((length, d), BF), sds((length, nq + 2 * nk), BF), sds((length, nq), BF), sds((length, 128), F32),
            sds((toks, d), F32), sds((toks, d + 128), BF), sds((toks, 128), F32), sds((length, d), BF),
        ),
        in_specs=[VM] * 7,
        out_specs=[VM] * 8,
        scratch_shapes=[
            pltpu.VMEM((length, d), BF), pltpu.VMEM((4, toks, d), BF), pltpu.VMEM((4, toks, d), BF),
            pltpu.SemaphoreType.DMA((2, 4)), pltpu.SemaphoreType.DMA((2, 4)), pltpu.SemaphoreType.DMA((2, 4)),
            pltpu.SemaphoreType.DMA,
        ],
        compiler_params=pltpu.CompilerParams(collective_id=1, has_side_effects=True, vmem_limit_bytes=56 * MIB),
        cost_estimate=pl.CostEstimate(flops=20 * 10**9, bytes_accessed=60 * 10**6, transcendentals=4 * 10**6),
    )(x, g, gains, named, wqkv, wo, wr)


def middle_kernel(
    experts, n2o_ref, gs_ref, gate_ref, mixed_ref, gain_ref, gu_hbm, wd_hbm, wr_ref,
    ggu_ref, gwd_ref, outp_ref, dmixed_ref, dproj_ref, grouter_ref,
    n2_ref, gu_ref, wd_ref, dpre_ref, hg_ref, send_ref, recv_ref, nsem, dsem, lsem,
):
    me = lax.axis_index("seq")
    toks, de = n2o_ref.shape
    d = de - 128
    ff = wd_ref.shape[0]
    fc = ff // experts
    load_gu = pltpu.make_async_copy(gu_hbm, gu_ref, lsem.at[0])
    load_wd = pltpu.make_async_copy(wd_hbm, wd_ref, lsem.at[1])
    load_gu.start()
    load_wd.start()
    greet(me)
    ng = Gather(me, n2o_ref, n2_ref, nsem)
    ng.start()
    load_gu.wait()
    load_wd.wait()

    @pl.loop(0, 4)
    def _(step):
        block = partner(me, step)
        rows = pl.ds(pl.multiple_of(block * toks, toks), toks)

        @pl.when(step == 0)
        def _():
            n2_ref[rows, :] = n2o_ref[...]

        @pl.when(step == 1)
        def _():
            ng.got_one()

        @pl.when(step == 2)
        def _():
            ng.got_two()

        @pl.when(step == 3)
        def _():
            ng.got_three()

        send_ref[step, :, d:] = jnp.zeros((toks, 128), BF)

        def one_expert(e, dgate):
            cols = pl.ds(pl.multiple_of(e * 2 * fc, 2 * fc), 2 * fc)
            hcols = pl.ds(pl.multiple_of(e * fc, fc), fc)
            pre = dot(n2_ref[rows, 0:d], gu_ref[:, cols])
            dh0 = dot_t(gs_ref[rows, :], wd_ref[hcols, :])
            packed = n2_ref[rows, d:].astype(F32)
            lane = lanes(packed.shape)
            mine = (lane == e) | (lane == e + experts)
            gate = jnp.sum(jnp.where(mine, packed, 0.0), axis=-1, keepdims=True)
            gp, up = pre[:, 0:fc], pre[:, fc:]
            sig = 1.0 / (1.0 + jnp.exp(-gp))
            act = gp * sig
            hid = (act * up).astype(BF).astype(F32)
            hg_ref[rows, hcols] = (gate * hid).astype(BF)
            dh = gate * dh0
            dpre_ref[rows, pl.ds(pl.multiple_of(e * 2 * fc, fc), fc)] = (
                dh * up * sig * (1.0 + gp * (1.0 - sig))).astype(BF)
            dpre_ref[rows, pl.ds(pl.multiple_of(e * 2 * fc + fc, fc), fc)] = (dh * act).astype(BF)
            return dgate + jnp.where(lane == e, jnp.sum(hid * dh0, axis=-1, keepdims=True), 0.0)

        dgate = lax.fori_loop(0, experts, one_expert, jnp.zeros((toks, 128), F32))
        send_ref[step, :, d:] = pack_two(dgate, experts)
        tile = 512

        @pl.loop(0, d // tile)
        def _(t):
            cols = pl.ds(pl.multiple_of(t * tile, tile), tile)
            send_ref[step, :, cols] = dot_t(dpre_ref[rows, :], gu_ref[cols, :]).astype(BF)

        @pl.when(step > 0)
        def _():
            send(send_ref.at[step], recv_ref.at[step], dsem, step, block).start()

        @pl.loop(0, d // tile)
        def _(t):
            cols = pl.ds(pl.multiple_of(t * tile, tile), tile)
            outp_ref[step, :, cols] = dot(hg_ref[rows, :], wd_ref[:, cols]).astype(BF)

    @pl.loop(0, d // 256)
    def _(t):
        cols = pl.ds(pl.multiple_of(t * 256, 256), 256)
        ggu_ref[cols, :] = t_dot(n2_ref[:, cols], dpre_ref[...]).astype(BF)

    @pl.loop(0, ff // 256)
    def _(t):
        cols = pl.ds(pl.multiple_of(t * 256, 256), 256)
        gwd_ref[cols, :] = t_dot(hg_ref[:, cols], gs_ref[...]).astype(BF)

    total = send_ref[0].astype(F32)
    for step in (1, 2, 3):
        send(send_ref.at[step], recv_ref.at[step], dsem, step, partner(me, step)).wait_recv()
        total = total + recv_ref[step].astype(F32)
    both = total[:, d:]
    lane = lanes(both.shape)
    dgate = jnp.where(lane < experts, both + pltpu.roll(both, 128 - experts, 1), 0.0)
    gates = gate_ref[...]
    dlog = (gates * (dgate - jnp.sum(gates * dgate, axis=-1, keepdims=True))).astype(BF)
    grouter_ref[...] = pack_two(t_dot(n2o_ref[:, 0:d], dlog), experts)
    dn = (total[:, 0:d] + dot_t(dlog, wr_ref[...])) * gain_ref[1:2, :]
    mixed = mixed_ref[...]
    r2 = rms_factor(mixed)
    own = gs_ref[pl.ds(pl.multiple_of(me * toks, toks), toks), :].astype(F32)
    dmixed = own + r2 * dn - mixed * (r2 * r2 * r2) * jnp.mean(dn * mixed, axis=-1, keepdims=True)
    dmixed_ref[...] = dmixed
    dproj_ref[...] = dmixed.astype(BF)
    ng.finish()
    for step in (1, 2, 3):
        send(send_ref.at[step], recv_ref.at[step], dsem, step, partner(me, step)).wait_send()


def middle(experts, n2o, gs, gates, mixed, gains, gu, wd, wr):
    toks, de = n2o.shape
    d = de - 128
    length = 4 * toks
    ff = wd.shape[0]
    sds = jax.ShapeDtypeStruct
    return pl.pallas_call(
        functools.partial(middle_kernel, experts),
        name="middle",
        out_shape=(
            sds((d, 2 * ff), BF), sds((ff, d), BF), sds((4, toks, d), BF), sds((toks, d), F32), sds((toks, d), BF),
            sds((d, 128), BF),
        ),
        in_specs=[VM] * 5 + [ANY] * 2 + [VM],
        out_specs=[VM] * 6,
        scratch_shapes=[
            pltpu.VMEM((length, de), BF), pltpu.VMEM((d, 2 * ff), BF), pltpu.VMEM((ff, d), BF),
            pltpu.VMEM((length, 2 * ff), BF), pltpu.VMEM((length, ff), BF),
            pltpu.VMEM((4, toks, de), BF), pltpu.VMEM((4, toks, de), BF),
            pltpu.SemaphoreType.DMA((2, 4)), pltpu.SemaphoreType.DMA((2, 4)), pltpu.SemaphoreType.DMA((2,)),
        ],
        compiler_params=pltpu.CompilerParams(collective_id=2, has_side_effects=True, vmem_limit_bytes=62 * MIB),
        cost_estimate=pl.CostEstimate(flops=60 * 10**9, bytes_accessed=80 * 10**6, transcendentals=4 * 10**6),
    )(n2o, gs, gates, mixed, gains, gu, wd, wr)


def back_kernel(
    nq, nk, x_ref, mixed_ref, dmixed_ref, dprojo_ref, gain_ref, n1_ref, qkv_ref, attn_ref, lse_ref, outp_ref,
    grouter_ref, wqkv_ref, wo_ref,
    out_ref, gin_ref, gqkv_ref, gwo_ref,
    dproj_ref, dattn_ref, dqkv_ref, dk_ref, dv_ref, send_ref, recv_ref, orecv_ref, psem, dsem, osem,
):
    me = lax.axis_index("seq")
    toks, d = x_ref.shape
    group = nq // nk
    greet(me)
    pg = Gather(me, dprojo_ref, dproj_ref, psem)
    pg.start()

    @pl.loop(0, 4)
    def _(step):
        block = partner(me, step)
        rows = pl.ds(pl.multiple_of(block * toks, toks), toks)

        @pl.when(step == 0)
        def _():
            dproj_ref[rows, :] = dprojo_ref[...]

        @pl.when(step == 1)
        def _():
            pg.got_one()

        @pl.when(step == 2)
        def _():
            pg.got_two()

        @pl.when(step == 3)
        def _():
            pg.got_three()

        dattn_ref[rows, :] = dot_t(dproj_ref[rows, :], wo_ref[...]).astype(BF)

    for step in (3, 2, 1):
        send(outp_ref.at[step], orecv_ref.at[step], osem, step, partner(me, step)).start()

    dk_ref[...] = jnp.zeros_like(dk_ref)
    dv_ref[...] = jnp.zeros_like(dv_ref)
    for b in range(4):
        upto = b * toks
        qrows = slice(upto, upto + toks)
        inside = lanes((toks, toks)) <= lax.broadcasted_iota(jnp.int32, (toks, toks), 0)
        for h in range(nq // HEAD_DIM):
            g = h // group
            hc = slice(h * HEAD_DIM, (h + 1) * HEAD_DIM)
            gc = slice(g * HEAD_DIM, (g + 1) * HEAD_DIM)
            q = qkv_ref[qrows, hc] * SCALE
            da = dattn_ref[qrows, hc]
            lse = lse_ref[qrows, h:h + 1]
            parts = ([slice(0, upto)] if b else []) + [qrows]
            probs, dprobs = [], []
            delta = 0.0
            for krows in parts:
                k = qkv_ref[krows, nq + g * HEAD_DIM: nq + (g + 1) * HEAD_DIM]
                v = qkv_ref[krows, nq + nk + g * HEAD_DIM: nq + nk + (g + 1) * HEAD_DIM]
                p = jnp.exp(dot_t(q, k) - lse)
                if krows is qrows:
                    p = jnp.where(inside, p, 0.0)
                dp = dot_t(da, v)
                delta = delta + jnp.sum(p * dp, axis=-1, keepdims=True)
                probs.append(p)
                dprobs.append(dp)
            dq = 0.0
            for krows, p, dp in zip(parts, probs, dprobs):
                k = qkv_ref[krows, nq + g * HEAD_DIM: nq + (g + 1) * HEAD_DIM]
                ds = (p * (dp - delta)).astype(BF)
                dq = dq + dot(ds, k)
                dk_ref[krows, gc] += t_dot(ds, q)
                dv_ref[krows, gc] += t_dot(p.astype(BF), da)
            dqkv_ref[qrows, hc] = (dq * SCALE).astype(BF)
    dqkv_ref[:, nq:nq + nk] = dk_ref[...].astype(BF)
    dqkv_ref[:, nq + nk:] = dv_ref[...].astype(BF)

    @pl.loop(0, 4)
    def _(turn):
        step = 3 - turn
        block = partner(me, step)
        rows = pl.ds(pl.multiple_of(block * toks, toks), toks)
        send_ref[step] = dot_t(dqkv_ref[rows, :], wqkv_ref[...]).astype(BF)

        @pl.when(step > 0)
        def _():
            send(send_ref.at[step], recv_ref.at[step], dsem, step, block).start()

    @pl.loop(0, d // 256)
    def _(t):
        cols = pl.ds(pl.multiple_of(t * 256, 256), 256)
        gqkv_ref[cols, 0:nq + 2 * nk] = t_dot(n1_ref[:, cols], dqkv_ref[...]).astype(BF)

    gqkv_ref[:, nq + 2 * nk:] = grouter_ref[...]

    @pl.loop(0, nq // 128)
    def _(t):
        cols = pl.ds(pl.multiple_of(t * 128, 128), 128)
        gwo_ref[cols, :] = t_dot(attn_ref[:, cols], dproj_ref[...]).astype(BF)

    out = mixed_ref[...] + outp_ref[0].astype(F32)
    for step in (1, 2, 3):
        send(outp_ref.at[step], orecv_ref.at[step], osem, step, partner(me, step)).wait_recv()
        out = out + orecv_ref[step].astype(F32)
    out_ref[...] = out.astype(BF)
    dn = send_ref[0].astype(F32)
    for step in (1, 2, 3):
        send(send_ref.at[step], recv_ref.at[step], dsem, step, partner(me, step)).wait_recv()
        dn = dn + recv_ref[step].astype(F32)
    dn = dn * gain_ref[0:1, :]
    xf = x_ref[...].astype(F32)
    r1 = rms_factor(xf)
    gin_ref[...] = (
        dmixed_ref[...] + r1 * dn - xf * (r1 * r1 * r1) * jnp.mean(dn * xf, axis=-1, keepdims=True)).astype(BF)
    pg.finish()
    for step in (1, 2, 3):
        send(send_ref.at[step], recv_ref.at[step], dsem, step, partner(me, step)).wait_send()
        send(outp_ref.at[step], orecv_ref.at[step], osem, step, partner(me, step)).wait_send()


def back(nq, nk, x, mixed, dmixed, dproj, gains, n1, qkv, attn, lse, outp, grouter, wqkv, wo):
    toks, d = x.shape
    length = 4 * toks
    sds = jax.ShapeDtypeStruct
    return pl.pallas_call(
        functools.partial(back_kernel, nq, nk),
        name="back",
        out_shape=(
            sds((toks, d), BF), sds((toks, d), BF), sds((d, nq + 2 * nk + 128), BF), sds((nq, d), BF),
        ),
        in_specs=[VM] * 13,
        out_specs=[VM] * 4,
        scratch_shapes=[
            pltpu.VMEM((length, d), BF), pltpu.VMEM((length, nq), BF), pltpu.VMEM((length, nq + 2 * nk), BF),
            pltpu.VMEM((length, nk), F32), pltpu.VMEM((length, nk), F32),
            pltpu.VMEM((4, toks, d), BF), pltpu.VMEM((4, toks, d), BF), pltpu.VMEM((4, toks, d), BF),
            pltpu.SemaphoreType.DMA((2, 4)), pltpu.SemaphoreType.DMA((2, 4)), pltpu.SemaphoreType.DMA((2, 4)),
        ],
        compiler_params=pltpu.CompilerParams(collective_id=3, has_side_effects=True, vmem_limit_bytes=62 * MIB),
        cost_estimate=pl.CostEstimate(flops=40 * 10**9, bytes_accessed=60 * 10**6, transcendentals=4 * 10**6),
    )(x, mixed, dmixed, dproj, gains, n1, qkv, attn, lse, outp, grouter, wqkv, wo)


def shards(x, cot, routes, gain_attn, w_query, w_key, w_value, w_out, gain_ffn, router, w_gate, w_up, w_down):
    n_seq = lax.axis_size("seq")
    n_fsdp = lax.axis_size("fsdp")
    rows, d = w_query.shape
    experts, ff_rows, _ = w_down.shape
    ff = w_gate.shape[2]
    fc = ff // n_seq

    extra = jnp.concatenate(
        [gain_attn[:, None], gain_ffn[:, None], router, jnp.zeros((rows, 128 - 2 - experts), BF)], axis=1
    )
    qkv = jnp.concatenate(
        [w_query.reshape(rows, n_seq, -1), w_key.reshape(rows, n_seq, -1), w_value.reshape(rows, n_seq, -1),
         jnp.broadcast_to(extra[:, None], (rows, n_seq, 128))], axis=2,
    )
    gu = jnp.stack([w_gate, w_up]).reshape(2, experts, rows, n_seq, fc).transpose(3, 2, 1, 0, 4)
    gu = gu.reshape(n_seq, rows, 2 * experts * fc)
    qkv = qkv.transpose(1, 0, 2)
    qkv = lax.all_to_all(qkv, "seq", split_axis=0, concat_axis=0, tiled=True)
    gu = lax.all_to_all(gu, "seq", split_axis=0, concat_axis=0, tiled=True)
    do = jnp.concatenate([w_down.reshape(experts * ff_rows, d), w_out], axis=0)
    qkv = lax.all_gather(qkv, "fsdp", axis=1).reshape(d, -1)
    do = lax.all_gather(do, "fsdp", axis=0)
    wo = do[:, experts * ff_rows:].reshape(-1, d)
    wd = do[:, : experts * ff_rows].reshape(n_fsdp, experts, ff_rows, d).transpose(1, 0, 2, 3).reshape(-1, d)
    gu = lax.all_gather(gu, "fsdp", axis=1).reshape(d, -1)

    nq, nk = w_query.shape[1] // n_seq, w_key.shape[1] // n_seq
    nqkv = nq + 2 * nk
    wqkv = qkv[:, :nqkv]
    gains = qkv[:, nqkv: nqkv + 8].T.astype(F32)
    wr = jnp.pad(qkv[:, nqkv + 2: nqkv + 2 + experts], ((0, 0), (0, 128 - experts)))
    hot = routes[0][:, :, None] == jnp.arange(128)[None, None, :]
    named = jnp.any(hot, axis=1).astype(F32)

    n1, proj, attn, lse, mixed, n2o, gates, gs = front(nq, nk, experts, x[0], cot[0], gains, named, wqkv, wo, wr)
    ggu, gwd, outp, dmixed, dproj, grouter = middle(experts, n2o, gs, gates, mixed, gains, gu, wd, wr)
    gwd = gwd.reshape(experts, n_fsdp, ff_rows, d).transpose(1, 0, 2, 3).reshape(-1, d)
    gwd = lax.psum_scatter(gwd, "fsdp", scatter_dimension=0, tiled=True)
    ggu = ggu.reshape(n_seq, n_fsdp, rows, -1).transpose(1, 0, 2, 3).reshape(n_fsdp * n_seq * rows, -1)
    ggu = lax.psum_scatter(ggu, "fsdp", scatter_dimension=0, tiled=True).reshape(n_seq, rows, -1)
    ggu = lax.all_to_all(ggu, "seq", split_axis=0, concat_axis=0, tiled=True)
    output, gin, gqkv, gwo = back(
        nq, nk, x[0], mixed, dmixed, dproj, gains, n1, proj, attn, lse, outp, grouter, wqkv, wo)
    gwo = lax.psum_scatter(gwo, "fsdp", scatter_dimension=0, tiled=True)
    gqkv = gqkv.reshape(n_seq, n_fsdp, rows, -1).transpose(1, 0, 2, 3).reshape(n_fsdp * n_seq * rows, -1)
    gqkv = lax.psum_scatter(gqkv, "fsdp", scatter_dimension=0, tiled=True).reshape(n_seq, rows, -1)
    gqkv = lax.all_to_all(gqkv, "seq", split_axis=0, concat_axis=0, tiled=True)

    gqkv = gqkv.astype(F32)
    g_query = gqkv[:, :, :nq].transpose(1, 0, 2).reshape(rows, -1)
    g_key = gqkv[:, :, nq: nq + nk].transpose(1, 0, 2).reshape(rows, -1)
    g_value = gqkv[:, :, nq + nk: nqkv].transpose(1, 0, 2).reshape(rows, -1)
    g_router = jnp.sum(gqkv[:, :, nqkv: nqkv + experts] + gqkv[:, :, nqkv + experts: nqkv + 2 * experts], axis=0)
    ggu = ggu.astype(F32).reshape(n_seq, rows, experts, 2, fc).transpose(3, 2, 1, 0, 4).reshape(2, experts, rows, ff)
    g_gate, g_up = ggu[0], ggu[1]
    g_gain_one = (
        jnp.sum(w_query.astype(F32) * g_query, axis=1) + jnp.sum(w_key.astype(F32) * g_key, axis=1)
        + jnp.sum(w_value.astype(F32) * g_value, axis=1)
    ) / gain_attn.astype(F32)
    g_gain_two = (
        jnp.sum(w_gate.astype(F32) * g_gate + w_up.astype(F32) * g_up, axis=(0, 2))
        + jnp.sum(router.astype(F32) * g_router, axis=1)
    ) / gain_ffn.astype(F32)
    return (
        output[None], gin[None], g_gain_one, g_query, g_key, g_value, gwo.astype(F32), g_gain_two, g_router,
        g_gate, g_up, gwd.astype(F32).reshape(experts, ff_rows, d),
    )


def solution(mesh):
    tok = P("fsdp", "seq", None)
    vec = P(("seq", "fsdp"))
    mat = P(("seq", "fsdp"), None)
    exp = P(None, ("seq", "fsdp"), None)
    return jax.shard_map(
        shards,
        mesh=mesh,
        in_specs=(tok, tok, tok, vec, mat, mat, mat, mat, vec, mat, exp, exp, exp),
        out_specs=(tok, tok, vec, mat, mat, mat, mat, vec, mat, exp, exp, exp),
        check_vma=False,
    )
```

```python
import functools

import jax
import jax.numpy as jnp
from jax import lax
from jax.experimental import pallas as pl
from jax.experimental.pallas import tpu as pltpu
from jax.sharding import PartitionSpec as P

HEAD_DIM = 64
EPS = 1e-06
SCALE = HEAD_DIM ** (-0.5)
BF = jnp.bfloat16
F32 = jnp.float32
MESH = pl.DeviceIdType.MESH
ANY = pl.BlockSpec(memory_space=pl.ANY)
VM = pl.BlockSpec(memory_space=pltpu.VMEM)
MIB = 2**20


def dot(a, b):
    return jnp.dot(a, b, preferred_element_type=F32)


def dot_t(a, b):
    return lax.dot_general(a, b, (((1,), (1,)), ((), ())), preferred_element_type=F32)


def t_dot(a, b):
    return lax.dot_general(a, b, (((0,), (0,)), ((), ())), preferred_element_type=F32)


def rms_factor(rows):
    return lax.rsqrt(jnp.mean(rows * rows, axis=-1, keepdims=True) + EPS)


def partner(me, step):
    return ((me // 2 + step // 2) % 2) * 2 + (me % 2 + step % 2) % 2


def send(src, dst, sems, slot, peer):
    return pltpu.make_async_remote_copy(
        src_ref=src, dst_ref=dst, send_sem=sems.at[0, slot], recv_sem=sems.at[1, slot],
        device_id={"seq": peer}, device_id_type=MESH,
    )


def greet(me, others):
    barrier = pltpu.get_barrier_semaphore()
    for step in (1, 2, 3):
        pl.semaphore_signal(barrier, inc=1, device_id={"seq": partner(me, step)}, device_id_type=MESH)
    pl.semaphore_wait(barrier, 3 + others)


class Gather:
    def __init__(self, me, own, buf, sems, base=0):
        rows = own.shape[0]
        half = rows // 2
        one, two = partner(me, 1), partner(me, 2)

        def part(owner, start, size):
            return buf.at[pl.ds(pl.multiple_of(owner * rows + start, half), size)]

        mine = part(me, 0, rows)
        self.first = send(own, mine, sems, base, one)
        self.second = send(own, mine, sems, base + 1, two)
        onward = part(one, 0, half)
        self.third = send(onward, onward, sems, base + 2, two)
        onward = part(two, half, half)
        self.fourth = send(onward, onward, sems, base + 3, one)

    def start(self):
        self.first.start()
        self.second.start()

    def got_one(self):
        self.first.wait_recv()
        self.third.start()

    def got_two(self):
        self.second.wait_recv()
        self.fourth.start()

    def got_three(self):
        self.third.wait_recv()
        self.fourth.wait_recv()

    def finish(self):
        for copy in (self.first, self.second, self.third, self.fourth):
            copy.wait_send()


def lanes(shape):
    return lax.broadcasted_iota(jnp.int32, shape, len(shape) - 1)


def pack_two(value, experts):
    high = value.astype(BF).astype(F32)
    low = value - high
    return jnp.where(lanes(value.shape) < experts, high, pltpu.roll(low, experts, 1)).astype(BF)


class Line:
    def __init__(self, region, sems):
        me = lax.axis_index("fsdp")
        self.last = lax.axis_size("fsdp") // 2 - 1
        self.z, self.core = me // 2, me % 2
        self.region, self.sems = region, sems

    def copy(self, slot, plane, core, target):
        part = self.region(plane * 2 + core)
        return pltpu.make_async_remote_copy(
            src_ref=part, dst_ref=part, send_sem=self.sems.at[0, slot], recv_sem=self.sems.at[1, slot],
            device_id={"fsdp": target}, device_id_type=MESH,
        )

    def up(self, hop):
        return self.copy(hop, self.z - hop, self.core, (self.z + 1) * 2 + self.core)

    def from_below(self, hop):
        return self.copy(hop, self.z - 1 - hop, self.core, self.z * 2 + self.core)

    def down(self, hop):
        return self.copy(3 + hop, self.z + hop, self.core, (self.z - 1) * 2 + self.core)

    def from_above(self, hop):
        return self.copy(3 + hop, self.z + 1 + hop, self.core, self.z * 2 + self.core)

    def across(self, plane):
        return self.copy(6 + plane, plane, self.core, self.z * 2 + 1 - self.core)

    def from_across(self, plane):
        return self.copy(6 + plane, plane, 1 - self.core, self.z * 2 + self.core)

    def start(self):
        pl.when(self.z < self.last)(lambda: self.up(0).start())
        pl.when(self.z > 0)(lambda: self.down(0).start())
        self.across(self.z).start()

    def step(self, hop):
        @pl.when(self.z > hop)
        def _():
            self.from_below(hop).wait_recv()
            if hop < 2:
                pl.when(self.z < self.last)(lambda: self.up(hop + 1).start())
            self.across(self.z - 1 - hop).start()

        @pl.when(self.z + hop < self.last)
        def _():
            self.from_above(hop).wait_recv()
            if hop < 2:
                pl.when(self.z > 0)(lambda: self.down(hop + 1).start())
            self.across(self.z + 1 + hop).start()

    def land(self):
        for plane in range(4):
            self.from_across(plane).wait_recv()

    def finish(self):
        for hop in range(3):
            pl.when((self.z >= hop) & (self.z < self.last))(lambda hop=hop: self.up(hop).wait_send())
            pl.when((self.z + hop <= self.last) & (self.z > 0))(lambda hop=hop: self.down(hop).wait_send())
        for plane in range(4):
            self.across(plane).wait_send()


def greet_line():
    me = lax.axis_index("fsdp")
    last = lax.axis_size("fsdp") // 2 - 1
    z, core = me // 2, me % 2
    barrier = pltpu.get_barrier_semaphore()

    @pl.when(z < last)
    def _():
        pl.semaphore_signal(barrier, inc=1, device_id={"fsdp": me + 2}, device_id_type=MESH)

    @pl.when(z > 0)
    def _():
        pl.semaphore_signal(barrier, inc=1, device_id={"fsdp": me - 2}, device_id_type=MESH)

    pl.semaphore_signal(barrier, inc=1, device_id={"fsdp": z * 2 + 1 - core}, device_id_type=MESH)
    return 1 + jnp.minimum(z, 1) + jnp.minimum(last - z, 1)


class Spread:
    def __init__(self, me, own, buf, shard, sems, local):
        self.copies = [
            send(own.at[partner(me, step)], buf.at[me, shard], sems, step, partner(me, step)) for step in (3, 2, 1)
        ]
        self.local = pltpu.make_async_copy(own.at[me], buf.at[me, shard], local)

    def start(self):
        self.local.start()
        for copy in self.copies:
            copy.start()

    def got(self):
        self.local.wait()
        for copy in self.copies:
            copy.wait_recv()

    def finish(self):
        for copy in self.copies:
            copy.wait_send()


def front_kernel(nq, nk, experts, inside, *refs):
    if inside:
        (x_ref, g_ref, named_ref, qkvo_ref, guo_ref, wdo_ref, woo_ref,
         n1_ref, qkv_ref, attn_ref, lse_ref, mixed_ref, n2_ref, gate_ref, gs_ref, gain_ref, ext_ref, wqkv_ref, wo_ref,
         gu_ref, wd_ref,
         xs_ref, send_ref, recv_ref, xsem, gsem, asem, lsem, qw_ref, spread_sem, line_sem) = refs
    else:
        (x_ref, g_ref, named_ref, wqkv_ref, wo_ref,
         n1_ref, qkv_ref, attn_ref, lse_ref, mixed_ref, n2_ref, gate_ref, gs_ref, gain_ref, ext_ref,
         xs_ref, send_ref, recv_ref, xsem, gsem, asem, lsem) = refs
    me = lax.axis_index("seq")
    toks, d = x_ref.shape
    group = nq // nk
    nqkv = nq + 2 * nk
    xg = Gather(me, x_ref, xs_ref, xsem)
    gg = Gather(me, g_ref, gs_ref, gsem)
    keep = pltpu.make_async_copy(g_ref, gs_ref.at[pl.ds(pl.multiple_of(me * toks, toks), toks)], lsem.at[0])
    keep.start()
    if inside:
        shard = lax.axis_index("fsdp")
        rows = woo_ref.shape[0]
        greet(me, greet_line())
        qkv_line = Line(lambda f: qw_ref.at[:, f], line_sem.at[0])
        wo_line = Line(lambda f: wo_ref.at[pl.ds(pl.multiple_of(f * rows, 16), rows)], line_sem.at[1])
        wd_line = Line(lambda f: wd_ref.at[:, f], line_sem.at[2])
        gu_line = Line(lambda f: gu_ref.at[:, f], line_sem.at[3])
        qkv_spread = Spread(me, qkvo_ref, qw_ref, shard, spread_sem.at[0], lsem.at[1])
        gu_spread = Spread(me, guo_ref, gu_ref, shard, spread_sem.at[1], lsem.at[2])
        place_wo = pltpu.make_async_copy(woo_ref, wo_line.region(shard), lsem.at[3])
        place_wd = pltpu.make_async_copy(wdo_ref, wd_line.region(shard), lsem.at[4])
        qkv_spread.start()
        place_wo.start()
        place_wd.start()
        xg.start()
        gu_spread.start()
        place_wo.wait()
        place_wd.wait()
        qkv_spread.got()
        qkv_line.start()
        wd_line.start()
        wo_line.start()
        xs_ref[pl.ds(pl.multiple_of(me * toks, toks), toks), :] = x_ref[...]
        qkv_line.step(0)
        gu_spread.got()
        gu_line.start()
        qkv_line.step(1)
        xg.got_one()
        xg.got_two()
        wd_line.step(0)
        wo_line.step(0)
        qkv_line.step(2)
        wo_line.step(1)
        wo_line.step(2)
        wd_line.step(1)
        xg.got_three()
        gg.start()
        qkv_line.land()
        for s in range(4):
            for f in range(8):
                wqkv_ref[s * 8 * rows + f * rows: s * 8 * rows + (f + 1) * rows, :] = qw_ref[s, f]
        wo_line.land()
    else:
        greet(me, 0)
        xg.start()
        xs_ref[pl.ds(pl.multiple_of(me * toks, toks), toks), :] = x_ref[...]
        xg.got_one()
        xg.got_two()
        xg.got_three()
        gg.start()
    ext = wqkv_ref[:, nqkv:]
    ext_ref[...] = ext
    gain_ref[...] = ext.astype(F32).T[experts:experts + 2, :]
    gain1 = gain_ref[0:1, :]

    @pl.loop(0, 4)
    def _(block):
        rows = pl.ds(pl.multiple_of(block * toks, toks), toks)
        xf = xs_ref[rows, :].astype(F32)
        n1_ref[rows, :] = (xf * rms_factor(xf) * gain1).astype(BF)
        proj = dot(n1_ref[rows, :], wqkv_ref[:, 0:nqkv]).astype(BF)
        qkv_ref[rows, :] = proj

    if inside:
        wd_line.step(2)
        gu_line.step(0)

    @pl.loop(0, 4)
    def _(turn):
        step = 3 - turn
        block = partner(me, step)
        rows = pl.ds(pl.multiple_of(block * toks, toks), toks)

        @pl.when(turn == 2)
        def _():
            gg.got_one()
            gg.got_two()
            if inside:
                gu_line.step(1)

        for b in range(4):

            @pl.when(block == b)
            def _(b=b):
                upto = b * toks
                qrows = slice(upto, upto + toks)
                inside = lanes((toks, toks)) <= lax.broadcasted_iota(jnp.int32, (toks, toks), 0)
                for h in range(nq // HEAD_DIM):
                    g = h // group
                    q = qkv_ref[qrows, h * HEAD_DIM:(h + 1) * HEAD_DIM] * SCALE
                    kc = slice(nq + g * HEAD_DIM, nq + (g + 1) * HEAD_DIM)
                    vc = slice(nq + nk + g * HEAD_DIM, nq + nk + (g + 1) * HEAD_DIM)
                    near = jnp.where(inside, dot_t(q, qkv_ref[qrows, kc]), -1e30)
                    top = jnp.max(near, axis=-1, keepdims=True)
                    if b:
                        far = dot_t(q, qkv_ref[0:upto, kc])
                        top = jnp.maximum(top, jnp.max(far, axis=-1, keepdims=True))
                    near = jnp.exp(near - top)
                    total = jnp.sum(near, axis=-1, keepdims=True)
                    if b:
                        far = jnp.exp(far - top)
                        total = total + jnp.sum(far, axis=-1, keepdims=True)
                    inv = 1.0 / total
                    res = dot((near * inv).astype(BF), qkv_ref[qrows, vc])
                    if b:
                        res = res + dot((far * inv).astype(BF), qkv_ref[0:upto, vc])
                    attn_ref[qrows, h * HEAD_DIM:(h + 1) * HEAD_DIM] = res.astype(BF)
                    lse_ref[qrows, h:h + 1] = top + jnp.log(total)

        send_ref[step] = dot(attn_ref[rows, :], wo_ref[...]).astype(BF)

        @pl.when(step > 0)
        def _():
            send(send_ref.at[step], recv_ref.at[step], asem, step, block).start()

    mixed = x_ref[...].astype(F32) + send_ref[0].astype(F32)
    for step in (1, 2, 3):
        send(send_ref.at[step], recv_ref.at[step], asem, step, partner(me, step)).wait_recv()
        mixed = mixed + recv_ref[step].astype(F32)
    if inside:
        gu_line.step(2)
    mixed_ref[...] = mixed
    n2 = (mixed * rms_factor(mixed) * gain_ref[1:2, :]).astype(BF)
    n2_ref[:, 0:d] = n2
    logits = dot(n2, ext_ref[...])
    named = named_ref[...] > 0.0
    top = jnp.max(jnp.where(named, logits, -1e30), axis=-1, keepdims=True)
    weight = jnp.where(named, jnp.exp(jnp.minimum(logits - top, 0.0)), 0.0)
    gates = weight / jnp.sum(weight, axis=-1, keepdims=True)
    gate_ref[...] = gates
    n2_ref[:, d:] = pack_two(gates, experts)
    gg.got_three()
    gg.finish()
    xg.finish()
    keep.wait()
    for step in (1, 2, 3):
        send(send_ref.at[step], recv_ref.at[step], asem, step, partner(me, step)).wait_send()
    if inside:
        wd_line.land()
        gu_line.land()
        for line in (qkv_line, wo_line, wd_line, gu_line):
            line.finish()
        qkv_spread.finish()
        gu_spread.finish()


def front(nq, nk, experts, x, g, named, weights, inside):
    toks, d = x.shape
    length = 4 * toks
    nqkv = nq + 2 * nk
    sds = jax.ShapeDtypeStruct
    out_shape = [
        sds((length, d), BF), sds((length, nqkv), BF), sds((length, nq), BF), sds((length, 128), F32),
        sds((toks, d), F32), sds((toks, d + 128), BF), sds((toks, 128), F32), sds((length, d), BF),
        sds((2, d), F32), sds((d, 128), BF),
    ]
    in_specs = [VM] * 5
    out_specs = [VM] * 10
    scratch = [
        pltpu.VMEM((length, d), BF), pltpu.VMEM((4, toks, d), BF), pltpu.VMEM((4, toks, d), BF),
        pltpu.SemaphoreType.DMA((2, 4)), pltpu.SemaphoreType.DMA((2, 4)), pltpu.SemaphoreType.DMA((2, 4)),
        pltpu.SemaphoreType.DMA((5,)),
    ]
    if inside:
        qkvo, guo, wdo, woo = weights
        in_specs = [VM] * 4 + [ANY] * 3
        out_shape += [
            sds((d, nqkv + 128), BF), sds((nq, d), BF), sds((4, 8) + guo.shape[1:], BF),
            sds((wdo.shape[0], 8) + wdo.shape[1:], BF),
        ]
        out_specs += [VM, VM, ANY, ANY]
        scratch += [
            pltpu.VMEM((4, 8) + qkvo.shape[1:], BF), pltpu.SemaphoreType.DMA((2, 2, 4)),
            pltpu.SemaphoreType.DMA((4, 2, 10)),
        ]
    return pl.pallas_call(
        functools.partial(front_kernel, nq, nk, experts, inside),
        name="front",
        out_shape=out_shape,
        in_specs=in_specs,
        out_specs=out_specs,
        scratch_shapes=scratch,
        compiler_params=pltpu.CompilerParams(collective_id=1, has_side_effects=True, vmem_limit_bytes=60 * MIB),
        cost_estimate=pl.CostEstimate(flops=20 * 10**9, bytes_accessed=60 * 10**6, transcendentals=4 * 10**6),
    )(x, g, named, *weights)


def moe_kernel(experts, shards, *refs):
    (n2o_ref, gs_ref, gu_hbm, wd_hbm) = refs[:4]
    if shards:
        grad_ref, refs = refs[4], refs[5:]
    else:
        ggu_ref, gwd_ref, refs = refs[4], refs[5], refs[6:]
    dn2_ref, hg_ref, n2_ref, gu_ref, wd_ref, dpre_ref, nsem, lsem = refs
    me = lax.axis_index("seq")
    toks, de = n2o_ref.shape
    d = de - 128
    ff = wd_ref.shape[0]
    fc = ff // experts
    load_gu = pltpu.make_async_copy(gu_hbm, gu_ref, lsem.at[0])
    load_wd = pltpu.make_async_copy(wd_hbm, wd_ref, lsem.at[1])
    load_gu.start()
    load_wd.start()
    greet(me, 0)
    ng = Gather(me, n2o_ref, n2_ref, nsem)
    ng.start()
    load_gu.wait()
    load_wd.wait()

    @pl.loop(0, 4)
    def _(step):
        block = partner(me, step)
        rows = pl.ds(pl.multiple_of(block * toks, toks), toks)

        @pl.when(step == 0)
        def _():
            n2_ref[rows, :] = n2o_ref[...]

        @pl.when(step == 1)
        def _():
            ng.got_one()

        @pl.when(step == 2)
        def _():
            ng.got_two()

        @pl.when(step == 3)
        def _():
            ng.got_three()

        def one_expert(e, dgate):
            cols = pl.ds(pl.multiple_of(e * 2 * fc, 2 * fc), 2 * fc)
            hcols = pl.ds(pl.multiple_of(e * fc, fc), fc)
            pre = dot(n2_ref[rows, 0:d], gu_ref[:, cols])
            dh0 = dot_t(gs_ref[rows, :], wd_ref[hcols, :])
            packed = n2_ref[rows, d:].astype(F32)
            lane = lanes(packed.shape)
            mine = (lane == e) | (lane == e + experts)
            gate = jnp.sum(jnp.where(mine, packed, 0.0), axis=-1, keepdims=True)
            gp, up = pre[:, 0:fc], pre[:, fc:]
            sig = 1.0 / (1.0 + jnp.exp(-gp))
            act = gp * sig
            hid = (act * up).astype(BF).astype(F32)
            hg_ref[rows, hcols] = (gate * hid).astype(BF)
            dh = gate * dh0
            dpre_ref[rows, pl.ds(pl.multiple_of(e * 2 * fc, fc), fc)] = (
                dh * up * sig * (1.0 + gp * (1.0 - sig))).astype(BF)
            dpre_ref[rows, pl.ds(pl.multiple_of(e * 2 * fc + fc, fc), fc)] = (dh * act).astype(BF)
            return dgate + jnp.where(lane == e, jnp.sum(hid * dh0, axis=-1, keepdims=True), 0.0)

        dgate = lax.fori_loop(0, experts, one_expert, jnp.zeros((toks, 128), F32))
        dn2_ref[step, :, d:] = pack_two(dgate, experts)
        tile = 512

        @pl.loop(0, d // tile)
        def _(t):
            cols = pl.ds(pl.multiple_of(t * tile, tile), tile)
            dn2_ref[step, :, cols] = dot_t(dpre_ref[rows, :], gu_ref[cols, :]).astype(BF)

    if shards:
        rows, wide = d // 4 // shards, 2 * fc

        @pl.loop(0, 4)
        def _(s):
            cols = pl.ds(pl.multiple_of(s * (d // 4), 128), d // 4)
            grad = t_dot(n2_ref[:, cols], dpre_ref[...]).astype(BF)
            for f in range(shards):
                for e in range(experts):
                    at = pl.ds(pl.multiple_of((s * experts + e) * rows, 16), rows)
                    grad_ref[f, at, :] = grad[f * rows:(f + 1) * rows, e * wide:(e + 1) * wide]

        lower = fc // shards
        parts = d // wide

        @pl.loop(0, experts)
        def _(e):
            cols = pl.ds(pl.multiple_of(e * fc, fc), fc)
            grad = t_dot(hg_ref[:, cols], gs_ref[...]).astype(BF)
            for f in range(shards):
                for c in range(parts):
                    at = pl.ds(pl.multiple_of(4 * experts * rows + (e * parts + c) * lower, 16), lower)
                    grad_ref[f, at, :] = grad[f * lower:(f + 1) * lower, c * wide:(c + 1) * wide]

    else:

        @pl.loop(0, d // 256)
        def _(t):
            cols = pl.ds(pl.multiple_of(t * 256, 256), 256)
            ggu_ref[cols, :] = t_dot(n2_ref[:, cols], dpre_ref[...]).astype(BF)

        @pl.loop(0, ff // 256)
        def _(t):
            cols = pl.ds(pl.multiple_of(t * 256, 256), 256)
            gwd_ref[cols, :] = t_dot(hg_ref[:, cols], gs_ref[...]).astype(BF)

    ng.finish()


def moe(experts, shards, n2o, gs, gu, wd):
    toks, de = n2o.shape
    d = de - 128
    length = 4 * toks
    ff = wd.shape[0]
    sds = jax.ShapeDtypeStruct
    wide = 2 * ff // experts
    if shards:
        grads = [sds((shards, 3 * ff * d // wide // shards, wide), BF)]
    else:
        grads = [sds((d, 2 * ff), BF), sds((ff, d), BF)]
    return pl.pallas_call(
        functools.partial(moe_kernel, experts, shards),
        name="moe",
        out_shape=grads + [sds((4, toks, de), BF), sds((length, ff), BF)],
        in_specs=[VM] * 2 + [ANY] * 2,
        out_specs=[VM] * (2 + len(grads)),
        scratch_shapes=[
            pltpu.VMEM((length, de), BF), pltpu.VMEM((d, 2 * ff), BF), pltpu.VMEM((ff, d), BF),
            pltpu.VMEM((length, 2 * ff), BF),
            pltpu.SemaphoreType.DMA((2, 4)), pltpu.SemaphoreType.DMA((2,)),
        ],
        compiler_params=pltpu.CompilerParams(collective_id=2, has_side_effects=True, vmem_limit_bytes=62 * MIB),
        cost_estimate=pl.CostEstimate(flops=40 * 10**9, bytes_accessed=80 * 10**6, transcendentals=4 * 10**6),
    )(n2o, gs, gu, wd)


def rest_kernel(nq, nk, experts, shards, *refs):
    (x_ref, g_ref, mixed_ref, gate_ref, n2o_ref, gain_ref, ext_ref, n1_ref, qkv_ref, attn_ref, lse_ref, wqkv_ref, wo_ref,
     dn2_ref, hg_ref, wd_ref) = refs[:16]
    out_ref, gin_ref = refs[16:18]
    if shards:
        grad_ref, refs = refs[18], refs[19:]
    else:
        gqkv_ref, gwo_ref, refs = refs[18], refs[19], refs[20:]
    (dmixed_ref, dproj_ref, dattn_ref, dqkv_ref, dk_ref, dv_ref, outp_ref, grouter_ref, send_ref, nrecv_ref, recv_ref,
     orecv_ref, nsem, psem, dsem, osem) = refs
    me = lax.axis_index("seq")
    toks, d = x_ref.shape
    group = nq // nk
    nqkv = nq + 2 * nk
    own = pl.ds(pl.multiple_of(me * toks, toks), toks)
    greet(me, 0)
    for step in (3, 2, 1):
        send(dn2_ref.at[step], nrecv_ref.at[step], nsem, step, partner(me, step)).start()

    @pl.loop(0, 4)
    def _(step):
        rows = pl.ds(pl.multiple_of(partner(me, step) * toks, toks), toks)
        outp_ref[step] = dot(hg_ref[rows, :], wd_ref[...]).astype(BF)

    total = dn2_ref[0].astype(F32)
    for step in (1, 2, 3):
        send(dn2_ref.at[step], nrecv_ref.at[step], nsem, step, partner(me, step)).wait_recv()
        total = total + nrecv_ref[step].astype(F32)
    both = total[:, d:]
    lane = lanes(both.shape)
    dgate = jnp.where(lane < experts, both + pltpu.roll(both, 128 - experts, 1), 0.0)
    gates = gate_ref[...]
    dlog = (gates * (dgate - jnp.sum(gates * dgate, axis=-1, keepdims=True))).astype(BF)
    dn = (total[:, 0:d] + dot_t(dlog, ext_ref[...])) * gain_ref[1:2, :]
    mixed = mixed_ref[...]
    r2 = rms_factor(mixed)
    dmixed = (
        g_ref[...].astype(F32) + r2 * dn - mixed * (r2 * r2 * r2) * jnp.mean(dn * mixed, axis=-1, keepdims=True))
    dmixed_ref[...] = dmixed
    dproj_ref[own, :] = dmixed.astype(BF)
    pg = Gather(me, dproj_ref.at[own], dproj_ref, psem)
    pg.start()
    grouter_ref[...] = pack_two(t_dot(n2o_ref[:, 0:d], dlog), experts)

    @pl.loop(0, 4)
    def _(step):
        rows = pl.ds(pl.multiple_of(partner(me, step) * toks, toks), toks)

        @pl.when(step == 1)
        def _():
            pg.got_one()

        @pl.when(step == 2)
        def _():
            pg.got_two()

        @pl.when(step == 3)
        def _():
            pg.got_three()

        dattn_ref[rows, :] = dot_t(dproj_ref[rows, :], wo_ref[...]).astype(BF)

    for step in (3, 2, 1):
        send(outp_ref.at[step], orecv_ref.at[step], osem, step, partner(me, step)).start()

    if shards:
        narrow = nqkv + 128
        part = nq // shards
        grad = t_dot(attn_ref[...], dproj_ref[...]).astype(BF)
        for f in range(shards):
            for c in range(d // narrow):
                at = 4 * (d // 4 // shards) + c * part
                grad_ref[f, at:at + part, :] = grad[f * part:(f + 1) * part, c * narrow:(c + 1) * narrow]
    else:

        @pl.loop(0, nq // 128)
        def _(t):
            cols = pl.ds(pl.multiple_of(t * 128, 128), 128)
            gwo_ref[cols, :] = t_dot(attn_ref[:, cols], dproj_ref[...]).astype(BF)

    dk_ref[...] = jnp.zeros_like(dk_ref)
    dv_ref[...] = jnp.zeros_like(dv_ref)
    for b in range(4):
        upto = b * toks
        qrows = slice(upto, upto + toks)
        inside = lanes((toks, toks)) <= lax.broadcasted_iota(jnp.int32, (toks, toks), 0)
        for h in range(nq // HEAD_DIM):
            g = h // group
            hc = slice(h * HEAD_DIM, (h + 1) * HEAD_DIM)
            gc = slice(g * HEAD_DIM, (g + 1) * HEAD_DIM)
            q = qkv_ref[qrows, hc] * SCALE
            da = dattn_ref[qrows, hc]
            lse = lse_ref[qrows, h:h + 1]
            parts = ([slice(0, upto)] if b else []) + [qrows]
            probs, dprobs = [], []
            delta = 0.0
            for krows in parts:
                k = qkv_ref[krows, nq + g * HEAD_DIM: nq + (g + 1) * HEAD_DIM]
                v = qkv_ref[krows, nq + nk + g * HEAD_DIM: nq + nk + (g + 1) * HEAD_DIM]
                p = jnp.exp(dot_t(q, k) - lse)
                if krows is qrows:
                    p = jnp.where(inside, p, 0.0)
                dp = dot_t(da, v)
                delta = delta + jnp.sum(p * dp, axis=-1, keepdims=True)
                probs.append(p)
                dprobs.append(dp)
            dq = 0.0
            for krows, p, dp in zip(parts, probs, dprobs):
                k = qkv_ref[krows, nq + g * HEAD_DIM: nq + (g + 1) * HEAD_DIM]
                ds = (p * (dp - delta)).astype(BF)
                dq = dq + dot(ds, k)
                dk_ref[krows, gc] += t_dot(ds, q)
                dv_ref[krows, gc] += t_dot(p.astype(BF), da)
            dqkv_ref[qrows, hc] = (dq * SCALE).astype(BF)
    dqkv_ref[:, nq:nq + nk] = dk_ref[...].astype(BF)
    dqkv_ref[:, nq + nk:] = dv_ref[...].astype(BF)

    @pl.loop(0, 4)
    def _(turn):
        step = 3 - turn
        block = partner(me, step)
        rows = pl.ds(pl.multiple_of(block * toks, toks), toks)
        send_ref[step] = dot_t(dqkv_ref[rows, :], wqkv_ref[:, 0:nqkv]).astype(BF)

        @pl.when(step > 0)
        def _():
            send(send_ref.at[step], recv_ref.at[step], dsem, step, block).start()

    if shards:
        part = d // 4 // shards

        @pl.loop(0, 4)
        def _(s):
            cols = pl.ds(pl.multiple_of(s * (d // 4), 128), d // 4)
            at = pl.ds(pl.multiple_of(s * part, 16), part)
            grad = t_dot(n1_ref[:, cols], dqkv_ref[...]).astype(BF)
            for f in range(shards):
                grad_ref[f, at, 0:nqkv] = grad[f * part:(f + 1) * part, :]
                of = pl.ds(pl.multiple_of(s * (d // 4) + f * part, 16), part)
                grad_ref[f, at, nqkv:] = grouter_ref[of, :]

    else:

        @pl.loop(0, d // 256)
        def _(t):
            cols = pl.ds(pl.multiple_of(t * 256, 256), 256)
            gqkv_ref[cols, 0:nqkv] = t_dot(n1_ref[:, cols], dqkv_ref[...]).astype(BF)

        gqkv_ref[:, nqkv:] = grouter_ref[...]

    out = mixed_ref[...] + outp_ref[0].astype(F32)
    for step in (1, 2, 3):
        send(outp_ref.at[step], orecv_ref.at[step], osem, step, partner(me, step)).wait_recv()
        out = out + orecv_ref[step].astype(F32)
    out_ref[...] = out.astype(BF)
    dn = send_ref[0].astype(F32)
    for step in (1, 2, 3):
        send(send_ref.at[step], recv_ref.at[step], dsem, step, partner(me, step)).wait_recv()
        dn = dn + recv_ref[step].astype(F32)
    dn = dn * gain_ref[0:1, :]
    xf = x_ref[...].astype(F32)
    r1 = rms_factor(xf)
    gin_ref[...] = (
        dmixed_ref[...] + r1 * dn - xf * (r1 * r1 * r1) * jnp.mean(dn * xf, axis=-1, keepdims=True)).astype(BF)
    pg.finish()
    for step in (1, 2, 3):
        send(dn2_ref.at[step], nrecv_ref.at[step], nsem, step, partner(me, step)).wait_send()
        send(send_ref.at[step], recv_ref.at[step], dsem, step, partner(me, step)).wait_send()
        send(outp_ref.at[step], orecv_ref.at[step], osem, step, partner(me, step)).wait_send()


def rest(nq, nk, experts, shards, *args):
    toks, d = args[0].shape
    length = 4 * toks
    nqkv = nq + 2 * nk
    sds = jax.ShapeDtypeStruct
    if shards:
        narrow = nqkv + 128
        grads = [sds((shards, d // shards + d // narrow * (nq // shards), narrow), BF)]
    else:
        grads = [sds((d, nqkv + 128), BF), sds((nq, d), BF)]
    sems = pltpu.SemaphoreType.DMA((2, 4))
    return pl.pallas_call(
        functools.partial(rest_kernel, nq, nk, experts, shards),
        name="rest",
        out_shape=[sds((toks, d), BF), sds((toks, d), BF)] + grads,
        in_specs=[VM] * 16,
        out_specs=[VM] * (2 + len(grads)),
        scratch_shapes=[
            pltpu.VMEM((toks, d), F32), pltpu.VMEM((length, d), BF), pltpu.VMEM((length, nq), BF),
            pltpu.VMEM((length, nqkv), BF), pltpu.VMEM((length, nk), F32), pltpu.VMEM((length, nk), F32),
            pltpu.VMEM((4, toks, d), BF), pltpu.VMEM((d, 128), BF), pltpu.VMEM((4, toks, d), BF),
            pltpu.VMEM((4, toks, d + 128), BF), pltpu.VMEM((4, toks, d), BF), pltpu.VMEM((4, toks, d), BF),
            sems, sems, sems, sems,
        ],
        compiler_params=pltpu.CompilerParams(collective_id=3, has_side_effects=True, vmem_limit_bytes=62 * MIB),
        cost_estimate=pl.CostEstimate(flops=60 * 10**9, bytes_accessed=80 * 10**6, transcendentals=4 * 10**6),
    )(*args)


def shards(x, cot, routes, gain_attn, w_query, w_key, w_value, w_out, gain_ffn, router, w_gate, w_up, w_down):
    n_seq = lax.axis_size("seq")
    n_fsdp = lax.axis_size("fsdp")
    rows, d = w_query.shape
    experts, ff_rows, _ = w_down.shape
    ff = w_gate.shape[2]
    fc = ff // n_seq

    nq, nk = w_query.shape[1] // n_seq, w_key.shape[1] // n_seq
    nqkv = nq + 2 * nk
    inside = n_seq == 4 and n_fsdp == 8 and rows % 16 == 0 and ff_rows % 16 == 0

    extra = jnp.concatenate(
        [router, gain_attn[:, None], gain_ffn[:, None], jnp.zeros((rows, 128 - 2 - experts), BF)], axis=1
    )
    qkv = jnp.concatenate(
        [w_query.reshape(rows, n_seq, -1), w_key.reshape(rows, n_seq, -1), w_value.reshape(rows, n_seq, -1),
         jnp.broadcast_to(extra[:, None], (rows, n_seq, 128))], axis=2,
    ).transpose(1, 0, 2)
    gu = jnp.stack([w_gate, w_up]).reshape(2, experts, rows, n_seq, fc).transpose(3, 2, 1, 0, 4)
    gu = gu.reshape(n_seq, rows, 2 * experts * fc)
    hot = routes[0][:, :, None] == jnp.arange(128)[None, None, :]
    named = jnp.any(hot, axis=1).astype(F32)
    if inside:
        (n1, proj, attn, lse, mixed, n2o, gates, gs, gains, ext, wqkv, wo, gu, wd) = front(
            nq, nk, experts, x[0], cot[0], named, (qkv, gu, w_down, w_out), True)
        gu = gu.reshape(d, -1)
        wd = wd.reshape(-1, d)
    else:
        qkv = lax.all_to_all(qkv, "seq", split_axis=0, concat_axis=0, tiled=True)
        gu = lax.all_to_all(gu, "seq", split_axis=0, concat_axis=0, tiled=True)
        do = jnp.concatenate([w_down.reshape(experts * ff_rows, d), w_out], axis=0)
        wqkv = lax.all_gather(qkv, "fsdp", axis=1).reshape(d, -1)
        do = lax.all_gather(do, "fsdp", axis=0)
        wo = do[:, experts * ff_rows:].reshape(-1, d)
        wd = do[:, : experts * ff_rows].reshape(n_fsdp, experts, ff_rows, d).transpose(1, 0, 2, 3).reshape(-1, d)
        gu = lax.all_gather(gu, "fsdp", axis=1).reshape(d, -1)
        (n1, proj, attn, lse, mixed, n2o, gates, gs, gains, ext) = front(
            nq, nk, experts, x[0], cot[0], named, (wqkv, wo), False)

    packed = n_fsdp if inside else 0
    *grads, dn2, hg = moe(experts, packed, n2o, gs, gu, wd)
    if inside:
        grad = lax.psum_scatter(grads[0], "fsdp", scatter_dimension=0, tiled=True)[0]
    else:
        ggu, gwd = grads
        gwd = gwd.reshape(experts, n_fsdp, ff_rows, d).transpose(1, 0, 2, 3).reshape(-1, d)
        gwd = lax.psum_scatter(gwd, "fsdp", scatter_dimension=0, tiled=True)
        ggu = ggu.reshape(n_seq, n_fsdp, rows, experts, 2 * fc).transpose(1, 0, 3, 2, 4)
        ggu = lax.psum_scatter(ggu, "fsdp", scatter_dimension=0, tiled=True).reshape(n_seq, experts * rows, 2 * fc)
    output, gin, *tail = rest(
        nq, nk, experts, packed, x[0], cot[0], mixed, gates, n2o, gains, ext, n1, proj, attn, lse, wqkv, wo, dn2, hg, wd)
    if inside:
        tail, grad = lax.optimization_barrier((tail[0], grad))
        tail = lax.psum_scatter(tail, "fsdp", scatter_dimension=0, tiled=True)[0]
        cut = n_seq * experts * rows
        ggu = grad[:cut].reshape(n_seq, experts * rows, 2 * fc)
        gwd = grad[cut:].reshape(experts, -1, ff_rows, 2 * fc).transpose(0, 2, 1, 3)
        gqkv = tail[: n_seq * rows].reshape(n_seq, rows, -1)
        gwo = tail[n_seq * rows:].reshape(-1, rows, nqkv + 128).transpose(1, 0, 2).reshape(rows, d)
    else:
        gqkv, gwo = tail
        gwo = lax.psum_scatter(gwo, "fsdp", scatter_dimension=0, tiled=True)
        gqkv = gqkv.reshape(n_seq, n_fsdp, rows, -1).transpose(1, 0, 2, 3).reshape(n_fsdp * n_seq * rows, -1)
        gqkv = lax.psum_scatter(gqkv, "fsdp", scatter_dimension=0, tiled=True).reshape(n_seq, rows, -1)
    ggu = lax.all_to_all(ggu, "seq", split_axis=0, concat_axis=0, tiled=True)
    gqkv = lax.all_to_all(gqkv, "seq", split_axis=0, concat_axis=0, tiled=True)

    gqkv = gqkv.astype(F32)
    g_query = gqkv[:, :, :nq].transpose(1, 0, 2).reshape(rows, -1)
    g_key = gqkv[:, :, nq: nq + nk].transpose(1, 0, 2).reshape(rows, -1)
    g_value = gqkv[:, :, nq + nk: nqkv].transpose(1, 0, 2).reshape(rows, -1)
    g_router = jnp.sum(gqkv[:, :, nqkv: nqkv + experts] + gqkv[:, :, nqkv + experts: nqkv + 2 * experts], axis=0)
    ggu = ggu.astype(F32).reshape(n_seq, experts, rows, 2, fc).transpose(3, 1, 2, 0, 4).reshape(2, experts, rows, ff)
    g_gate, g_up = ggu[0], ggu[1]
    g_gain_one = (
        jnp.sum(w_query.astype(F32) * g_query, axis=1) + jnp.sum(w_key.astype(F32) * g_key, axis=1)
        + jnp.sum(w_value.astype(F32) * g_value, axis=1)
    ) / gain_attn.astype(F32)
    g_gain_two = (
        jnp.sum(w_gate.astype(F32) * g_gate + w_up.astype(F32) * g_up, axis=(0, 2))
        + jnp.sum(router.astype(F32) * g_router, axis=1)
    ) / gain_ffn.astype(F32)
    return (
        output[None], gin[None], g_gain_one, g_query, g_key, g_value, gwo.astype(F32), g_gain_two, g_router,
        g_gate, g_up, gwd.astype(F32).reshape(experts, ff_rows, d),
    )


def solution(mesh):
    tok = P("fsdp", "seq", None)
    vec = P(("seq", "fsdp"))
    mat = P(("seq", "fsdp"), None)
    exp = P(None, ("seq", "fsdp"), None)
    return jax.shard_map(
        shards,
        mesh=mesh,
        in_specs=(tok, tok, tok, vec, mat, mat, mat, mat, vec, mat, exp, exp, exp),
        out_specs=(tok, tok, vec, mat, mat, mat, mat, vec, mat, exp, exp, exp),
        check_vma=False,
    )
```

```python
import functools

import jax
import jax.numpy as jnp
from jax import lax
from jax.experimental import pallas as pl
from jax.experimental.pallas import tpu as pltpu
from jax.sharding import PartitionSpec as P

HEAD_DIM = 64
EPS = 1e-06
SCALE = HEAD_DIM ** (-0.5)
BF = jnp.bfloat16
F32 = jnp.float32
MESH = pl.DeviceIdType.MESH
ANY = pl.BlockSpec(memory_space=pl.ANY)
VM = pl.BlockSpec(memory_space=pltpu.VMEM)
MIB = 2**20


def dot(a, b):
    return jnp.dot(a, b, preferred_element_type=F32)


def dot_t(a, b):
    return lax.dot_general(a, b, (((1,), (1,)), ((), ())), preferred_element_type=F32)


def t_dot(a, b):
    return lax.dot_general(a, b, (((0,), (0,)), ((), ())), preferred_element_type=F32)


def rms_factor(rows):
    return lax.rsqrt(jnp.mean(rows * rows, axis=-1, keepdims=True) + EPS)


def partner(me, step):
    return ((me // 2 + step // 2) % 2) * 2 + (me % 2 + step % 2) % 2


def send(src, dst, sems, slot, peer):
    return pltpu.make_async_remote_copy(
        src_ref=src, dst_ref=dst, send_sem=sems.at[0, slot], recv_sem=sems.at[1, slot],
        device_id={"seq": peer}, device_id_type=MESH,
    )


def greet(me, others):
    barrier = pltpu.get_barrier_semaphore()
    for step in (1, 2, 3):
        pl.semaphore_signal(barrier, inc=1, device_id={"seq": partner(me, step)}, device_id_type=MESH)
    pl.semaphore_wait(barrier, 3 + others)


class Gather:
    def __init__(self, me, own, buf, sems, base=0):
        rows = own.shape[0]
        half = rows // 2
        one, two = partner(me, 1), partner(me, 2)

        def part(owner, start, size):
            return buf.at[pl.ds(pl.multiple_of(owner * rows + start, half), size)]

        mine = part(me, 0, rows)
        self.first = send(own, mine, sems, base, one)
        self.second = send(own, mine, sems, base + 1, two)
        onward = part(one, 0, half)
        self.third = send(onward, onward, sems, base + 2, two)
        onward = part(two, half, half)
        self.fourth = send(onward, onward, sems, base + 3, one)

    def start(self):
        self.first.start()
        self.second.start()

    def got_one(self):
        self.first.wait_recv()
        self.third.start()

    def got_two(self):
        self.second.wait_recv()
        self.fourth.start()

    def got_three(self):
        self.third.wait_recv()
        self.fourth.wait_recv()

    def finish(self):
        for copy in (self.first, self.second, self.third, self.fourth):
            copy.wait_send()


class Scatter:
    def __init__(self, me, parts, got, held, sems, extra=0, kind="whole"):
        half = parts.shape[1] // 2
        one, two = partner(me, 1), partner(me, 2)
        self.top, self.low = pl.ds(0, half), pl.ds(half, half)
        self.parts, self.got, self.held, self.extra = parts, got, held, extra

        def copy(slot, step, rows, peer, src=None):
            return send(parts.at[step, rows] if src is None else src, got.at[step - 1, rows], sems, slot, peer)

        self.early = self.late = ()
        if kind != "late":
            self.far_top = copy(0, 3, self.top, one)
            self.far_low = copy(1, 3, self.low, two)
            self.one_top = copy(2, 1, self.top, one)
            self.two_low = copy(3, 2, self.low, two)
            self.early = (self.far_top, self.far_low, self.one_top, self.two_low)
        if kind != "early":
            self.one_low = copy(4, 1, self.low, one, held.at[0])
            self.two_top = copy(5, 2, self.top, two, held.at[1])
            self.late = (self.one_low, self.two_top)

    def start(self, step):
        @pl.when(step == 3)
        def _():
            self.far_top.start()
            self.far_low.start()

        pl.when(step == 2)(self.two_low.start)
        pl.when(step == 1)(self.one_top.start)

    def onward(self):
        for slot, step, rows, arrived, copy in ((0, 1, self.low, 1, self.one_low), (1, 2, self.top, 0, self.two_top)):
            if self.early:
                self.early[arrived].wait_recv()
            both = self.parts[step, rows, :].astype(F32) + self.got[2, rows, :].astype(F32)
            self.held[slot] = both.astype(BF)
            if self.extra:
                tail = both[:, -128:]
                whole = tail + pltpu.roll(tail, 128 - self.extra, 1)
                self.held[slot, :, -128:] = pack_two(jnp.where(lanes(tail.shape) < self.extra, whole, 0.0), self.extra)
            copy.start()

    def arrive(self):
        for copy in self.early[2:] + self.late:
            copy.wait_recv()

    def total(self):
        self.arrive()
        return self.parts[0].astype(F32) + self.got[0].astype(F32) + self.got[1].astype(F32)

    def finish(self):
        for copy in self.early + self.late:
            copy.wait_send()


def lanes(shape):
    return lax.broadcasted_iota(jnp.int32, shape, len(shape) - 1)


def pack_two(value, experts):
    high = value.astype(BF).astype(F32)
    low = value - high
    return jnp.where(lanes(value.shape) < experts, high, pltpu.roll(low, experts, 1)).astype(BF)


class Line:
    def __init__(self, region, sems):
        me = lax.axis_index("fsdp")
        self.last = lax.axis_size("fsdp") // 2 - 1
        self.z, self.core = me // 2, me % 2
        self.region, self.sems = region, sems

    def copy(self, slot, plane, core, target):
        part = self.region(plane * 2 + core)
        return pltpu.make_async_remote_copy(
            src_ref=part, dst_ref=part, send_sem=self.sems.at[0, slot], recv_sem=self.sems.at[1, slot],
            device_id={"fsdp": target}, device_id_type=MESH,
        )

    def up(self, hop):
        return self.copy(hop, self.z - hop, self.core, (self.z + 1) * 2 + self.core)

    def from_below(self, hop):
        return self.copy(hop, self.z - 1 - hop, self.core, self.z * 2 + self.core)

    def down(self, hop):
        return self.copy(3 + hop, self.z + hop, self.core, (self.z - 1) * 2 + self.core)

    def from_above(self, hop):
        return self.copy(3 + hop, self.z + 1 + hop, self.core, self.z * 2 + self.core)

    def across(self, plane):
        return self.copy(6 + plane, plane, self.core, self.z * 2 + 1 - self.core)

    def from_across(self, plane):
        return self.copy(6 + plane, plane, 1 - self.core, self.z * 2 + self.core)

    def start(self):
        pl.when(self.z < self.last)(lambda: self.up(0).start())
        pl.when(self.z > 0)(lambda: self.down(0).start())
        self.across(self.z).start()

    def step(self, hop):
        @pl.when(self.z > hop)
        def _():
            self.from_below(hop).wait_recv()
            if hop < 2:
                pl.when(self.z < self.last)(lambda: self.up(hop + 1).start())
            self.across(self.z - 1 - hop).start()

        @pl.when(self.z + hop < self.last)
        def _():
            self.from_above(hop).wait_recv()
            if hop < 2:
                pl.when(self.z > 0)(lambda: self.down(hop + 1).start())
            self.across(self.z + 1 + hop).start()

    def land(self):
        for plane in range(4):
            self.from_across(plane).wait_recv()

    def finish(self):
        for hop in range(3):
            pl.when((self.z >= hop) & (self.z < self.last))(lambda hop=hop: self.up(hop).wait_send())
            pl.when((self.z + hop <= self.last) & (self.z > 0))(lambda hop=hop: self.down(hop).wait_send())
        for plane in range(4):
            self.across(plane).wait_send()


class Collect:
    def __init__(self, mine, cross, below, above, sems):
        me = lax.axis_index("fsdp")
        self.z, self.core = me // 2, me % 2
        self.mine, self.cross, self.below, self.above, self.sems = mine, cross, below, above, sems

    def copy(self, slot, src, dst, target):
        return pltpu.make_async_remote_copy(
            src_ref=src, dst_ref=dst, send_sem=self.sems.at[0, slot], recv_sem=self.sems.at[1, slot],
            device_id={"fsdp": target}, device_id_type=MESH,
        )

    def over(self, plane):
        return self.copy(plane, self.mine.at[plane, 1 - self.core], self.cross.at[plane], self.z * 2 + 1 - self.core)

    def up(self, plane, src):
        return self.copy(4 + plane, src.at[plane], self.below.at[plane], (self.z + 1) * 2 + self.core)

    def down(self, plane, src):
        return self.copy(8 + plane, src.at[plane], self.above.at[plane], (self.z - 1) * 2 + self.core)

    def start(self):
        for plane in range(4):
            self.over(plane).start()

    def combine(self):
        for plane in (3, 0, 2, 1):
            self.over(plane).wait_recv()
            both = self.mine[plane, self.core].astype(F32) + self.cross[plane].astype(F32)
            self.cross[plane] = both.astype(BF)

            if plane == 3:
                pl.when(self.z == 0)(self.up(3, self.cross).start)
            if plane == 0:
                pl.when(self.z == 3)(self.down(0, self.cross).start)

    def step(self, turn):
        high, low = 3 - turn, turn
        z = self.z

        if turn < 2:

            @pl.when(z == 0)
            def _():
                self.up(high, self.cross).wait_send()
                self.up(high - 1, self.cross).start()

            @pl.when(z == 3)
            def _():
                self.down(low, self.cross).wait_send()
                self.down(low + 1, self.cross).start()

        @pl.when((z > 0) & (z <= high))
        def _():
            self.up(high, self.below).wait_recv()

        @pl.when((z > 0) & (z < high))
        def _():
            self.below[high] = (self.below[high].astype(F32) + self.cross[high].astype(F32)).astype(BF)
            self.up(high, self.below).start()

        @pl.when((z < 3) & (z >= low))
        def _():
            self.down(low, self.above).wait_recv()

        @pl.when((z < 3) & (z > low))
        def _():
            self.above[low] = (self.above[low].astype(F32) + self.cross[low].astype(F32)).astype(BF)
            self.down(low, self.above).start()

    def total(self, out):
        z = self.z
        out[...] = self.cross[z].astype(F32)

        @pl.when(z > 0)
        def _():
            out[...] += self.below[z].astype(F32)

        @pl.when(z < 3)
        def _():
            out[...] += self.above[z].astype(F32)

    def finish(self):
        z = self.z
        for plane in range(4):
            self.over(plane).wait_send()
            pl.when((z > 0) & (z < 3) & (z < plane))(self.up(plane, self.below).wait_send)
            pl.when((z > 0) & (z < 3) & (z > plane))(self.down(plane, self.above).wait_send)
        pl.when(z == 0)(self.up(1, self.cross).wait_send)
        pl.when(z == 3)(self.down(2, self.cross).wait_send)


def load(pairs, sems, first=0):
    copies = [pltpu.make_async_copy(a, b, sems.at[first + i]) for i, (a, b) in enumerate(pairs)]
    for copy in copies:
        copy.start()
    return copies


def greet_line():
    me = lax.axis_index("fsdp")
    last = lax.axis_size("fsdp") // 2 - 1
    z, core = me // 2, me % 2
    barrier = pltpu.get_barrier_semaphore()

    @pl.when(z < last)
    def _():
        pl.semaphore_signal(barrier, inc=1, device_id={"fsdp": me + 2}, device_id_type=MESH)

    @pl.when(z > 0)
    def _():
        pl.semaphore_signal(barrier, inc=1, device_id={"fsdp": me - 2}, device_id_type=MESH)

    pl.semaphore_signal(barrier, inc=1, device_id={"fsdp": z * 2 + 1 - core}, device_id_type=MESH)
    return 1 + jnp.minimum(z, 1) + jnp.minimum(last - z, 1)


class Spread:
    def __init__(self, me, chunk, place, sems, local):
        self.copies = [send(chunk(partner(me, step)), place, sems, step, partner(me, step)) for step in (3, 2, 1)]
        self.local = pltpu.make_async_copy(chunk(me), place, local)

    def start(self):
        self.local.start()
        for copy in self.copies:
            copy.start()

    def got(self):
        self.local.wait()
        for copy in self.copies:
            copy.wait_recv()

    def finish(self):
        for copy in self.copies:
            copy.wait_send()


def front_kernel(nq, nk, experts, inside, *refs):
    if inside:
        (x_ref, g_ref, named_ref, query_own, key_own, value_own, extra_own, gate_own, up_own, woo_ref,
         n1_ref, qkv_ref, attn_ref, lse_ref, mixed_ref, n2_ref, gate_ref, gs_ref, gain_ref, ext_ref, wqkv_ref, wo_ref,
         gu_ref,
         cols_ref, xs_ref, send_ref, recv_ref, held_ref, xsem, gsem, asem, lsem, qw_ref, spread_sem, line_sem) = refs
    else:
        (x_ref, g_ref, named_ref, wqkv_ref, wo_ref,
         n1_ref, qkv_ref, attn_ref, lse_ref, mixed_ref, n2_ref, gate_ref, gs_ref, gain_ref, ext_ref,
         cols_ref, xs_ref, send_ref, recv_ref, held_ref, xsem, gsem, asem, lsem) = refs
    me = lax.axis_index("seq")
    toks, d = x_ref.shape
    group = nq // nk
    nqkv = nq + 2 * nk
    xg = Gather(me, x_ref, xs_ref, xsem)
    gg = Gather(me, g_ref, gs_ref, gsem)
    keep = pltpu.make_async_copy(g_ref, gs_ref.at[pl.ds(pl.multiple_of(me * toks, toks), toks)], lsem.at[0])
    keep.start()
    ao = Scatter(me, send_ref, recv_ref, held_ref, asem)
    if inside:
        shard = lax.axis_index("fsdp")
        rows = woo_ref.shape[0]
        greet(me, greet_line())
        qkv_line = Line(lambda f: qw_ref.at[:, f], line_sem.at[0])
        wo_line = Line(lambda f: wo_ref.at[pl.ds(pl.multiple_of(f * rows, 16), rows)], line_sem.at[1])
        gu_line = Line(lambda f: gu_ref.at[:, :, :, f], line_sem.at[2])
        spreads = []

        def spread(own, width, place):
            def chunk(c):
                cols = pl.ds(pl.multiple_of(c * width, 128), width)
                return own.at[:, cols] if len(own.shape) == 2 else own.at[:, :, cols]

            at = len(spreads)
            spreads.append(Spread(me, chunk if width else lambda c: own, place, spread_sem.at[at], lsem.at[2 + at]))

        spread(query_own, nq, qw_ref.at[me, shard, :, pl.ds(0, nq)])
        spread(key_own, nk, qw_ref.at[me, shard, :, pl.ds(nq, nk)])
        spread(value_own, nk, qw_ref.at[me, shard, :, pl.ds(nq + nk, nk)])
        spread(extra_own, 0, qw_ref.at[me, shard, :, pl.ds(nqkv, 128)])
        spread(gate_own, gate_own.shape[2] // 4, gu_ref.at[0, :, me, shard])
        spread(up_own, gate_own.shape[2] // 4, gu_ref.at[1, :, me, shard])
        place_wo = pltpu.make_async_copy(woo_ref, wo_line.region(shard), lsem.at[1])
        for one in spreads[:4]:
            one.start()
        place_wo.start()
        xg.start()
        for one in spreads[4:]:
            one.start()
        for one in spreads[:4]:
            one.got()
        qkv_line.start()
        place_wo.wait()
        xs_ref[pl.ds(pl.multiple_of(me * toks, toks), toks), :] = x_ref[...]
        qkv_line.step(0)
        qkv_line.step(1)
        wo_line.start()
        for one in spreads[4:]:
            one.got()
        gu_line.start()
        xg.got_one()
        xg.got_two()
        qkv_line.step(2)
        wo_line.step(0)
        qkv_line.land()
        wo_line.step(1)
        xg.got_three()
        gg.start()
        for s in range(4):
            for f in range(8):
                wqkv_ref[s * 8 * rows + f * rows: s * 8 * rows + (f + 1) * rows, :] = qw_ref[s, f]
    else:
        greet(me, 0)
        xg.start()
        xs_ref[pl.ds(pl.multiple_of(me * toks, toks), toks), :] = x_ref[...]
        xg.got_one()
        xg.got_two()
        xg.got_three()
        gg.start()
    ext = wqkv_ref[:, nqkv:]
    ext_ref[...] = ext
    gain_ref[...] = ext.astype(F32).T[experts:experts + 2, :]
    gain1 = gain_ref[0:1, :]
    cols_ref[...] = jnp.zeros_like(cols_ref)

    @pl.loop(0, 4)
    def _(block):
        rows = pl.ds(pl.multiple_of(block * toks, toks), toks)
        xf = xs_ref[rows, :].astype(F32)
        n1_ref[rows, :] = (xf * rms_factor(xf) * gain1).astype(BF)
        proj = dot(n1_ref[rows, :], wqkv_ref[:, 0:nqkv]).astype(BF)
        qkv_ref[rows, :] = proj

    if inside:
        wo_line.step(2)
        gu_line.step(0)
        wo_line.land()

    @pl.loop(0, 4)
    def _(turn):
        step = 3 - turn
        block = partner(me, step)
        rows = pl.ds(pl.multiple_of(block * toks, toks), toks)

        @pl.when(turn == 2)
        def _():
            gg.got_one()
            gg.got_two()

        for b in range(4):

            @pl.when(block == b)
            def _(b=b):
                upto = b * toks
                qrows = slice(upto, upto + toks)
                inside = lanes((toks, toks)) <= lax.broadcasted_iota(jnp.int32, (toks, toks), 0)
                for h in range(nq // HEAD_DIM):
                    g = h // group
                    q = qkv_ref[qrows, h * HEAD_DIM:(h + 1) * HEAD_DIM] * SCALE
                    kc = slice(nq + g * HEAD_DIM, nq + (g + 1) * HEAD_DIM)
                    vc = slice(nq + nk + g * HEAD_DIM, nq + nk + (g + 1) * HEAD_DIM)
                    near = jnp.where(inside, dot_t(q, qkv_ref[qrows, kc]), -1e30)
                    top = jnp.max(near, axis=-1, keepdims=True)
                    if b:
                        far = dot_t(q, qkv_ref[0:upto, kc])
                        top = jnp.maximum(top, jnp.max(far, axis=-1, keepdims=True))
                    near = jnp.exp(near - top)
                    total = jnp.sum(near, axis=-1, keepdims=True)
                    if b:
                        far = jnp.exp(far - top)
                        total = total + jnp.sum(far, axis=-1, keepdims=True)
                    inv = 1.0 / total
                    res = dot((near * inv).astype(BF), qkv_ref[qrows, vc])
                    if b:
                        res = res + dot((far * inv).astype(BF), qkv_ref[0:upto, vc])
                    attn_ref[qrows, h * HEAD_DIM:(h + 1) * HEAD_DIM] = res.astype(BF)
                    cols_ref[qrows, h:h + 1] = top + jnp.log(total)

        send_ref[step] = dot(attn_ref[rows, :], wo_ref[...]).astype(BF)

        ao.start(step)

    ao.onward()
    lse_ref[...] = cols_ref[...].T[0:8, :]
    if inside:
        gu_line.step(1)
    mixed = x_ref[...].astype(F32) + ao.total()
    if inside:
        gu_line.step(2)
    mixed_ref[...] = mixed
    n2 = (mixed * rms_factor(mixed) * gain_ref[1:2, :]).astype(BF)
    n2_ref[:, 0:d] = n2
    logits = dot(n2, ext_ref[...])
    named = named_ref[...] > 0.0
    top = jnp.max(jnp.where(named, logits, -1e30), axis=-1, keepdims=True)
    weight = jnp.where(named, jnp.exp(jnp.minimum(logits - top, 0.0)), 0.0)
    gates = weight / jnp.sum(weight, axis=-1, keepdims=True)
    gate_ref[...] = gates
    n2_ref[:, d:] = pack_two(gates, experts)
    gg.got_three()
    gg.finish()
    xg.finish()
    keep.wait()
    ao.finish()
    if inside:
        gu_line.land()
        for line in (qkv_line, wo_line, gu_line):
            line.finish()
        for one in spreads:
            one.finish()


def front(nq, nk, experts, x, g, named, weights, inside):
    toks, d = x.shape
    length = 4 * toks
    nqkv = nq + 2 * nk
    sds = jax.ShapeDtypeStruct
    out_shape = [
        sds((length, d), BF), sds((length, nqkv), BF), sds((length, nq), BF), sds((8, length), F32),
        sds((toks, d), F32), sds((toks, d + 128), BF), sds((toks, 128), F32), sds((length, d), BF),
        sds((2, d), F32), sds((d, 128), BF),
    ]
    in_specs = [VM] * 5
    out_specs = [VM] * 10
    scratch = [
        pltpu.VMEM((length, 128), F32), pltpu.VMEM((length, d), BF), pltpu.VMEM((4, toks, d), BF),
        pltpu.VMEM((3, toks, d), BF), pltpu.VMEM((2, toks // 2, d), BF),
        pltpu.SemaphoreType.DMA((2, 4)), pltpu.SemaphoreType.DMA((2, 4)), pltpu.SemaphoreType.DMA((2, 6)),
        pltpu.SemaphoreType.DMA((8,)),
    ]
    if inside:
        query, key, value, extra, gate, up, woo = weights
        rows, fc = query.shape[0], gate.shape[2] // 4
        in_specs = [VM] * 3 + [ANY] * 7
        out_shape += [sds((d, nqkv + 128), BF), sds((nq, d), BF), sds((2, experts, 4, 8, rows, fc), BF)]
        out_specs += [VM, VM, ANY]
        scratch += [
            pltpu.VMEM((4, 8, rows, nqkv + 128), BF), pltpu.SemaphoreType.DMA((6, 2, 4)),
            pltpu.SemaphoreType.DMA((3, 2, 10)),
        ]
    return pl.pallas_call(
        functools.partial(front_kernel, nq, nk, experts, inside),
        name="front",
        out_shape=out_shape,
        in_specs=in_specs,
        out_specs=out_specs,
        scratch_shapes=scratch,
        compiler_params=pltpu.CompilerParams(collective_id=1, has_side_effects=True, vmem_limit_bytes=60 * MIB),
        cost_estimate=pl.CostEstimate(flops=20 * 10**9, bytes_accessed=60 * 10**6, transcendentals=4 * 10**6),
    )(x, g, named, *weights)


def moe_kernel(experts, shards, *refs):
    n2o_ref, gs_hbm, gu_hbm, wd_hbm = refs[:4]
    ggu_ref, refs = refs[4], refs[:4] + refs[5:]
    if not shards:
        gwd_ref, refs = refs[4], refs[:4] + refs[5:]
    wd_out, hg_out, dn2_ref, part_ref = refs[4:8]
    refs = refs[:1] * 2 + refs
    (n2_ref, gs_ref, gu_ref, wd_ref, pre_ref, hid_ref, hg_ref, dpre_ref, grad_ref, nsem, dsem, lsem) = refs[10:22]
    me = lax.axis_index("seq")
    toks, de = n2o_ref.shape
    d = de - 128
    length, ff = hg_ref.shape
    fc = ff // experts
    load_gu = load(
        [(gu_hbm.at[m, e], gu_ref.at[:, pl.ds((2 * e + m) * fc, fc)]) for e in range(experts) for m in range(2)], lsem, 10)
    (load_gs,) = load([(gs_hbm, gs_ref)], lsem, 1)
    if shards:
        (wsem,) = refs[22:]
        wd_line = Line(lambda f: wd_ref.at[:, f], wsem)
        (load_wd,) = load([(wd_hbm, wd_ref.at[:, lax.axis_index("fsdp")])], lsem, 2)
        greet(me, greet_line())
        load_wd.wait()
        wd_line.start()
    else:
        (load_wd,) = load([(wd_hbm, wd_ref)], lsem, 2)
        greet(me, 0)
    ng = Gather(me, n2o_ref, n2_ref, nsem)
    ng.start()
    ns = Scatter(me, dn2_ref, part_ref, None, dsem, experts, "early")
    for copy in load_gu:
        copy.wait()

    def gate_of(rows, e):
        packed = n2_ref[rows, d:].astype(F32)
        lane = lanes(packed.shape)
        return jnp.sum(jnp.where((lane == e) | (lane == e + experts), packed, 0.0), axis=-1, keepdims=True)

    @pl.loop(0, 4)
    def _(step):
        block = partner(me, step)
        rows = pl.ds(pl.multiple_of(block * toks, toks), toks)

        @pl.when(step == 0)
        def _():
            n2_ref[rows, :] = n2o_ref[...]

        @pl.when(step == 1)
        def _():
            if shards:
                wd_line.step(0)
            ng.got_one()

        @pl.when(step == 2)
        def _():
            ng.got_two()
            if shards:
                wd_line.step(1)

        @pl.when(step == 3)
        def _():
            ng.got_three()
            if shards:
                wd_line.step(2)

        @pl.loop(0, experts)
        def _(e):
            cols = pl.ds(pl.multiple_of(e * 2 * fc, 2 * fc), 2 * fc)
            hcols = pl.ds(pl.multiple_of(e * fc, fc), fc)
            pre = dot(n2_ref[rows, 0:d], gu_ref[:, cols])
            gp, up = pre[:, 0:fc], pre[:, fc:]
            sig = 1.0 / (1.0 + jnp.exp(-gp))
            act = gp * sig
            hid = (act * up).astype(BF)
            hid_ref[rows, hcols] = hid
            hg_ref[rows, hcols] = (gate_of(rows, e) * hid.astype(F32)).astype(BF)
            pre_ref[rows, pl.ds(pl.multiple_of(e * 2 * fc, fc), fc)] = up * sig * (1.0 + gp * (1.0 - sig))
            pre_ref[rows, pl.ds(pl.multiple_of(e * 2 * fc + fc, fc), fc)] = act

    (save_hg,) = load([(hg_ref, hg_out)], lsem, 3)
    load_gs.wait()
    if shards:
        rows, wide = d // 4 // shards, 2 * fc
        low, parts = fc // shards, d // wide

        def save(slot, start, size):
            part = pl.ds(pl.multiple_of(start, 16), size)
            return pltpu.make_async_copy(grad_ref.at[:, part], ggu_ref.at[:, part], lsem.at[5 + slot])

        @pl.loop(0, experts)
        def _(e):
            cols = pl.ds(pl.multiple_of(e * fc, fc), fc)
            grad = t_dot(hg_ref[:, cols], gs_ref[...]).astype(BF)
            for f in range(shards):
                for c in range(parts):
                    at = pl.ds(pl.multiple_of(4 * experts * rows + (e * parts + c) * low, 16), low)
                    grad_ref[f, at, :] = grad[f * low:(f + 1) * low, c * wide:(c + 1) * wide]

        save_low = save(4, 4 * experts * rows, experts * parts * low)
        save_low.start()
        wd_line.land()
    else:

        @pl.loop(0, experts)
        def _(e):
            cols = pl.ds(pl.multiple_of(e * fc, fc), fc)
            grad_ref[cols, 0:d] = t_dot(hg_ref[:, cols], gs_ref[...]).astype(BF)

        load_wd.wait()
        (save_gwd,) = load([(grad_ref.at[pl.ds(0, ff), pl.ds(0, d)], gwd_ref)], lsem, 5)
    (save_wd,) = load([(wd_ref, wd_out)], lsem, 4)

    @pl.loop(0, 4)
    def _(turn):
        step = 3 - turn
        rows = pl.ds(pl.multiple_of(partner(me, step) * toks, toks), toks)

        def one_expert(e, dgate):
            hcols = pl.ds(pl.multiple_of(e * fc, fc), fc)
            left = pl.ds(pl.multiple_of(e * 2 * fc, fc), fc)
            right = pl.ds(pl.multiple_of(e * 2 * fc + fc, fc), fc)
            dh0 = dot_t(gs_ref[rows, :], wd_ref[e].reshape(fc, d))
            dh = gate_of(rows, e) * dh0
            dpre_ref[rows, left] = (dh * pre_ref[rows, left]).astype(BF)
            dpre_ref[rows, right] = (dh * pre_ref[rows, right]).astype(BF)
            sums = jnp.sum(hid_ref[rows, hcols].astype(F32) * dh0, axis=-1, keepdims=True)
            return dgate + jnp.where(lanes(dgate.shape) == e, sums, 0.0)

        dgate = lax.fori_loop(0, experts, one_expert, jnp.zeros((toks, 128), F32))
        dn2_ref[step, :, d:] = pack_two(dgate, experts)
        tile = 512

        @pl.loop(0, d // tile)
        def _(t):
            cols = pl.ds(pl.multiple_of(t * tile, tile), tile)
            dn2_ref[step, :, cols] = dot_t(dpre_ref[rows, :], gu_ref[cols, :]).astype(BF)

        ns.start(step)

    if shards:
        @pl.loop(0, 4)
        def _(s):
            cols = pl.ds(pl.multiple_of(s * (d // 4), 128), d // 4)
            grad = t_dot(n2_ref[:, cols], dpre_ref[...]).astype(BF)
            for f in range(shards):
                for e in range(experts):
                    at = pl.ds(pl.multiple_of((s * experts + e) * rows, 16), rows)
                    grad_ref[f, at, :] = grad[f * rows:(f + 1) * rows, e * wide:(e + 1) * wide]
            save(s, s * experts * rows, experts * rows).start()

        for s in range(4):
            save(s, s * experts * rows, experts * rows).wait()
        save_low.wait()
        wd_line.finish()
    else:
        save_gwd.wait()

        @pl.loop(0, d // 256)
        def _(t):
            cols = pl.ds(pl.multiple_of(t * 256, 256), 256)
            grad_ref[cols, :] = t_dot(n2_ref[:, cols], dpre_ref[...]).astype(BF)

        (save_ggu,) = load([(grad_ref, ggu_ref)], lsem, 6)
        save_ggu.wait()
    for copy in ns.early:
        copy.wait_recv()
    ns.finish()
    ng.finish()
    save_hg.wait()
    save_wd.wait()


def moe(experts, shards, n2o, gs, gu, wd):
    toks, de = n2o.shape
    d = de - 128
    length = 4 * toks
    fc = gu.shape[3]
    ff = experts * fc
    sds = jax.ShapeDtypeStruct
    dma = pltpu.SemaphoreType.DMA
    if shards:
        low = fc // shards
        whole = (experts, shards, low, d)
        grads = [sds((shards, 3 * ff * d // (2 * fc) // shards, 2 * fc), BF)]
        grad = pltpu.VMEM(grads[0].shape, BF)
        more = [dma((2, 10))]
    else:
        whole = (experts, fc, d)
        grads = [sds((d, 2 * ff), BF), sds((ff, d), BF)]
        grad = pltpu.VMEM((d, 2 * ff), BF)
        more = []
    return pl.pallas_call(
        functools.partial(moe_kernel, experts, shards),
        name="moe",
        out_shape=grads + [sds(whole, BF), sds((length, ff), BF), sds((4, toks, de), BF), sds((3, toks, de), BF)],
        in_specs=[VM] + [ANY] * 3,
        out_specs=[ANY] * len(grads) + [ANY, ANY, VM, ANY],
        scratch_shapes=[
            pltpu.VMEM((length, de), BF), pltpu.VMEM((length, d), BF), pltpu.VMEM((d, 2 * ff), BF),
            pltpu.VMEM(whole, BF), pltpu.VMEM((length, 2 * ff), F32), pltpu.VMEM((length, ff), BF),
            pltpu.VMEM((length, ff), BF), pltpu.VMEM((length, 2 * ff), BF), grad,
            dma((2, 4)), dma((2, 6)), dma((10 + 2 * experts,)),
        ] + more,
        compiler_params=pltpu.CompilerParams(collective_id=2, has_side_effects=True, vmem_limit_bytes=62 * MIB),
        cost_estimate=pl.CostEstimate(flops=40 * 10**9, bytes_accessed=80 * 10**6, transcendentals=4 * 10**6),
    )(n2o, gs, gu, wd)


def rest_kernel(nq, nk, experts, shards, *refs):
    x_ref, g_ref, mixed_ref, gate_ref, n2o_ref, gain_ref, ext_ref = refs[:7]
    n1_hbm, qkv_hbm, attn_hbm, lse_hbm, wqkv_hbm, wo_hbm, dn2_hbm, part_hbm, hg_hbm, wd_hbm = refs[7:17]
    out_ref, gin_ref, refs = refs[17], refs[18], refs[19:]
    if shards:
        gq_ref, gk_ref, gv_ref, gr_ref, gwo_ref = refs[:5]
        refs = refs[5:]
    else:
        gqkv_ref, gwo_ref = refs[:2]
        refs = refs[2:]
    (n1_ref, qkv_ref, attn_ref, lse_ref, wqkv_ref, wo_ref, dn2_ref, nrecv_ref, hg_ref, wd_ref,
     dmixed_ref, dproj_ref, dattn_ref, dqkv_ref, dk_ref, dv_ref, outp_ref, grouter_ref,
     nheld_ref, send_ref, recv_ref, held_ref, orecv_ref, oheld_ref, nsem, psem, dsem, osem, lsem) = refs[:29]
    me = lax.axis_index("seq")
    toks, d = x_ref.shape
    group = nq // nk
    nqkv = nq + 2 * nk
    own = pl.ds(pl.multiple_of(me * toks, toks), toks)
    upper, lower = pl.ds(0, toks // 2), pl.ds(toks // 2, toks // 2)
    early = load([
        (dn2_hbm.at[pl.ds(0, 3)], dn2_ref), (part_hbm.at[2], nrecv_ref.at[2]),
        (part_hbm.at[0, upper], nrecv_ref.at[0, upper]), (part_hbm.at[1, lower], nrecv_ref.at[1, lower]),
    ], lsem)
    next_loads = load([(hg_hbm, hg_ref), (wd_hbm, wd_ref)], lsem, 4)
    late_loads = load([
        (wo_hbm, wo_ref), (attn_hbm, attn_ref), (qkv_hbm, qkv_ref), (lse_hbm, lse_ref), (wqkv_hbm, wqkv_ref),
        (n1_hbm, n1_ref),
    ], lsem, 6)
    if shards:
        wmine, wcross, wbelow, wabove, qmine, qcross, qbelow, qabove, fin_ref, cut_ref, land_ref, wsem, qsem, ssem = refs[29:]
        wc = Collect(wmine, wcross, wbelow, wabove, wsem)
        qc = Collect(qmine, qcross, qbelow, qabove, qsem)
        greet(me, greet_line())
    else:
        greet(me, 0)
    ns = Scatter(me, dn2_ref, nrecv_ref, nheld_ref, nsem, experts, "late")
    os = Scatter(me, outp_ref, orecv_ref, oheld_ref, osem)
    ds = Scatter(me, send_ref, recv_ref, held_ref, dsem)
    for copy in early:
        copy.wait()
    ns.onward()
    for copy in next_loads:
        copy.wait()

    @pl.loop(0, 4)
    def _(step):
        rows = pl.ds(pl.multiple_of(partner(me, step) * toks, toks), toks)
        outp_ref[step] = dot(hg_ref[rows, :], wd_ref[...]).astype(BF)

    total = ns.total()
    os.start(3)
    both = total[:, d:]
    lane = lanes(both.shape)
    dgate = jnp.where(lane < experts, both + pltpu.roll(both, 128 - experts, 1), 0.0)
    gates = gate_ref[...]
    dlog = (gates * (dgate - jnp.sum(gates * dgate, axis=-1, keepdims=True))).astype(BF)
    dn = (total[:, 0:d] + dot_t(dlog, ext_ref[...])) * gain_ref[1:2, :]
    mixed = mixed_ref[...]
    r2 = rms_factor(mixed)
    dmixed = (
        g_ref[...].astype(F32) + r2 * dn - mixed * (r2 * r2 * r2) * jnp.mean(dn * mixed, axis=-1, keepdims=True))
    dmixed_ref[...] = dmixed
    dproj_ref[own, :] = dmixed.astype(BF)
    pg = Gather(me, dproj_ref.at[own], dproj_ref, psem)
    pg.start()
    grouter_ref[...] = pack_two(t_dot(n2o_ref[:, 0:d], dlog), experts)
    for copy in late_loads:
        copy.wait()

    dk_ref[...] = jnp.zeros_like(dk_ref)
    dv_ref[...] = jnp.zeros_like(dv_ref)

    @pl.loop(0, 4)
    def _(step):
        block = partner(me, step)
        rows = pl.ds(pl.multiple_of(block * toks, toks), toks)

        @pl.when(step == 1)
        def _():
            pg.got_one()

        @pl.when(step == 2)
        def _():
            pg.got_two()

        @pl.when(step == 3)
        def _():
            pg.got_three()

            os.start(1)
            os.start(2)
            if shards:
                low = nq // shards
                grad = t_dot(attn_ref[...], dproj_ref[...]).astype(BF)
                for f in range(shards):
                    wmine[f // 2, f % 2] = grad[f * low:(f + 1) * low]
                wc.start()

        dattn_ref[rows, :] = dot_t(dproj_ref[rows, :], wo_ref[...]).astype(BF)
        for b in range(4):

            @pl.when(block == b)
            def _(b=b):
                upto = b * toks
                qrows = slice(upto, upto + toks)
                inside = lax.broadcasted_iota(jnp.int32, (toks, toks), 0) <= lanes((toks, toks))
                for h in range(nq // HEAD_DIM):
                    g = h // group
                    hc = slice(h * HEAD_DIM, (h + 1) * HEAD_DIM)
                    gc = slice(g * HEAD_DIM, (g + 1) * HEAD_DIM)
                    q = qkv_ref[qrows, hc] * SCALE
                    da = dattn_ref[qrows, hc]
                    lse = lse_ref[h:h + 1, qrows]
                    parts = ([slice(0, upto)] if b else []) + [qrows]
                    probs, dprobs = [], []
                    delta = 0.0
                    for krows in parts:
                        k = qkv_ref[krows, nq + g * HEAD_DIM: nq + (g + 1) * HEAD_DIM]
                        v = qkv_ref[krows, nq + nk + g * HEAD_DIM: nq + nk + (g + 1) * HEAD_DIM]
                        p = jnp.exp(dot_t(k, q) - lse)
                        if krows is qrows:
                            p = jnp.where(inside, p, 0.0)
                        dp = dot_t(v, da)
                        delta = delta + jnp.sum(p * dp, axis=0, keepdims=True)
                        probs.append(p)
                        dprobs.append(dp)
                    dq = 0.0
                    for krows, p, dp in zip(parts, probs, dprobs):
                        k = qkv_ref[krows, nq + g * HEAD_DIM: nq + (g + 1) * HEAD_DIM]
                        dsc = (p * (dp - delta)).astype(BF)
                        dq = dq + t_dot(k, dsc)
                        dk_ref[krows, gc] += dot(dsc, q)
                        dv_ref[krows, gc] += dot(p.astype(BF), da)
                    dqkv_ref[qrows, hc] = (dq.T * SCALE).astype(BF)

    dqkv_ref[:, nq:nq + nk] = dk_ref[...].astype(BF)
    dqkv_ref[:, nq + nk:] = dv_ref[...].astype(BF)

    os.onward()
    if shards:
        wc.combine()
        part = d // 4 // shards

        @pl.loop(0, 4)
        def _(s):
            cols = pl.ds(pl.multiple_of(s * (d // 4), 128), d // 4)
            at = pl.ds(pl.multiple_of(s * part, 16), part)
            grad = t_dot(n1_ref[:, cols], dqkv_ref[...]).astype(BF)
            for f in range(shards):
                qmine[f // 2, f % 2, at, 0:nqkv] = grad[f * part:(f + 1) * part, :]
                of = pl.ds(pl.multiple_of(s * (d // 4) + f * part, 16), part)
                qmine[f // 2, f % 2, at, nqkv:] = grouter_ref[of, :]

        qc.start()
        wc.step(0)
        qc.combine()

    @pl.loop(0, 4)
    def _(turn):
        step = 3 - turn
        block = partner(me, step)
        rows = pl.ds(pl.multiple_of(block * toks, toks), toks)
        send_ref[step] = dot_t(dqkv_ref[rows, :], wqkv_ref[:, 0:nqkv]).astype(BF)
        ds.start(step)

    if shards:
        wc.step(1)
        qc.step(0)
        wc.step(2)
        ds.onward()
        qc.step(1)
        qc.step(2)
        qc.total(fin_ref)
        for s in range(4):
            cut_ref[s] = fin_ref[s * part:(s + 1) * part, :].astype(BF)
        spread = Spread(me, lambda c: cut_ref.at[c], land_ref.at[me], ssem, lsem.at[12])
        spread.start()
        wc.total(gwo_ref)
    else:
        ds.onward()

        @pl.loop(0, d // 256)
        def _(t):
            cols = pl.ds(pl.multiple_of(t * 256, 256), 256)
            gqkv_ref[cols, 0:nqkv] = t_dot(n1_ref[:, cols], dqkv_ref[...]).astype(BF)

        gqkv_ref[:, nqkv:] = grouter_ref[...]

        @pl.loop(0, nq // 128)
        def _(t):
            cols = pl.ds(pl.multiple_of(t * 128, 128), 128)
            gwo_ref[cols, :] = t_dot(attn_ref[:, cols], dproj_ref[...]).astype(BF)

    out_ref[...] = (mixed_ref[...] + os.total()).astype(BF)
    dn = ds.total() * gain_ref[0:1, :]
    xf = x_ref[...].astype(F32)
    r1 = rms_factor(xf)
    gin_ref[...] = (
        dmixed_ref[...] + r1 * dn - xf * (r1 * r1 * r1) * jnp.mean(dn * xf, axis=-1, keepdims=True)).astype(BF)
    if shards:
        spread.got()
        router = 0.0
        for s in range(4):
            piece = land_ref[s].astype(F32)
            gq_ref[:, s * nq:(s + 1) * nq] = piece[:, 0:nq]
            gk_ref[:, s * nk:(s + 1) * nk] = piece[:, nq:nq + nk]
            gv_ref[:, s * nk:(s + 1) * nk] = piece[:, nq + nk:nqkv]
            router = router + piece[:, nqkv:]
        gr_ref[...] = router
        spread.finish()
        wc.finish()
        qc.finish()
    pg.finish()
    ns.finish()
    os.finish()
    ds.finish()


def rest(nq, nk, experts, shards, rows, *args):
    toks, d = args[0].shape
    length = 4 * toks
    nqkv = nq + 2 * nk
    wide = nqkv + 128
    sds = jax.ShapeDtypeStruct
    dma = pltpu.SemaphoreType.DMA
    if shards:
        grads = [sds((rows, 4 * nq), F32), sds((rows, 4 * nk), F32), sds((rows, 4 * nk), F32), sds((rows, 128), F32),
                 sds((rows, d), F32)]
        more = [pltpu.VMEM((4, 2, rows, d), BF)] + [pltpu.VMEM((4, rows, d), BF)] * 3
        more += [pltpu.VMEM((4, 2, 4 * rows, wide), BF)] + [pltpu.VMEM((4, 4 * rows, wide), BF)] * 3
        more += [pltpu.VMEM((4 * rows, wide), F32)] + [pltpu.VMEM((4, rows, wide), BF)] * 2
        more += [dma((2, 12)), dma((2, 12)), dma((2, 4))]
    else:
        grads = [sds((d, wide), BF), sds((nq, d), BF)]
        more = []
    half = pltpu.VMEM((2, toks // 2, d), BF)
    blocks, three = pltpu.VMEM((4, toks, d), BF), pltpu.VMEM((3, toks, d), BF)
    return pl.pallas_call(
        functools.partial(rest_kernel, nq, nk, experts, shards),
        name="rest",
        out_shape=[sds((toks, d), BF), sds((toks, d), BF)] + grads,
        in_specs=[VM] * 7 + [ANY] * 10,
        out_specs=[VM] * (2 + len(grads)),
        scratch_shapes=[
            pltpu.VMEM((length, d), BF), pltpu.VMEM((length, nqkv), BF), pltpu.VMEM((length, nq), BF),
            pltpu.VMEM((8, length), F32), pltpu.VMEM((d, wide), BF), pltpu.VMEM((nq, d), BF),
            pltpu.VMEM((3, toks, d + 128), BF), pltpu.VMEM((3, toks, d + 128), BF), pltpu.VMEM(args[15].shape, BF),
            pltpu.VMEM(args[16].shape, BF),
            pltpu.VMEM((toks, d), F32), pltpu.VMEM((length, d), BF), pltpu.VMEM((length, nq), BF),
            pltpu.VMEM((length, nqkv), BF), pltpu.VMEM((length, nk), F32), pltpu.VMEM((length, nk), F32),
            blocks, pltpu.VMEM((d, 128), BF),
            pltpu.VMEM((2, toks // 2, d + 128), BF), blocks, three, half, three, half,
            dma((2, 6)), dma((2, 4)), dma((2, 6)), dma((2, 6)), dma((13,)),
        ] + more,
        compiler_params=pltpu.CompilerParams(collective_id=3, has_side_effects=True, vmem_limit_bytes=63 * MIB),
        cost_estimate=pl.CostEstimate(flops=60 * 10**9, bytes_accessed=80 * 10**6, transcendentals=4 * 10**6),
    )(*args)


def shards(x, cot, routes, gain_attn, w_query, w_key, w_value, w_out, gain_ffn, router, w_gate, w_up, w_down):
    n_seq = lax.axis_size("seq")
    n_fsdp = lax.axis_size("fsdp")
    rows, d = w_query.shape
    experts, ff_rows, _ = w_down.shape
    ff = w_gate.shape[2]
    fc = ff // n_seq

    nq, nk = w_query.shape[1] // n_seq, w_key.shape[1] // n_seq
    nqkv = nq + 2 * nk
    inside = n_seq == 4 and n_fsdp == 8 and rows % 16 == 0 and ff_rows % 16 == 0

    extra = jnp.concatenate(
        [router, gain_attn[:, None], gain_ffn[:, None], jnp.zeros((rows, 128 - 2 - experts), BF)], axis=1
    )
    hot = routes[0][:, :, None] == jnp.arange(128)[None, None, :]
    named = jnp.any(hot, axis=1).astype(F32)
    if inside:
        (n1, proj, attn, lse, mixed, n2o, gates, gs, gains, ext, wqkv, wo, gu) = front(
            nq, nk, experts, x[0], cot[0], named, (w_query, w_key, w_value, extra, w_gate, w_up, w_out), True)
        gu = gu.reshape(2, experts, d, fc)
        wd = w_down
    else:
        qkv = jnp.concatenate(
            [w_query.reshape(rows, n_seq, -1), w_key.reshape(rows, n_seq, -1), w_value.reshape(rows, n_seq, -1),
             jnp.broadcast_to(extra[:, None], (rows, n_seq, 128))], axis=2,
        ).transpose(1, 0, 2)
        gu = jnp.stack([w_gate, w_up]).reshape(2, experts, rows, n_seq, fc).transpose(3, 2, 0, 1, 4)
        gu = gu.reshape(n_seq, rows, 2 * experts * fc)
        qkv = lax.all_to_all(qkv, "seq", split_axis=0, concat_axis=0, tiled=True)
        gu = lax.all_to_all(gu, "seq", split_axis=0, concat_axis=0, tiled=True)
        do = jnp.concatenate([w_down.reshape(experts * ff_rows, d), w_out], axis=0)
        wqkv = lax.all_gather(qkv, "fsdp", axis=1).reshape(d, -1)
        do = lax.all_gather(do, "fsdp", axis=0)
        wo = do[:, experts * ff_rows:].reshape(-1, d)
        wd = do[:, : experts * ff_rows].reshape(n_fsdp, experts, ff_rows, d).transpose(1, 0, 2, 3)
        wd = wd.reshape(experts, -1, d)
        gu = lax.all_gather(gu, "fsdp", axis=1).reshape(d, 2, experts, fc).transpose(1, 2, 0, 3)
        (n1, proj, attn, lse, mixed, n2o, gates, gs, gains, ext) = front(
            nq, nk, experts, x[0], cot[0], named, (wqkv, wo), False)

    packed = n_fsdp if inside else 0
    *grads, wd, hg, dn2, part = moe(experts, packed, n2o, gs, gu, wd)
    if inside:
        grad = lax.psum_scatter(grads[0], "fsdp", scatter_dimension=0, tiled=True)[0]
        cut = n_seq * experts * rows
        ggu = grad[:cut].reshape(n_seq, experts * rows, 2 * fc)
        gwd = grad[cut:].reshape(experts, -1, ff_rows, 2 * fc).transpose(0, 2, 1, 3).reshape(experts, ff_rows, d)
    else:
        ggu, gwd = grads
        gwd = gwd.reshape(experts, n_fsdp, ff_rows, d).transpose(1, 0, 2, 3).reshape(-1, d)
        gwd = lax.psum_scatter(gwd, "fsdp", scatter_dimension=0, tiled=True).reshape(experts, ff_rows, d)
        ggu = ggu.reshape(n_seq, n_fsdp, rows, experts, 2 * fc).transpose(1, 0, 3, 2, 4)
        ggu = lax.psum_scatter(ggu, "fsdp", scatter_dimension=0, tiled=True).reshape(n_seq, experts * rows, 2 * fc)
    output, gin, *tail = rest(
        nq, nk, experts, packed, rows, x[0], cot[0], mixed, gates, n2o, gains, ext, n1, proj, attn, lse, wqkv, wo, dn2,
        part, hg, wd.reshape(-1, d))
    ggu = lax.all_to_all(ggu, "seq", split_axis=0, concat_axis=0, tiled=True)
    if inside:
        g_query, g_key, g_value, g_router, gwo = tail
        g_router = g_router[:, :experts] + g_router[:, experts: 2 * experts]
    else:
        gqkv, gwo = tail
        gwo = lax.psum_scatter(gwo, "fsdp", scatter_dimension=0, tiled=True)
        gqkv = gqkv.reshape(n_seq, n_fsdp, rows, -1).transpose(1, 0, 2, 3).reshape(n_fsdp * n_seq * rows, -1)
        gqkv = lax.psum_scatter(gqkv, "fsdp", scatter_dimension=0, tiled=True).reshape(n_seq, rows, -1)
        gqkv = lax.all_to_all(gqkv, "seq", split_axis=0, concat_axis=0, tiled=True)
        gqkv = gqkv.astype(F32)
        g_query = gqkv[:, :, :nq].transpose(1, 0, 2).reshape(rows, -1)
        g_key = gqkv[:, :, nq: nq + nk].transpose(1, 0, 2).reshape(rows, -1)
        g_value = gqkv[:, :, nq + nk: nqkv].transpose(1, 0, 2).reshape(rows, -1)
        g_router = jnp.sum(gqkv[:, :, nqkv: nqkv + experts] + gqkv[:, :, nqkv + experts: nqkv + 2 * experts], axis=0)
    ggu = ggu.astype(F32).reshape(n_seq, experts, rows, 2, fc).transpose(3, 1, 2, 0, 4).reshape(2, experts, rows, ff)
    g_gate, g_up = ggu[0], ggu[1]
    g_gain_one = (
        jnp.sum(w_query.astype(F32) * g_query, axis=1) + jnp.sum(w_key.astype(F32) * g_key, axis=1)
        + jnp.sum(w_value.astype(F32) * g_value, axis=1)
    ) / gain_attn.astype(F32)
    g_gain_two = (
        jnp.sum(w_gate.astype(F32) * g_gate + w_up.astype(F32) * g_up, axis=(0, 2))
        + jnp.sum(router.astype(F32) * g_router, axis=1)
    ) / gain_ffn.astype(F32)
    return (
        output[None], gin[None], g_gain_one, g_query, g_key, g_value, gwo.astype(F32), g_gain_two, g_router,
        g_gate, g_up, gwd.astype(F32),
    )


def solution(mesh):
    tok = P("fsdp", "seq", None)
    vec = P(("seq", "fsdp"))
    mat = P(("seq", "fsdp"), None)
    exp = P(None, ("seq", "fsdp"), None)
    return jax.shard_map(
        shards,
        mesh=mesh,
        in_specs=(tok, tok, tok, vec, mat, mat, mat, mat, vec, mat, exp, exp, exp),
        out_specs=(tok, tok, vec, mat, mat, mat, mat, vec, mat, exp, exp, exp),
        check_vma=False,
    )
```

```python
import functools

import jax
import jax.numpy as jnp
from jax import lax
from jax.experimental import pallas as pl
from jax.experimental.pallas import tpu as pltpu
from jax.sharding import PartitionSpec as P

HEAD_DIM = 64
EPS = 1e-06
SCALE = HEAD_DIM ** (-0.5)
BF = jnp.bfloat16
F32 = jnp.float32
MESH = pl.DeviceIdType.MESH
ANY = pl.BlockSpec(memory_space=pl.ANY)
VM = pl.BlockSpec(memory_space=pltpu.VMEM)
MIB = 2**20


def dot(a, b):
    return jnp.dot(a, b, preferred_element_type=F32)


def dot_t(a, b):
    return lax.dot_general(a, b, (((1,), (1,)), ((), ())), preferred_element_type=F32)


def t_dot(a, b):
    return lax.dot_general(a, b, (((0,), (0,)), ((), ())), preferred_element_type=F32)


def rms_factor(rows):
    return lax.rsqrt(jnp.mean(rows * rows, axis=-1, keepdims=True) + EPS)


def partner(me, step):
    return ((me // 2 + step // 2) % 2) * 2 + (me % 2 + step % 2) % 2


def send(src, dst, sems, slot, peer):
    return pltpu.make_async_remote_copy(
        src_ref=src, dst_ref=dst, send_sem=sems.at[0, slot], recv_sem=sems.at[1, slot],
        device_id={"seq": peer}, device_id_type=MESH,
    )


def greet(me, others):
    barrier = pltpu.get_barrier_semaphore()
    for step in (1, 2, 3):
        pl.semaphore_signal(barrier, inc=1, device_id={"seq": partner(me, step)}, device_id_type=MESH)
    pl.semaphore_wait(barrier, 3 + others)


class Gather:
    def __init__(self, me, own, buf, sems, base=0):
        rows = own.shape[0]
        half = rows // 2
        one, two = partner(me, 1), partner(me, 2)

        def part(owner, start, size):
            return buf.at[pl.ds(pl.multiple_of(owner * rows + start, half), size)]

        mine = part(me, 0, rows)
        self.first = send(own, mine, sems, base, one)
        self.second = send(own, mine, sems, base + 1, two)
        onward = part(one, 0, half)
        self.third = send(onward, onward, sems, base + 2, two)
        onward = part(two, half, half)
        self.fourth = send(onward, onward, sems, base + 3, one)

    def start(self):
        self.first.start()
        self.second.start()

    def got_one(self):
        self.first.wait_recv()
        self.third.start()

    def got_two(self):
        self.second.wait_recv()
        self.fourth.start()

    def got_three(self):
        self.third.wait_recv()
        self.fourth.wait_recv()

    def finish(self):
        for copy in (self.first, self.second, self.third, self.fourth):
            copy.wait_send()


class Scatter:
    def __init__(self, me, parts, got, held, sems, extra=0, kind="whole"):
        half = parts.shape[1] // 2
        one, two = partner(me, 1), partner(me, 2)
        self.top, self.low = pl.ds(0, half), pl.ds(half, half)
        self.parts, self.got, self.held, self.extra = parts, got, held, extra

        def copy(slot, step, rows, peer, src=None):
            return send(parts.at[step, rows] if src is None else src, got.at[step - 1, rows], sems, slot, peer)

        self.early = self.late = ()
        if kind != "late":
            self.far_top = copy(0, 3, self.top, one)
            self.far_low = copy(1, 3, self.low, two)
            self.one_top = copy(2, 1, self.top, one)
            self.two_low = copy(3, 2, self.low, two)
            self.early = (self.far_top, self.far_low, self.one_top, self.two_low)
        if kind != "early":
            self.one_low = copy(4, 1, self.low, one, held.at[0])
            self.two_top = copy(5, 2, self.top, two, held.at[1])
            self.late = (self.one_low, self.two_top)

    def start(self, step):
        @pl.when(step == 3)
        def _():
            self.far_top.start()
            self.far_low.start()

        pl.when(step == 2)(self.two_low.start)
        pl.when(step == 1)(self.one_top.start)

    def onward(self):
        for slot, step, rows, arrived, copy in ((0, 1, self.low, 1, self.one_low), (1, 2, self.top, 0, self.two_top)):
            if self.early:
                self.early[arrived].wait_recv()
            both = self.parts[step, rows, :].astype(F32) + self.got[2, rows, :].astype(F32)
            self.held[slot] = both.astype(BF)
            if self.extra:
                tail = both[:, -128:]
                whole = tail + pltpu.roll(tail, 128 - self.extra, 1)
                self.held[slot, :, -128:] = pack_two(jnp.where(lanes(tail.shape) < self.extra, whole, 0.0), self.extra)
            copy.start()

    def arrive(self):
        for copy in self.early[2:] + self.late:
            copy.wait_recv()

    def total(self):
        self.arrive()
        return self.parts[0].astype(F32) + self.got[0].astype(F32) + self.got[1].astype(F32)

    def finish(self):
        for copy in self.early + self.late:
            copy.wait_send()


def lanes(shape):
    return lax.broadcasted_iota(jnp.int32, shape, len(shape) - 1)


def pack_two(value, experts):
    high = value.astype(BF).astype(F32)
    low = value - high
    return jnp.where(lanes(value.shape) < experts, high, pltpu.roll(low, experts, 1)).astype(BF)


class Line:
    def __init__(self, region, sems):
        me = lax.axis_index("fsdp")
        self.last = lax.axis_size("fsdp") // 2 - 1
        self.z, self.core = me // 2, me % 2
        self.region, self.sems = region, sems

    def copy(self, slot, plane, core, target):
        part = self.region(plane * 2 + core)
        return pltpu.make_async_remote_copy(
            src_ref=part, dst_ref=part, send_sem=self.sems.at[0, slot], recv_sem=self.sems.at[1, slot],
            device_id={"fsdp": target}, device_id_type=MESH,
        )

    def up(self, hop):
        return self.copy(hop, self.z - hop, self.core, (self.z + 1) * 2 + self.core)

    def from_below(self, hop):
        return self.copy(hop, self.z - 1 - hop, self.core, self.z * 2 + self.core)

    def down(self, hop):
        return self.copy(3 + hop, self.z + hop, self.core, (self.z - 1) * 2 + self.core)

    def from_above(self, hop):
        return self.copy(3 + hop, self.z + 1 + hop, self.core, self.z * 2 + self.core)

    def across(self, plane):
        return self.copy(6 + plane, plane, self.core, self.z * 2 + 1 - self.core)

    def from_across(self, plane):
        return self.copy(6 + plane, plane, 1 - self.core, self.z * 2 + self.core)

    def start(self):
        pl.when(self.z < self.last)(lambda: self.up(0).start())
        pl.when(self.z > 0)(lambda: self.down(0).start())
        self.across(self.z).start()

    def step(self, hop):
        @pl.when(self.z > hop)
        def _():
            self.from_below(hop).wait_recv()
            if hop < 2:
                pl.when(self.z < self.last)(lambda: self.up(hop + 1).start())
            self.across(self.z - 1 - hop).start()

        @pl.when(self.z + hop < self.last)
        def _():
            self.from_above(hop).wait_recv()
            if hop < 2:
                pl.when(self.z > 0)(lambda: self.down(hop + 1).start())
            self.across(self.z + 1 + hop).start()

    def land(self):
        for plane in range(4):
            self.from_across(plane).wait_recv()

    def finish(self):
        for hop in range(3):
            pl.when((self.z >= hop) & (self.z < self.last))(lambda hop=hop: self.up(hop).wait_send())
            pl.when((self.z + hop <= self.last) & (self.z > 0))(lambda hop=hop: self.down(hop).wait_send())
        for plane in range(4):
            self.across(plane).wait_send()


class Collect:
    def __init__(self, mine, cross, below, above, sems):
        me = lax.axis_index("fsdp")
        self.z, self.core = me // 2, me % 2
        self.mine, self.cross, self.below, self.above, self.sems = mine, cross, below, above, sems

    def copy(self, slot, src, dst, target):
        return pltpu.make_async_remote_copy(
            src_ref=src, dst_ref=dst, send_sem=self.sems.at[0, slot], recv_sem=self.sems.at[1, slot],
            device_id={"fsdp": target}, device_id_type=MESH,
        )

    def over(self, plane):
        return self.copy(plane, self.mine.at[plane, 1 - self.core], self.cross.at[plane], self.z * 2 + 1 - self.core)

    def up(self, plane, src):
        return self.copy(4 + plane, src.at[plane], self.below.at[plane], (self.z + 1) * 2 + self.core)

    def down(self, plane, src):
        return self.copy(8 + plane, src.at[plane], self.above.at[plane], (self.z - 1) * 2 + self.core)

    def start(self):
        for plane in range(4):
            self.over(plane).start()

    def combine(self):
        for plane in (3, 0, 2, 1):
            self.over(plane).wait_recv()
            both = self.mine[plane, self.core].astype(F32) + self.cross[plane].astype(F32)
            self.cross[plane] = both.astype(BF)

            if plane == 3:
                pl.when(self.z == 0)(self.up(3, self.cross).start)
            if plane == 0:
                pl.when(self.z == 3)(self.down(0, self.cross).start)

    def step(self, turn):
        high, low = 3 - turn, turn
        z = self.z

        if turn < 2:

            @pl.when(z == 0)
            def _():
                self.up(high, self.cross).wait_send()
                self.up(high - 1, self.cross).start()

            @pl.when(z == 3)
            def _():
                self.down(low, self.cross).wait_send()
                self.down(low + 1, self.cross).start()

        @pl.when((z > 0) & (z <= high))
        def _():
            self.up(high, self.below).wait_recv()

        @pl.when((z > 0) & (z < high))
        def _():
            self.below[high] = (self.below[high].astype(F32) + self.cross[high].astype(F32)).astype(BF)
            self.up(high, self.below).start()

        @pl.when((z < 3) & (z >= low))
        def _():
            self.down(low, self.above).wait_recv()

        @pl.when((z < 3) & (z > low))
        def _():
            self.above[low] = (self.above[low].astype(F32) + self.cross[low].astype(F32)).astype(BF)
            self.down(low, self.above).start()

    def total(self, out):
        z = self.z
        out[...] = self.cross[z].astype(F32)

        @pl.when(z > 0)
        def _():
            out[...] += self.below[z].astype(F32)

        @pl.when(z < 3)
        def _():
            out[...] += self.above[z].astype(F32)

    def finish(self):
        z = self.z
        for plane in range(4):
            self.over(plane).wait_send()
            pl.when((z > 0) & (z < 3) & (z < plane))(self.up(plane, self.below).wait_send)
            pl.when((z > 0) & (z < 3) & (z > plane))(self.down(plane, self.above).wait_send)
        pl.when(z == 0)(self.up(1, self.cross).wait_send)
        pl.when(z == 3)(self.down(2, self.cross).wait_send)


def load(pairs, sems, first=0):
    copies = [pltpu.make_async_copy(a, b, sems.at[first + i]) for i, (a, b) in enumerate(pairs)]
    for copy in copies:
        copy.start()
    return copies


def greet_line():
    me = lax.axis_index("fsdp")
    last = lax.axis_size("fsdp") // 2 - 1
    z, core = me // 2, me % 2
    barrier = pltpu.get_barrier_semaphore()

    @pl.when(z < last)
    def _():
        pl.semaphore_signal(barrier, inc=1, device_id={"fsdp": me + 2}, device_id_type=MESH)

    @pl.when(z > 0)
    def _():
        pl.semaphore_signal(barrier, inc=1, device_id={"fsdp": me - 2}, device_id_type=MESH)

    pl.semaphore_signal(barrier, inc=1, device_id={"fsdp": z * 2 + 1 - core}, device_id_type=MESH)
    return 1 + jnp.minimum(z, 1) + jnp.minimum(last - z, 1)


class Spread:
    def __init__(self, me, chunk, place, sems, local):
        self.copies = [send(chunk(partner(me, step)), place, sems, step, partner(me, step)) for step in (3, 2, 1)]
        self.local = pltpu.make_async_copy(chunk(me), place, local)

    def start(self):
        self.local.start()
        for copy in self.copies:
            copy.start()

    def got(self):
        self.local.wait()
        for copy in self.copies:
            copy.wait_recv()

    def finish(self):
        for copy in self.copies:
            copy.wait_send()


def front_kernel(nq, nk, experts, inside, *refs):
    if inside:
        (x_ref, g_ref, named_ref, query_own, key_own, value_own, extra_own, gate_own, up_own, woo_ref,
         n1_out, qkv_out, attn_out, lse_ref, mixed_ref, n2_ref, gate_ref, gs_ref, gain_ref, ext_ref, wqkv_out, wo_out,
         gu_ref, n1_ref, qkv_ref, attn_ref, vsem, wqkv_ref, wo_ref,
         cols_ref, xs_ref, send_ref, recv_ref, held_ref, xsem, gsem, asem, lsem, qw_ref, spread_sem, line_sem) = refs
    else:
        (x_ref, g_ref, named_ref, wqkv_ref, wo_ref,
         n1_out, qkv_out, attn_out, lse_ref, mixed_ref, n2_ref, gate_ref, gs_ref, gain_ref, ext_ref,
         n1_ref, qkv_ref, attn_ref, vsem,
         cols_ref, xs_ref, send_ref, recv_ref, held_ref, xsem, gsem, asem, lsem) = refs
    me = lax.axis_index("seq")
    toks, d = x_ref.shape
    group = nq // nk
    nqkv = nq + 2 * nk
    xg = Gather(me, x_ref, xs_ref, xsem)
    gg = Gather(me, g_ref, gs_ref, gsem)
    keep = pltpu.make_async_copy(g_ref, gs_ref.at[pl.ds(pl.multiple_of(me * toks, toks), toks)], lsem.at[0])
    keep.start()
    ao = Scatter(me, send_ref, recv_ref, held_ref, asem)
    if inside:
        shard = lax.axis_index("fsdp")
        rows = woo_ref.shape[0]
        greet(me, greet_line())
        qkv_line = Line(lambda f: qw_ref.at[:, f], line_sem.at[0])
        wo_line = Line(lambda f: wo_ref.at[pl.ds(pl.multiple_of(f * rows, 16), rows)], line_sem.at[1])
        gu_line = Line(lambda f: gu_ref.at[:, :, :, f], line_sem.at[2])
        spreads = []

        def spread(own, width, place):
            def chunk(c):
                cols = pl.ds(pl.multiple_of(c * width, 128), width)
                return own.at[:, cols] if len(own.shape) == 2 else own.at[:, :, cols]

            at = len(spreads)
            spreads.append(Spread(me, chunk if width else lambda c: own, place, spread_sem.at[at], lsem.at[2 + at]))

        spread(query_own, nq, qw_ref.at[me, shard, :, pl.ds(0, nq)])
        spread(key_own, nk, qw_ref.at[me, shard, :, pl.ds(nq, nk)])
        spread(value_own, nk, qw_ref.at[me, shard, :, pl.ds(nq + nk, nk)])
        spread(extra_own, 0, qw_ref.at[me, shard, :, pl.ds(nqkv, 128)])
        spread(gate_own, gate_own.shape[2] // 4, gu_ref.at[0, :, me, shard])
        spread(up_own, gate_own.shape[2] // 4, gu_ref.at[1, :, me, shard])
        place_wo = pltpu.make_async_copy(woo_ref, wo_line.region(shard), lsem.at[1])
        for one in spreads[:4]:
            one.start()
        place_wo.start()
        xg.start()
        for one in spreads[4:]:
            one.start()
        for one in spreads[:4]:
            one.got()
        qkv_line.start()
        place_wo.wait()
        xs_ref[pl.ds(pl.multiple_of(me * toks, toks), toks), :] = x_ref[...]
        qkv_line.step(0)
        qkv_line.step(1)
        wo_line.start()
        for one in spreads[4:]:
            one.got()
        gu_line.start()
        xg.got_one()
        xg.got_two()
        qkv_line.step(2)
        wo_line.step(0)
        qkv_line.land()
        wo_line.step(1)
        xg.got_three()
        gg.start()
        for s in range(4):
            for f in range(8):
                wqkv_ref[s * 8 * rows + f * rows: s * 8 * rows + (f + 1) * rows, :] = qw_ref[s, f]
    else:
        greet(me, 0)
        xg.start()
        xs_ref[pl.ds(pl.multiple_of(me * toks, toks), toks), :] = x_ref[...]
        xg.got_one()
        xg.got_two()
        xg.got_three()
        gg.start()
    ext = wqkv_ref[:, nqkv:]
    ext_ref[...] = ext
    gain_ref[...] = ext.astype(F32).T[experts:experts + 2, :]
    gain1 = gain_ref[0:1, :]
    cols_ref[...] = jnp.zeros_like(cols_ref)

    @pl.loop(0, 4)
    def _(block):
        rows = pl.ds(pl.multiple_of(block * toks, toks), toks)
        xf = xs_ref[rows, :].astype(F32)
        n1_ref[rows, :] = (xf * rms_factor(xf) * gain1).astype(BF)
        proj = dot(n1_ref[rows, :], wqkv_ref[:, 0:nqkv]).astype(BF)
        qkv_ref[rows, :] = proj

    saves = load([(n1_ref, n1_out), (qkv_ref, qkv_out)], vsem)
    if inside:
        wo_line.step(2)
        gu_line.step(0)
        wo_line.land()
        saves += load([(wqkv_ref, wqkv_out), (wo_ref, wo_out)], vsem, 3)

    @pl.loop(0, 4)
    def _(turn):
        step = 3 - turn
        block = partner(me, step)
        rows = pl.ds(pl.multiple_of(block * toks, toks), toks)

        for b in range(4):

            @pl.when(block == b)
            def _(b=b):
                upto = b * toks
                qrows = slice(upto, upto + toks)
                inside = lanes((toks, toks)) <= lax.broadcasted_iota(jnp.int32, (toks, toks), 0)
                for h in range(nq // HEAD_DIM):
                    g = h // group
                    q = qkv_ref[qrows, h * HEAD_DIM:(h + 1) * HEAD_DIM] * SCALE
                    kc = slice(nq + g * HEAD_DIM, nq + (g + 1) * HEAD_DIM)
                    vc = slice(nq + nk + g * HEAD_DIM, nq + nk + (g + 1) * HEAD_DIM)
                    near = jnp.where(inside, dot_t(q, qkv_ref[qrows, kc]), -1e30)
                    top = jnp.max(near, axis=-1, keepdims=True)
                    if b:
                        far = dot_t(q, qkv_ref[0:upto, kc])
                        top = jnp.maximum(top, jnp.max(far, axis=-1, keepdims=True))
                    near = jnp.exp(near - top)
                    total = jnp.sum(near, axis=-1, keepdims=True)
                    if b:
                        far = jnp.exp(far - top)
                        total = total + jnp.sum(far, axis=-1, keepdims=True)
                    inv = 1.0 / total
                    res = dot((near * inv).astype(BF), qkv_ref[qrows, vc])
                    if b:
                        res = res + dot((far * inv).astype(BF), qkv_ref[0:upto, vc])
                    attn_ref[qrows, h * HEAD_DIM:(h + 1) * HEAD_DIM] = res.astype(BF)
                    cols_ref[qrows, h:h + 1] = top + jnp.log(total)

        send_ref[step] = dot(attn_ref[rows, :], wo_ref[...]).astype(BF)

        ao.start(step)

    saves += load([(attn_ref, attn_out)], vsem, 2)
    ao.onward()
    gg.got_one()
    gg.got_two()
    lse_ref[...] = cols_ref[...].T[0:8, :]
    if inside:
        gu_line.step(1)
    mixed = x_ref[...].astype(F32) + ao.total()
    if inside:
        gu_line.step(2)
    mixed_ref[...] = mixed
    n2 = (mixed * rms_factor(mixed) * gain_ref[1:2, :]).astype(BF)
    n2_ref[:, 0:d] = n2
    logits = dot(n2, ext_ref[...])
    lane = lanes(logits.shape)
    named = (lane == named_ref[:, 0:1]) | (lane == named_ref[:, 1:2])
    top = jnp.max(jnp.where(named, logits, -1e30), axis=-1, keepdims=True)
    weight = jnp.where(named, jnp.exp(jnp.minimum(logits - top, 0.0)), 0.0)
    gates = weight / jnp.sum(weight, axis=-1, keepdims=True)
    gate_ref[...] = gates
    n2_ref[:, d:] = pack_two(gates, experts)
    gg.got_three()
    gg.finish()
    xg.finish()
    keep.wait()
    for copy in saves:
        copy.wait()
    ao.finish()
    if inside:
        gu_line.land()
        for line in (qkv_line, wo_line, gu_line):
            line.finish()
        for one in spreads:
            one.finish()


def front(nq, nk, experts, x, g, named, weights, inside):
    toks, d = x.shape
    length = 4 * toks
    nqkv = nq + 2 * nk
    sds = jax.ShapeDtypeStruct
    out_shape = [
        sds((length, d), BF), sds((length, nqkv), BF), sds((length, nq), BF), sds((8, length), F32),
        sds((toks, d), F32), sds((toks, d + 128), BF), sds((toks, 128), F32), sds((length, d), BF),
        sds((2, d), F32), sds((d, 128), BF),
    ]
    in_specs = [VM] * 5
    out_specs = [ANY] * 3 + [VM] * 4 + [ANY] + [VM] * 2
    scratch = [
        pltpu.VMEM((length, d), BF), pltpu.VMEM((length, nqkv), BF), pltpu.VMEM((length, nq), BF),
        pltpu.SemaphoreType.DMA((5,)),
    ]
    if inside:
        scratch += [pltpu.VMEM((d, nqkv + 128), BF), pltpu.VMEM((nq, d), BF)]
    scratch += [
        pltpu.VMEM((length, 128), F32), pltpu.VMEM((length, d), BF), pltpu.VMEM((4, toks, d), BF),
        pltpu.VMEM((3, toks, d), BF), pltpu.VMEM((2, toks // 2, d), BF),
        pltpu.SemaphoreType.DMA((2, 4)), pltpu.SemaphoreType.DMA((2, 4)), pltpu.SemaphoreType.DMA((2, 6)),
        pltpu.SemaphoreType.DMA((8,)),
    ]
    if inside:
        query, key, value, extra, gate, up, woo = weights
        rows, fc = query.shape[0], gate.shape[2] // 4
        in_specs = [VM] * 3 + [ANY] * 7
        out_shape += [sds((d, nqkv + 128), BF), sds((nq, d), BF), sds((2, experts, 4, 8, rows, fc), BF)]
        out_specs += [ANY, ANY, ANY]
        scratch += [
            pltpu.VMEM((4, 8, rows, nqkv + 128), BF), pltpu.SemaphoreType.DMA((6, 2, 4)),
            pltpu.SemaphoreType.DMA((3, 2, 10)),
        ]
    return pl.pallas_call(
        functools.partial(front_kernel, nq, nk, experts, inside),
        name="front",
        out_shape=out_shape,
        in_specs=in_specs,
        out_specs=out_specs,
        scratch_shapes=scratch,
        compiler_params=pltpu.CompilerParams(collective_id=1, has_side_effects=True, vmem_limit_bytes=60 * MIB),
        cost_estimate=pl.CostEstimate(flops=20 * 10**9, bytes_accessed=60 * 10**6, transcendentals=4 * 10**6),
    )(x, g, named, *weights)


def hidden_kernel(experts, shards, *refs):
    (n2o_ref, gs_hbm, gu_hbm, wd_hbm, gwd_ref, wd_out, n2_out, hg_out, hid_out, pre_out,
     n2_ref, gs_ref, gu_ref, wd_ref, pre_ref, hid_ref, hg_ref, grad_ref, nsem, lsem, ssem) = refs[:21]
    me = lax.axis_index("seq")
    toks, de = n2o_ref.shape
    d = de - 128
    length, ff = hg_ref.shape
    fc = ff // experts
    load_gu = load(
        [(gu_hbm.at[m, e], gu_ref.at[:, pl.ds((2 * e + m) * fc, fc)]) for e in range(experts) for m in range(2)], lsem, 6)
    (load_gs,) = load([(gs_hbm, gs_ref)], lsem, 1)
    if shards:
        (wsem,) = refs[21:]
        wd_line = Line(lambda f: wd_ref.at[:, f], wsem)
        (load_wd,) = load([(wd_hbm, wd_ref.at[:, lax.axis_index("fsdp")])], lsem, 2)
        greet(me, greet_line())
        load_wd.wait()
        wd_line.start()
    else:
        (load_wd,) = load([(wd_hbm, wd_ref)], lsem, 2)
        greet(me, 0)
        load_wd.wait()
    ng = Gather(me, n2o_ref, n2_ref, nsem)
    ng.start()
    for copy in load_gu:
        copy.wait()

    def gate_of(rows, e):
        packed = n2_ref[rows, d:].astype(F32)
        lane = lanes(packed.shape)
        return jnp.sum(jnp.where((lane == e) | (lane == e + experts), packed, 0.0), axis=-1, keepdims=True)

    def saves(step):
        rows = pl.ds(pl.multiple_of(partner(me, step) * toks, toks), toks)
        return [
            pltpu.make_async_copy(a.at[rows], b.at[rows], ssem.at[i, step])
            for i, (a, b) in enumerate(((hg_ref, hg_out), (hid_ref, hid_out), (pre_ref, pre_out), (n2_ref, n2_out)))
        ]

    @pl.loop(0, 4)
    def _(step):
        block = partner(me, step)
        rows = pl.ds(pl.multiple_of(block * toks, toks), toks)

        @pl.when(step == 0)
        def _():
            n2_ref[rows, :] = n2o_ref[...]

        @pl.when(step == 1)
        def _():
            if shards:
                wd_line.step(0)
            ng.got_one()

        @pl.when(step == 2)
        def _():
            ng.got_two()
            if shards:
                wd_line.step(1)

        @pl.when(step == 3)
        def _():
            ng.got_three()
            if shards:
                wd_line.step(2)

        @pl.loop(0, experts)
        def _(e):
            cols = pl.ds(pl.multiple_of(e * 2 * fc, 2 * fc), 2 * fc)
            hcols = pl.ds(pl.multiple_of(e * fc, fc), fc)
            pre = dot(n2_ref[rows, 0:d], gu_ref[:, cols])
            gp, up = pre[:, 0:fc], pre[:, fc:]
            sig = 1.0 / (1.0 + jnp.exp(-gp))
            act = gp * sig
            hid = (act * up).astype(BF)
            hid_ref[rows, hcols] = hid
            hg_ref[rows, hcols] = (gate_of(rows, e) * hid.astype(F32)).astype(BF)
            pre_ref[rows, pl.ds(pl.multiple_of(e * 2 * fc, fc), fc)] = up * sig * (1.0 + gp * (1.0 - sig))
            pre_ref[rows, pl.ds(pl.multiple_of(e * 2 * fc + fc, fc), fc)] = act

        for copy in saves(step):
            copy.start()

    load_gs.wait()
    if shards:
        low, wide = fc // shards, 2 * fc
        parts = d // wide

        @pl.loop(0, experts - 1)
        def _(e):
            cols = pl.ds(pl.multiple_of(e * fc, fc), fc)
            grad = t_dot(hg_ref[:, cols], gs_ref[...]).astype(BF)
            for f in range(shards):
                for c in range(parts):
                    at = pl.ds(pl.multiple_of((e * parts + c) * low, 16), low)
                    grad_ref[f, at, :] = grad[f * low:(f + 1) * low, c * wide:(c + 1) * wide]

        wd_line.land()
    else:

        @pl.loop(0, experts)
        def _(e):
            cols = pl.ds(pl.multiple_of(e * fc, fc), fc)
            grad_ref[cols, :] = t_dot(hg_ref[:, cols], gs_ref[...]).astype(BF)

    last = load([(grad_ref, gwd_ref), (wd_ref, wd_out)], lsem, 3)
    for step in range(4):
        for copy in saves(step):
            copy.wait()
    for copy in last:
        copy.wait()
    ng.finish()
    if shards:
        wd_line.finish()


def hidden(experts, shards, n2o, gs, gu, wd):
    toks, de = n2o.shape
    d = de - 128
    length = 4 * toks
    fc = gu.shape[3]
    ff = experts * fc
    sds = jax.ShapeDtypeStruct
    dma = pltpu.SemaphoreType.DMA
    whole = (experts, shards, fc // shards, d) if shards else (experts, fc, d)
    grad = (shards, (ff - fc) * d // (2 * fc) // shards, 2 * fc) if shards else (ff, d)
    return pl.pallas_call(
        functools.partial(hidden_kernel, experts, shards),
        name="hidden",
        out_shape=[
            sds(grad, BF), sds(whole, BF), sds((length, de), BF), sds((length, ff), BF), sds((length, ff), BF),
            sds((length, 2 * ff), F32),
        ],
        in_specs=[VM] + [ANY] * 3,
        out_specs=[ANY] * 6,
        scratch_shapes=[
            pltpu.VMEM((length, de), BF), pltpu.VMEM((length, d), BF), pltpu.VMEM((d, 2 * ff), BF),
            pltpu.VMEM(whole, BF), pltpu.VMEM((length, 2 * ff), F32), pltpu.VMEM((length, ff), BF),
            pltpu.VMEM((length, ff), BF), pltpu.VMEM(grad, BF),
            dma((2, 4)), dma((6 + 2 * experts,)), dma((4, 4)),
        ] + ([dma((2, 10))] if shards else []),
        compiler_params=pltpu.CompilerParams(collective_id=2, has_side_effects=True, vmem_limit_bytes=60 * MIB),
        cost_estimate=pl.CostEstimate(flops=20 * 10**9, bytes_accessed=50 * 10**6, transcendentals=4 * 10**6),
    )(n2o, gs, gu, wd)


def moe_kernel(experts, shards, n2_hbm, gs_hbm, gu_hbm, wd_hbm, hid_hbm, pre_hbm, hg_hbm, ggu_ref, dn2_ref, part_ref,
               n2_ref, gs_ref, gu_ref, wd_ref, pre_ref, hid_ref, dpre_ref, grad_ref, hg_ref, dsem, lsem, bsem):
    me = lax.axis_index("seq")
    length, d = gs_ref.shape
    toks = length // 4
    ff = hid_ref.shape[1]
    fc = ff // experts
    (load_wd,) = load([(wd_hbm, wd_ref)], lsem, 0)

    def blocks(step):
        rows = pl.ds(pl.multiple_of(partner(me, step) * toks, toks), toks)
        return [
            pltpu.make_async_copy(a.at[rows], b.at[rows], bsem.at[i, step])
            for i, (a, b) in enumerate(((n2_hbm, n2_ref), (gs_hbm, gs_ref), (hid_hbm, hid_ref), (pre_hbm, pre_ref)))
        ]

    for copy in blocks(3):
        copy.start()
    load_gu = load(
        [(gu_hbm.at[m, e], gu_ref.at[:, pl.ds((2 * e + m) * fc, fc)]) for e in range(experts) for m in range(2)], lsem, 6)
    for step in (2, 1, 0):
        for copy in blocks(step):
            copy.start()
    (load_hg,) = load([(hg_hbm.at[:, pl.ds(ff - fc, fc)], hg_ref)], lsem, 5)
    greet(me, 0)
    ns = Scatter(me, dn2_ref, part_ref, None, dsem, experts, "early")
    load_wd.wait()

    @pl.loop(0, 4)
    def _(turn):
        step = 3 - turn
        rows = pl.ds(pl.multiple_of(partner(me, step) * toks, toks), toks)
        for copy in blocks(step):
            copy.wait()

        def one_expert(e, dgate):
            hcols = pl.ds(pl.multiple_of(e * fc, fc), fc)
            left = pl.ds(pl.multiple_of(e * 2 * fc, fc), fc)
            right = pl.ds(pl.multiple_of(e * 2 * fc + fc, fc), fc)
            packed = n2_ref[rows, d:].astype(F32)
            lane = lanes(packed.shape)
            gate = jnp.sum(jnp.where((lane == e) | (lane == e + experts), packed, 0.0), axis=-1, keepdims=True)
            dh0 = dot_t(gs_ref[rows, :], wd_ref[e].reshape(fc, d))
            dh = gate * dh0
            dpre_ref[rows, left] = (dh * pre_ref[rows, left]).astype(BF)
            dpre_ref[rows, right] = (dh * pre_ref[rows, right]).astype(BF)
            sums = jnp.sum(hid_ref[rows, hcols].astype(F32) * dh0, axis=-1, keepdims=True)
            return dgate + jnp.where(lane == e, sums, 0.0)

        dgate = lax.fori_loop(0, experts, one_expert, jnp.zeros((toks, 128), F32), unroll=True)
        dn2_ref[step, :, d:] = pack_two(dgate, experts)

        @pl.when(turn == 0)
        def _():
            for copy in load_gu:
                copy.wait()

        tile = 512

        @pl.loop(0, d // tile)
        def _(t):
            cols = pl.ds(pl.multiple_of(t * tile, tile), tile)
            dn2_ref[step, :, cols] = dot_t(dpre_ref[rows, :], gu_ref[cols, :]).astype(BF)

        ns.start(step)

    if shards:
        rows, wide = d // 4 // shards, 2 * fc

        def save(s):
            part = pl.ds(pl.multiple_of(s * experts * rows, 16), experts * rows)
            return pltpu.make_async_copy(grad_ref.at[:, part], ggu_ref.at[:, part], lsem.at[1 + s])

        low, parts = fc // shards, d // wide
        base = 4 * experts * rows
        load_hg.wait()
        grad = t_dot(hg_ref[...], gs_ref[...]).astype(BF)
        for f in range(shards):
            for c in range(parts):
                at = base + c * low
                grad_ref[f, at:at + low, :] = grad[f * low:(f + 1) * low, c * wide:(c + 1) * wide]
        rest_part = pl.ds(base, parts * low)
        (save_last,) = load([(grad_ref.at[:, rest_part], ggu_ref.at[:, rest_part])], lsem, 0)

        @pl.loop(0, 4)
        def _(s):
            cols = pl.ds(pl.multiple_of(s * (d // 4), 128), d // 4)
            grad = t_dot(n2_ref[:, cols], dpre_ref[...]).astype(BF)
            for f in range(shards):
                for e in range(experts):
                    at = pl.ds(pl.multiple_of((s * experts + e) * rows, 16), rows)
                    grad_ref[f, at, :] = grad[f * rows:(f + 1) * rows, e * wide:(e + 1) * wide]
            save(s).start()

        for s in range(4):
            save(s).wait()
        save_last.wait()
    else:
        load_hg.wait()

        @pl.loop(0, d // 256)
        def _(t):
            cols = pl.ds(pl.multiple_of(t * 256, 256), 256)
            grad_ref[cols, :] = t_dot(n2_ref[:, cols], dpre_ref[...]).astype(BF)

        (save_ggu,) = load([(grad_ref, ggu_ref)], lsem, 1)
        save_ggu.wait()
    for copy in ns.early:
        copy.wait_recv()
    ns.finish()


def moe(experts, shards, n2, gs, gu, wd, hid, pre, hg):
    length, de = n2.shape
    d = de - 128
    toks = length // 4
    fc = gu.shape[3]
    ff = experts * fc
    sds = jax.ShapeDtypeStruct
    dma = pltpu.SemaphoreType.DMA
    grad = (shards, (2 * ff + fc) * d // (2 * fc) // shards, 2 * fc) if shards else (d, 2 * ff)
    return pl.pallas_call(
        functools.partial(moe_kernel, experts, shards),
        name="moe",
        out_shape=[sds(grad, BF), sds((4, toks, de), BF), sds((3, toks, de), BF)],
        in_specs=[ANY] * 7,
        out_specs=[ANY, VM, ANY],
        scratch_shapes=[
            pltpu.VMEM((length, de), BF), pltpu.VMEM((length, d), BF), pltpu.VMEM((d, 2 * ff), BF),
            pltpu.VMEM(wd.shape, BF), pltpu.VMEM((length, 2 * ff), F32), pltpu.VMEM((length, ff), BF),
            pltpu.VMEM((length, 2 * ff), BF), pltpu.VMEM(grad, BF), pltpu.VMEM((length, fc), BF),
            dma((2, 6)), dma((6 + 2 * experts,)), dma((4, 4)),
        ],
        compiler_params=pltpu.CompilerParams(collective_id=4, has_side_effects=True, vmem_limit_bytes=60 * MIB),
        cost_estimate=pl.CostEstimate(flops=40 * 10**9, bytes_accessed=60 * 10**6, transcendentals=10**6),
    )(n2, gs, gu, wd, hid, pre, hg)


def rest_kernel(nq, nk, experts, shards, *refs):
    x_ref, g_ref, mixed_ref, gate_ref, n2o_ref, gain_ref, ext_ref = refs[:7]
    n1_hbm, qkv_hbm, attn_hbm, lse_hbm, wqkv_hbm, wo_hbm, dn2_hbm, part_hbm, hg_hbm, wd_hbm = refs[7:17]
    out_ref, gin_ref, refs = refs[17], refs[18], refs[19:]
    if shards:
        gq_ref, gk_ref, gv_ref, gr_ref, gwo_ref = refs[:5]
        refs = refs[5:]
    else:
        gqkv_ref, gwo_ref = refs[:2]
        refs = refs[2:]
    (n1_ref, qkv_ref, attn_ref, lse_ref, wqkv_ref, wo_ref, dn2_ref, nrecv_ref, hg_ref, wd_ref,
     dmixed_ref, dproj_ref, dattn_ref, dqkv_ref, dk_ref, dv_ref, outp_ref, grouter_ref,
     nheld_ref, send_ref, recv_ref, held_ref, orecv_ref, oheld_ref, nsem, psem, dsem, osem, lsem) = refs[:29]
    me = lax.axis_index("seq")
    toks, d = x_ref.shape
    group = nq // nk
    nqkv = nq + 2 * nk
    own = pl.ds(pl.multiple_of(me * toks, toks), toks)
    upper, lower = pl.ds(0, toks // 2), pl.ds(toks // 2, toks // 2)
    early = load([
        (dn2_hbm.at[pl.ds(0, 3)], dn2_ref), (part_hbm.at[2], nrecv_ref.at[2]),
        (part_hbm.at[0, upper], nrecv_ref.at[0, upper]), (part_hbm.at[1, lower], nrecv_ref.at[1, lower]),
    ], lsem)
    next_loads = load([(hg_hbm, hg_ref), (wd_hbm, wd_ref)], lsem, 4)
    late_loads = load([
        (wo_hbm, wo_ref), (attn_hbm, attn_ref), (qkv_hbm, qkv_ref), (lse_hbm, lse_ref), (wqkv_hbm, wqkv_ref),
        (n1_hbm, n1_ref),
    ], lsem, 6)
    if shards:
        wmine, wcross, wbelow, wabove, qmine, qcross, qbelow, qabove, fin_ref, cut_ref, land_ref, wsem, qsem, ssem = refs[29:]
        wc = Collect(wmine, wcross, wbelow, wabove, wsem)
        qc = Collect(qmine, qcross, qbelow, qabove, qsem)
        greet(me, greet_line())
    else:
        greet(me, 0)
    ns = Scatter(me, dn2_ref, nrecv_ref, nheld_ref, nsem, experts, "late")
    os = Scatter(me, outp_ref, orecv_ref, oheld_ref, osem)
    ds = Scatter(me, send_ref, recv_ref, held_ref, dsem)
    for copy in early:
        copy.wait()
    ns.onward()
    for copy in next_loads:
        copy.wait()

    @pl.loop(0, 4)
    def _(step):
        rows = pl.ds(pl.multiple_of(partner(me, step) * toks, toks), toks)
        outp_ref[step] = dot(hg_ref[rows, :], wd_ref[...]).astype(BF)

    total = ns.total()
    os.start(3)
    both = total[:, d:]
    lane = lanes(both.shape)
    dgate = jnp.where(lane < experts, both + pltpu.roll(both, 128 - experts, 1), 0.0)
    gates = gate_ref[...]
    dlog = (gates * (dgate - jnp.sum(gates * dgate, axis=-1, keepdims=True))).astype(BF)
    dn = (total[:, 0:d] + dot_t(dlog, ext_ref[...])) * gain_ref[1:2, :]
    mixed = mixed_ref[...]
    r2 = rms_factor(mixed)
    dmixed = (
        g_ref[...].astype(F32) + r2 * dn - mixed * (r2 * r2 * r2) * jnp.mean(dn * mixed, axis=-1, keepdims=True))
    dmixed_ref[...] = dmixed
    dproj_ref[own, :] = dmixed.astype(BF)
    pg = Gather(me, dproj_ref.at[own], dproj_ref, psem)
    pg.start()
    grouter_ref[...] = pack_two(t_dot(n2o_ref[:, 0:d], dlog), experts)
    for copy in late_loads:
        copy.wait()

    dk_ref[...] = jnp.zeros_like(dk_ref)
    dv_ref[...] = jnp.zeros_like(dv_ref)

    @pl.loop(0, 4)
    def _(step):
        block = partner(me, step)
        rows = pl.ds(pl.multiple_of(block * toks, toks), toks)

        @pl.when(step == 1)
        def _():
            pg.got_one()

        @pl.when(step == 2)
        def _():
            pg.got_two()

        @pl.when(step == 3)
        def _():
            pg.got_three()

            os.start(1)
            os.start(2)
            if shards:
                low = nq // shards
                grad = t_dot(attn_ref[...], dproj_ref[...]).astype(BF)
                for f in range(shards):
                    wmine[f // 2, f % 2] = grad[f * low:(f + 1) * low]
                wc.start()

        dattn_ref[rows, :] = dot_t(dproj_ref[rows, :], wo_ref[...]).astype(BF)
        for b in range(4):

            @pl.when(block == b)
            def _(b=b):
                upto = b * toks
                qrows = slice(upto, upto + toks)
                inside = lax.broadcasted_iota(jnp.int32, (toks, toks), 0) <= lanes((toks, toks))
                for h in range(nq // HEAD_DIM):
                    g = h // group
                    hc = slice(h * HEAD_DIM, (h + 1) * HEAD_DIM)
                    gc = slice(g * HEAD_DIM, (g + 1) * HEAD_DIM)
                    q = qkv_ref[qrows, hc] * SCALE
                    da = dattn_ref[qrows, hc]
                    lse = lse_ref[h:h + 1, qrows]
                    parts = ([slice(0, upto)] if b else []) + [qrows]
                    probs, dprobs = [], []
                    delta = 0.0
                    for krows in parts:
                        k = qkv_ref[krows, nq + g * HEAD_DIM: nq + (g + 1) * HEAD_DIM]
                        v = qkv_ref[krows, nq + nk + g * HEAD_DIM: nq + nk + (g + 1) * HEAD_DIM]
                        p = jnp.exp(dot_t(k, q) - lse)
                        if krows is qrows:
                            p = jnp.where(inside, p, 0.0)
                        dp = dot_t(v, da)
                        delta = delta + jnp.sum(p * dp, axis=0, keepdims=True)
                        probs.append(p)
                        dprobs.append(dp)
                    dq = 0.0
                    for krows, p, dp in zip(parts, probs, dprobs):
                        k = qkv_ref[krows, nq + g * HEAD_DIM: nq + (g + 1) * HEAD_DIM]
                        dsc = (p * (dp - delta)).astype(BF)
                        dq = dq + t_dot(k, dsc)
                        dk_ref[krows, gc] += dot(dsc, q)
                        dv_ref[krows, gc] += dot(p.astype(BF), da)
                    dqkv_ref[qrows, hc] = (dq.T * SCALE).astype(BF)

    dqkv_ref[:, nq:nq + nk] = dk_ref[...].astype(BF)
    dqkv_ref[:, nq + nk:] = dv_ref[...].astype(BF)

    os.onward()
    if shards:
        part = d // 4 // shards

        @pl.loop(0, 4)
        def _(s):
            cols = pl.ds(pl.multiple_of(s * (d // 4), 128), d // 4)
            at = pl.ds(pl.multiple_of(s * part, 16), part)
            grad = t_dot(n1_ref[:, cols], dqkv_ref[...]).astype(BF)
            for f in range(shards):
                qmine[f // 2, f % 2, at, 0:nqkv] = grad[f * part:(f + 1) * part, :]
                of = pl.ds(pl.multiple_of(s * (d // 4) + f * part, 16), part)
                qmine[f // 2, f % 2, at, nqkv:] = grouter_ref[of, :]

        qc.start()
        wc.combine()

    @pl.loop(0, 4)
    def _(turn):
        step = 3 - turn
        block = partner(me, step)
        rows = pl.ds(pl.multiple_of(block * toks, toks), toks)
        send_ref[step] = dot_t(dqkv_ref[rows, :], wqkv_ref[:, 0:nqkv]).astype(BF)
        ds.start(step)

    if shards:
        qc.combine()
        wc.step(0)
        qc.step(0)
        ds.onward()
        wc.step(1)
        qc.step(1)
        wc.step(2)
        qc.step(2)
        qc.total(fin_ref)
        for s in range(4):
            cut_ref[s] = fin_ref[s * part:(s + 1) * part, :].astype(BF)
        spread = Spread(me, lambda c: cut_ref.at[c], land_ref.at[me], ssem, lsem.at[12])
        spread.start()
        wc.total(gwo_ref)
    else:
        ds.onward()

        @pl.loop(0, d // 256)
        def _(t):
            cols = pl.ds(pl.multiple_of(t * 256, 256), 256)
            gqkv_ref[cols, 0:nqkv] = t_dot(n1_ref[:, cols], dqkv_ref[...]).astype(BF)

        gqkv_ref[:, nqkv:] = grouter_ref[...]

        @pl.loop(0, nq // 128)
        def _(t):
            cols = pl.ds(pl.multiple_of(t * 128, 128), 128)
            gwo_ref[cols, :] = t_dot(attn_ref[:, cols], dproj_ref[...]).astype(BF)

    out_ref[...] = (mixed_ref[...] + os.total()).astype(BF)
    dn = ds.total() * gain_ref[0:1, :]
    xf = x_ref[...].astype(F32)
    r1 = rms_factor(xf)
    gin_ref[...] = (
        dmixed_ref[...] + r1 * dn - xf * (r1 * r1 * r1) * jnp.mean(dn * xf, axis=-1, keepdims=True)).astype(BF)
    if shards:
        spread.got()
        router = 0.0
        for s in range(4):
            piece = land_ref[s].astype(F32)
            gq_ref[:, s * nq:(s + 1) * nq] = piece[:, 0:nq]
            gk_ref[:, s * nk:(s + 1) * nk] = piece[:, nq:nq + nk]
            gv_ref[:, s * nk:(s + 1) * nk] = piece[:, nq + nk:nqkv]
            router = router + piece[:, nqkv:]
        gr_ref[...] = router
        spread.finish()
        wc.finish()
        qc.finish()
    pg.finish()
    ns.finish()
    os.finish()
    ds.finish()


def rest(nq, nk, experts, shards, rows, *args):
    toks, d = args[0].shape
    length = 4 * toks
    nqkv = nq + 2 * nk
    wide = nqkv + 128
    sds = jax.ShapeDtypeStruct
    dma = pltpu.SemaphoreType.DMA
    if shards:
        grads = [sds((rows, 4 * nq), F32), sds((rows, 4 * nk), F32), sds((rows, 4 * nk), F32), sds((rows, 128), F32),
                 sds((rows, d), F32)]
        more = [pltpu.VMEM((4, 2, rows, d), BF)] + [pltpu.VMEM((4, rows, d), BF)] * 3
        more += [pltpu.VMEM((4, 2, 4 * rows, wide), BF)] + [pltpu.VMEM((4, 4 * rows, wide), BF)] * 3
        more += [pltpu.VMEM((4 * rows, wide), F32)] + [pltpu.VMEM((4, rows, wide), BF)] * 2
        more += [dma((2, 12)), dma((2, 12)), dma((2, 4))]
    else:
        grads = [sds((d, wide), BF), sds((nq, d), BF)]
        more = []
    half = pltpu.VMEM((2, toks // 2, d), BF)
    blocks, three = pltpu.VMEM((4, toks, d), BF), pltpu.VMEM((3, toks, d), BF)
    return pl.pallas_call(
        functools.partial(rest_kernel, nq, nk, experts, shards),
        name="rest",
        out_shape=[sds((toks, d), BF), sds((toks, d), BF)] + grads,
        in_specs=[VM] * 7 + [ANY] * 10,
        out_specs=[VM] * (2 + len(grads)),
        scratch_shapes=[
            pltpu.VMEM((length, d), BF), pltpu.VMEM((length, nqkv), BF), pltpu.VMEM((length, nq), BF),
            pltpu.VMEM((8, length), F32), pltpu.VMEM((d, wide), BF), pltpu.VMEM((nq, d), BF),
            pltpu.VMEM((3, toks, d + 128), BF), pltpu.VMEM((3, toks, d + 128), BF), pltpu.VMEM(args[15].shape, BF),
            pltpu.VMEM(args[16].shape, BF),
            pltpu.VMEM((toks, d), F32), pltpu.VMEM((length, d), BF), pltpu.VMEM((length, nq), BF),
            pltpu.VMEM((length, nqkv), BF), pltpu.VMEM((length, nk), F32), pltpu.VMEM((length, nk), F32),
            blocks, pltpu.VMEM((d, 128), BF),
            pltpu.VMEM((2, toks // 2, d + 128), BF), blocks, three, half, three, half,
            dma((2, 6)), dma((2, 4)), dma((2, 6)), dma((2, 6)), dma((13,)),
        ] + more,
        compiler_params=pltpu.CompilerParams(collective_id=3, has_side_effects=True, vmem_limit_bytes=63 * MIB),
        cost_estimate=pl.CostEstimate(flops=60 * 10**9, bytes_accessed=80 * 10**6, transcendentals=4 * 10**6),
    )(*args)


def swap_kernel(own_ref, land_ref, ssem, lsem):
    me = lax.axis_index("seq")
    size = land_ref.shape[1]
    greet(me, 0)
    spread = Spread(me, lambda c: own_ref.at[pl.ds(pl.multiple_of(c * size, 16), size)], land_ref.at[me], ssem, lsem.at[0])
    spread.start()
    spread.got()
    spread.finish()


def swap(own, size):
    return pl.pallas_call(
        swap_kernel,
        name="swap",
        out_shape=jax.ShapeDtypeStruct((4, size, own.shape[1]), BF),
        in_specs=[ANY],
        out_specs=ANY,
        scratch_shapes=[pltpu.SemaphoreType.DMA((2, 4)), pltpu.SemaphoreType.DMA((1,))],
        compiler_params=pltpu.CompilerParams(collective_id=5, has_side_effects=True),
    )(own)


def finish_kernel(gu_ref, low_ref, last_ref, out_in, gin_in, gq_ref, gk_ref, gv_ref, gr_ref, gwo_ref, wq_ref, wk_ref, wv_ref,
                  extra_ref, gate_ref, up_ref,
                  out_ref, gin_ref, gone_ref, q_ref, k_ref, v_ref, o_ref, gtwo_ref, r_ref, ggate_ref, gup_ref, gdown_ref):
    for source, target in (
        (out_in, out_ref), (gin_in, gin_ref), (gq_ref, q_ref), (gk_ref, k_ref), (gv_ref, v_ref), (gwo_ref, o_ref)
    ):
        target[...] = source[...]
    experts, rows, _ = gate_ref.shape
    fc = gu_ref.shape[2] // 2
    low, d = gdown_ref.shape[1:]

    def inner(a, b):
        return jnp.sum(a[...].astype(F32) * b[...], axis=-1, keepdims=True)

    extra = extra_ref[...].astype(F32)

    def row(column):
        return jnp.broadcast_to(column, (rows, 128)).T[0:1, :]

    gain = extra[:, experts:experts + 1]
    gone_ref[...] = row((inner(wq_ref, gq_ref) + inner(wk_ref, gk_ref) + inner(wv_ref, gv_ref)) / gain)
    both = gr_ref[...]
    router = (both + pltpu.roll(both, 128 - experts, 1))[:, 0:experts]
    r_ref[...] = router
    sums = jnp.sum(extra[:, 0:experts] * router, axis=-1, keepdims=True)
    for e in range(experts):
        for s in range(4):
            piece = gu_ref[s, e * rows:(e + 1) * rows, :].astype(F32)
            ggate_ref[e, :, s * fc:(s + 1) * fc] = piece[:, 0:fc]
            gup_ref[e, :, s * fc:(s + 1) * fc] = piece[:, fc:]
        sums = sums + inner(gate_ref.at[e], ggate_ref.at[e]) + inner(up_ref.at[e], gup_ref.at[e])
    gtwo_ref[...] = row(sums / extra[:, experts + 1:experts + 2])
    parts = d // (2 * fc)
    for e in range(experts):
        source, base = (low_ref, e * parts * low) if e < experts - 1 else (last_ref, 4 * experts * rows)
        for c in range(parts):
            at = base + c * low
            gdown_ref[e, :, c * 2 * fc:(c + 1) * 2 * fc] = source[at:at + low, :].astype(F32)


def finish(*args):
    gu, low, last, out, gin, gq, gk, gv, gr, gwo, wq, wk, wv, extra, gate, up = args
    sds = jax.ShapeDtypeStruct
    rows = gq.shape[0]
    column = sds((1, rows), F32)
    experts = gate.shape[0]
    return pl.pallas_call(
        finish_kernel,
        name="finish",
        out_shape=[
            sds(out.shape, BF), sds(gin.shape, BF), column, sds(gq.shape, F32), sds(gk.shape, F32), sds(gv.shape, F32),
            sds(gwo.shape, F32), column, sds((rows, experts), F32), sds(gate.shape, F32), sds(gate.shape, F32),
            sds((experts, low.size // (experts - 1) // gwo.shape[1], gwo.shape[1]), F32),
        ],
        in_specs=[VM] * 16,
        out_specs=[VM] * 12,
        compiler_params=pltpu.CompilerParams(vmem_limit_bytes=56 * MIB),
        cost_estimate=pl.CostEstimate(flops=10**6, bytes_accessed=12 * 10**6, transcendentals=0),
    )(*args)


def shards(x, cot, routes, gain_attn, w_query, w_key, w_value, w_out, gain_ffn, router, w_gate, w_up, w_down):
    n_seq = lax.axis_size("seq")
    n_fsdp = lax.axis_size("fsdp")
    rows, d = w_query.shape
    experts, ff_rows, _ = w_down.shape
    ff = w_gate.shape[2]
    fc = ff // n_seq

    nq, nk = w_query.shape[1] // n_seq, w_key.shape[1] // n_seq
    nqkv = nq + 2 * nk
    inside = n_seq == 4 and n_fsdp == 8 and rows % 16 == 0 and ff_rows % 16 == 0

    extra = jnp.concatenate(
        [router, gain_attn[:, None], gain_ffn[:, None], jnp.zeros((rows, 128 - 2 - experts), BF)], axis=1
    )
    named = routes[0]
    if inside:
        (n1, proj, attn, lse, mixed, n2o, gates, gs, gains, ext, wqkv, wo, gu) = front(
            nq, nk, experts, x[0], cot[0], named, (w_query, w_key, w_value, extra, w_gate, w_up, w_out), True)
        gu = gu.reshape(2, experts, d, fc)
        wd = w_down
    else:
        qkv = jnp.concatenate(
            [w_query.reshape(rows, n_seq, -1), w_key.reshape(rows, n_seq, -1), w_value.reshape(rows, n_seq, -1),
             jnp.broadcast_to(extra[:, None], (rows, n_seq, 128))], axis=2,
        ).transpose(1, 0, 2)
        gu = jnp.stack([w_gate, w_up]).reshape(2, experts, rows, n_seq, fc).transpose(3, 2, 0, 1, 4)
        gu = gu.reshape(n_seq, rows, 2 * experts * fc)
        qkv = lax.all_to_all(qkv, "seq", split_axis=0, concat_axis=0, tiled=True)
        gu = lax.all_to_all(gu, "seq", split_axis=0, concat_axis=0, tiled=True)
        do = jnp.concatenate([w_down.reshape(experts * ff_rows, d), w_out], axis=0)
        wqkv = lax.all_gather(qkv, "fsdp", axis=1).reshape(d, -1)
        do = lax.all_gather(do, "fsdp", axis=0)
        wo = do[:, experts * ff_rows:].reshape(-1, d)
        wd = do[:, : experts * ff_rows].reshape(n_fsdp, experts, ff_rows, d).transpose(1, 0, 2, 3)
        wd = wd.reshape(experts, -1, d)
        gu = lax.all_gather(gu, "fsdp", axis=1).reshape(d, 2, experts, fc).transpose(1, 2, 0, 3)
        (n1, proj, attn, lse, mixed, n2o, gates, gs, gains, ext) = front(
            nq, nk, experts, x[0], cot[0], named, (wqkv, wo), False)

    packed = n_fsdp if inside else 0
    gwd, wd, n2, hg, hid, pre = hidden(experts, packed, n2o, gs, gu, wd)
    if inside:
        gwd = lax.psum_scatter(gwd, "fsdp", scatter_dimension=0, tiled=True)[0]
    else:
        gwd = gwd.reshape(experts, n_fsdp, ff_rows, d).transpose(1, 0, 2, 3).reshape(-1, d)
        gwd = lax.psum_scatter(gwd, "fsdp", scatter_dimension=0, tiled=True).reshape(experts, ff_rows, d)
    ggu, dn2, part = moe(experts, packed, n2, gs, gu, wd, hid, pre, hg)
    if inside:
        ggu, gwd = lax.optimization_barrier((ggu, gwd))
        ggu = lax.psum_scatter(ggu, "fsdp", scatter_dimension=0, tiled=True)[0]
    else:
        ggu = ggu.reshape(n_seq, n_fsdp, rows, experts, 2 * fc).transpose(1, 0, 3, 2, 4)
        ggu = lax.psum_scatter(ggu, "fsdp", scatter_dimension=0, tiled=True).reshape(n_seq, experts * rows, 2 * fc)
    output, gin, *tail = rest(
        nq, nk, experts, packed, rows, x[0], cot[0], mixed, gates, n2o, gains, ext, n1, proj, attn, lse, wqkv, wo, dn2,
        part, hg, wd.reshape(-1, d))
    ggu, tail = lax.optimization_barrier((ggu, tail))
    if inside:
        g_query, g_key, g_value, g_router, gwo = tail
        output, gin, one, g_query, g_key, g_value, gwo, two, g_router, g_gate, g_up, gwd = finish(
            swap(ggu, experts * rows), gwd, ggu, output, gin, g_query, g_key, g_value, g_router, gwo, w_query, w_key, w_value,
            extra, w_gate, w_up)
        return (
            output[None], gin[None], one[0], g_query, g_key, g_value, gwo, two[0], g_router, g_gate, g_up, gwd,
        )
    else:
        ggu = lax.all_to_all(ggu, "seq", split_axis=0, concat_axis=0, tiled=True)
        gqkv, gwo = tail
        gwo = lax.psum_scatter(gwo, "fsdp", scatter_dimension=0, tiled=True)
        gqkv = gqkv.reshape(n_seq, n_fsdp, rows, -1).transpose(1, 0, 2, 3).reshape(n_fsdp * n_seq * rows, -1)
        gqkv = lax.psum_scatter(gqkv, "fsdp", scatter_dimension=0, tiled=True).reshape(n_seq, rows, -1)
        gqkv = lax.all_to_all(gqkv, "seq", split_axis=0, concat_axis=0, tiled=True)
        gqkv = gqkv.astype(F32)
        g_query = gqkv[:, :, :nq].transpose(1, 0, 2).reshape(rows, -1)
        g_key = gqkv[:, :, nq: nq + nk].transpose(1, 0, 2).reshape(rows, -1)
        g_value = gqkv[:, :, nq + nk: nqkv].transpose(1, 0, 2).reshape(rows, -1)
        g_router = jnp.sum(gqkv[:, :, nqkv: nqkv + experts] + gqkv[:, :, nqkv + experts: nqkv + 2 * experts], axis=0)
    ggu = ggu.astype(F32).reshape(n_seq, experts, rows, 2, fc).transpose(3, 1, 2, 0, 4).reshape(2, experts, rows, ff)
    g_gate, g_up = ggu[0], ggu[1]
    g_gain_one = (
        jnp.sum(w_query.astype(F32) * g_query, axis=1) + jnp.sum(w_key.astype(F32) * g_key, axis=1)
        + jnp.sum(w_value.astype(F32) * g_value, axis=1)
    ) / gain_attn.astype(F32)
    g_gain_two = (
        jnp.sum(w_gate.astype(F32) * g_gate + w_up.astype(F32) * g_up, axis=(0, 2))
        + jnp.sum(router.astype(F32) * g_router, axis=1)
    ) / gain_ffn.astype(F32)
    return (
        output[None], gin[None], g_gain_one, g_query, g_key, g_value, gwo.astype(F32), g_gain_two, g_router,
        g_gate, g_up, gwd.astype(F32),
    )


def solution(mesh):
    tok = P("fsdp", "seq", None)
    vec = P(("seq", "fsdp"))
    mat = P(("seq", "fsdp"), None)
    exp = P(None, ("seq", "fsdp"), None)
    return jax.shard_map(
        shards,
        mesh=mesh,
        in_specs=(tok, tok, tok, vec, mat, mat, mat, mat, vec, mat, exp, exp, exp),
        out_specs=(tok, tok, vec, mat, mat, mat, mat, vec, mat, exp, exp, exp),
        check_vma=False,
    )
```

```python
import functools

import jax
import jax.numpy as jnp
from jax import lax
from jax.experimental import pallas as pl
from jax.experimental.pallas import tpu as pltpu
from jax.sharding import PartitionSpec as P

HEAD_DIM = 64
EPS = 1e-06
SCALE = HEAD_DIM ** (-0.5)
BF = jnp.bfloat16
F32 = jnp.float32
MESH = pl.DeviceIdType.MESH
ANY = pl.BlockSpec(memory_space=pl.ANY)
VM = pl.BlockSpec(memory_space=pltpu.VMEM)
MIB = 2**20


def dot(a, b):
    return jnp.dot(a, b, preferred_element_type=F32)


def dot_t(a, b):
    return lax.dot_general(a, b, (((1,), (1,)), ((), ())), preferred_element_type=F32)


def t_dot(a, b):
    return lax.dot_general(a, b, (((0,), (0,)), ((), ())), preferred_element_type=F32)


def rms_factor(rows):
    return lax.rsqrt(jnp.mean(rows * rows, axis=-1, keepdims=True) + EPS)


def partner(me, step):
    return ((me // 2 + step // 2) % 2) * 2 + (me % 2 + step % 2) % 2


def send(src, dst, sems, slot, peer):
    return pltpu.make_async_remote_copy(
        src_ref=src, dst_ref=dst, send_sem=sems.at[0, slot], recv_sem=sems.at[1, slot],
        device_id={"seq": peer}, device_id_type=MESH,
    )


def greet(me, others):
    barrier = pltpu.get_barrier_semaphore()
    for step in (1, 2, 3):
        pl.semaphore_signal(barrier, inc=1, device_id={"seq": partner(me, step)}, device_id_type=MESH)
    pl.semaphore_wait(barrier, 3 + others)


class Gather:
    def __init__(self, me, own, buf, sems, base=0):
        rows = own.shape[0]
        half = rows // 2
        one, two = partner(me, 1), partner(me, 2)

        def part(owner, start, size):
            return buf.at[pl.ds(pl.multiple_of(owner * rows + start, half), size)]

        mine = part(me, 0, rows)
        self.first = send(own, mine, sems, base, one)
        self.second = send(own, mine, sems, base + 1, two)
        onward = part(one, 0, half)
        self.third = send(onward, onward, sems, base + 2, two)
        onward = part(two, half, half)
        self.fourth = send(onward, onward, sems, base + 3, one)

    def start(self):
        self.first.start()
        self.second.start()

    def got_one(self):
        self.first.wait_recv()
        self.third.start()

    def got_two(self):
        self.second.wait_recv()
        self.fourth.start()

    def got_three(self):
        self.third.wait_recv()
        self.fourth.wait_recv()

    def finish(self):
        for copy in (self.first, self.second, self.third, self.fourth):
            copy.wait_send()


class Scatter:
    def __init__(self, me, parts, got, held, sems, extra=0, kind="whole"):
        half = parts.shape[1] // 2
        one, two = partner(me, 1), partner(me, 2)
        self.top, self.low = pl.ds(0, half), pl.ds(half, half)
        self.parts, self.got, self.held, self.extra = parts, got, held, extra

        def copy(slot, step, rows, peer, src=None):
            return send(parts.at[step, rows] if src is None else src, got.at[step - 1, rows], sems, slot, peer)

        self.early = self.late = ()
        if kind != "late":
            self.far_top = copy(0, 3, self.top, one)
            self.far_low = copy(1, 3, self.low, two)
            self.one_top = copy(2, 1, self.top, one)
            self.two_low = copy(3, 2, self.low, two)
            self.early = (self.far_top, self.far_low, self.one_top, self.two_low)
        if kind != "early":
            self.one_low = copy(4, 1, self.low, one, held.at[0])
            self.two_top = copy(5, 2, self.top, two, held.at[1])
            self.late = (self.one_low, self.two_top)

    def start(self, step):
        @pl.when(step == 3)
        def _():
            self.far_top.start()
            self.far_low.start()

        pl.when(step == 2)(self.two_low.start)
        pl.when(step == 1)(self.one_top.start)

    def onward(self):
        for slot, step, rows, arrived, copy in ((0, 1, self.low, 1, self.one_low), (1, 2, self.top, 0, self.two_top)):
            if self.early:
                self.early[arrived].wait_recv()
            both = self.parts[step, rows, :].astype(F32) + self.got[2, rows, :].astype(F32)
            self.held[slot] = both.astype(BF)
            if self.extra:
                tail = both[:, -128:]
                whole = tail + pltpu.roll(tail, 128 - self.extra, 1)
                self.held[slot, :, -128:] = pack_two(jnp.where(lanes(tail.shape) < self.extra, whole, 0.0), self.extra)
            copy.start()

    def arrive(self):
        for copy in self.early[2:] + self.late:
            copy.wait_recv()

    def total(self):
        self.arrive()
        return self.parts[0].astype(F32) + self.got[0].astype(F32) + self.got[1].astype(F32)

    def finish(self):
        for copy in self.early + self.late:
            copy.wait_send()


def lanes(shape):
    return lax.broadcasted_iota(jnp.int32, shape, len(shape) - 1)


def pack_two(value, experts):
    high = value.astype(BF).astype(F32)
    low = value - high
    return jnp.where(lanes(value.shape) < experts, high, pltpu.roll(low, experts, 1)).astype(BF)


class Line:
    def __init__(self, region, sems):
        me = lax.axis_index("fsdp")
        self.last = lax.axis_size("fsdp") // 2 - 1
        self.z, self.core = me // 2, me % 2
        self.region, self.sems = region, sems

    def copy(self, slot, plane, core, target):
        part = self.region(plane * 2 + core)
        return pltpu.make_async_remote_copy(
            src_ref=part, dst_ref=part, send_sem=self.sems.at[0, slot], recv_sem=self.sems.at[1, slot],
            device_id={"fsdp": target}, device_id_type=MESH,
        )

    def up(self, hop):
        return self.copy(hop, self.z - hop, self.core, (self.z + 1) * 2 + self.core)

    def from_below(self, hop):
        return self.copy(hop, self.z - 1 - hop, self.core, self.z * 2 + self.core)

    def down(self, hop):
        return self.copy(3 + hop, self.z + hop, self.core, (self.z - 1) * 2 + self.core)

    def from_above(self, hop):
        return self.copy(3 + hop, self.z + 1 + hop, self.core, self.z * 2 + self.core)

    def across(self, plane):
        return self.copy(6 + plane, plane, self.core, self.z * 2 + 1 - self.core)

    def from_across(self, plane):
        return self.copy(6 + plane, plane, 1 - self.core, self.z * 2 + self.core)

    def start(self):
        pl.when(self.z < self.last)(lambda: self.up(0).start())
        pl.when(self.z > 0)(lambda: self.down(0).start())
        self.across(self.z).start()

    def step(self, hop):
        @pl.when(self.z > hop)
        def _():
            self.from_below(hop).wait_recv()
            if hop < 2:
                pl.when(self.z < self.last)(lambda: self.up(hop + 1).start())
            self.across(self.z - 1 - hop).start()

        @pl.when(self.z + hop < self.last)
        def _():
            self.from_above(hop).wait_recv()
            if hop < 2:
                pl.when(self.z > 0)(lambda: self.down(hop + 1).start())
            self.across(self.z + 1 + hop).start()

    def land(self):
        for plane in range(4):
            self.from_across(plane).wait_recv()

    def finish(self):
        for hop in range(3):
            pl.when((self.z >= hop) & (self.z < self.last))(lambda hop=hop: self.up(hop).wait_send())
            pl.when((self.z + hop <= self.last) & (self.z > 0))(lambda hop=hop: self.down(hop).wait_send())
        for plane in range(4):
            self.across(plane).wait_send()


class Collect:
    def __init__(self, mine, cross, below, above, sems):
        me = lax.axis_index("fsdp")
        self.z, self.core = me // 2, me % 2
        self.mine, self.cross, self.below, self.above, self.sems = mine, cross, below, above, sems

    def copy(self, slot, src, dst, target):
        return pltpu.make_async_remote_copy(
            src_ref=src, dst_ref=dst, send_sem=self.sems.at[0, slot], recv_sem=self.sems.at[1, slot],
            device_id={"fsdp": target}, device_id_type=MESH,
        )

    def over(self, plane):
        return self.copy(plane, self.mine.at[plane, 1 - self.core], self.cross.at[plane], self.z * 2 + 1 - self.core)

    def up(self, plane, src):
        return self.copy(4 + plane, src.at[plane], self.below.at[plane], (self.z + 1) * 2 + self.core)

    def down(self, plane, src):
        return self.copy(8 + plane, src.at[plane], self.above.at[plane], (self.z - 1) * 2 + self.core)

    def start(self):
        for plane in range(4):
            self.over(plane).start()

    def combine(self):
        for plane in (3, 0, 2, 1):
            self.over(plane).wait_recv()
            both = self.mine[plane, self.core].astype(F32) + self.cross[plane].astype(F32)
            self.cross[plane] = both.astype(BF)

            if plane == 3:
                pl.when(self.z == 0)(self.up(3, self.cross).start)
            if plane == 0:
                pl.when(self.z == 3)(self.down(0, self.cross).start)

    def step(self, turn):
        high, low = 3 - turn, turn
        z = self.z

        if turn < 2:

            @pl.when(z == 0)
            def _():
                self.up(high, self.cross).wait_send()
                self.up(high - 1, self.cross).start()

            @pl.when(z == 3)
            def _():
                self.down(low, self.cross).wait_send()
                self.down(low + 1, self.cross).start()

        @pl.when((z > 0) & (z <= high))
        def _():
            self.up(high, self.below).wait_recv()

        @pl.when((z > 0) & (z < high))
        def _():
            self.below[high] = (self.below[high].astype(F32) + self.cross[high].astype(F32)).astype(BF)
            self.up(high, self.below).start()

        @pl.when((z < 3) & (z >= low))
        def _():
            self.down(low, self.above).wait_recv()

        @pl.when((z < 3) & (z > low))
        def _():
            self.above[low] = (self.above[low].astype(F32) + self.cross[low].astype(F32)).astype(BF)
            self.down(low, self.above).start()

    def total(self, out):
        z = self.z
        out[...] = self.cross[z].astype(F32)

        @pl.when(z > 0)
        def _():
            out[...] += self.below[z].astype(F32)

        @pl.when(z < 3)
        def _():
            out[...] += self.above[z].astype(F32)

    def finish(self):
        z = self.z
        for plane in range(4):
            self.over(plane).wait_send()
            pl.when((z > 0) & (z < 3) & (z < plane))(self.up(plane, self.below).wait_send)
            pl.when((z > 0) & (z < 3) & (z > plane))(self.down(plane, self.above).wait_send)
        pl.when(z == 0)(self.up(1, self.cross).wait_send)
        pl.when(z == 3)(self.down(2, self.cross).wait_send)


def load(pairs, sems, first=0):
    copies = [pltpu.make_async_copy(a, b, sems.at[first + i]) for i, (a, b) in enumerate(pairs)]
    for copy in copies:
        copy.start()
    return copies


def greet_line():
    me = lax.axis_index("fsdp")
    last = lax.axis_size("fsdp") // 2 - 1
    z, core = me // 2, me % 2
    barrier = pltpu.get_barrier_semaphore()

    @pl.when(z < last)
    def _():
        pl.semaphore_signal(barrier, inc=1, device_id={"fsdp": me + 2}, device_id_type=MESH)

    @pl.when(z > 0)
    def _():
        pl.semaphore_signal(barrier, inc=1, device_id={"fsdp": me - 2}, device_id_type=MESH)

    pl.semaphore_signal(barrier, inc=1, device_id={"fsdp": z * 2 + 1 - core}, device_id_type=MESH)
    return 1 + jnp.minimum(z, 1) + jnp.minimum(last - z, 1)


class Spread:
    def __init__(self, me, chunk, place, sems, local):
        self.copies = [send(chunk(partner(me, step)), place, sems, step, partner(me, step)) for step in (3, 2, 1)]
        self.local = pltpu.make_async_copy(chunk(me), place, local)

    def start(self):
        self.local.start()
        for copy in self.copies:
            copy.start()

    def got(self):
        self.local.wait()
        for copy in self.copies:
            copy.wait_recv()

    def finish(self):
        for copy in self.copies:
            copy.wait_send()


def front_kernel(nq, nk, experts, inside, *refs):
    if inside:
        (x_ref, g_ref, named_ref, query_own, key_own, value_own, extra_wide, gate_own, up_own, woo_ref,
         n1_out, qkv_out, attn_out, lse_ref, mixed_ref, n2_ref, gate_ref, gs_ref, gain_ref, ext_ref, wqkv_out, wo_out,
         gu_ref, n1_ref, qkv_ref, attn_ref, vsem, wqkv_ref, wo_ref, extra_own,
         cols_ref, xs_ref, send_ref, recv_ref, held_ref, xsem, gsem, asem, lsem, qw_ref, spread_sem, line_sem) = refs
    else:
        (x_ref, g_ref, named_ref, wqkv_ref, wo_ref,
         n1_out, qkv_out, attn_out, lse_ref, mixed_ref, n2_ref, gate_ref, gs_ref, gain_ref, ext_ref,
         n1_ref, qkv_ref, attn_ref, vsem,
         cols_ref, xs_ref, send_ref, recv_ref, held_ref, xsem, gsem, asem, lsem) = refs
    me = lax.axis_index("seq")
    toks, d = x_ref.shape
    group = nq // nk
    nqkv = nq + 2 * nk
    xg = Gather(me, x_ref, xs_ref, xsem)
    gg = Gather(me, g_ref, gs_ref, gsem)
    keep = pltpu.make_async_copy(g_ref, gs_ref.at[pl.ds(pl.multiple_of(me * toks, toks), toks)], lsem.at[0])
    keep.start()
    ao = Scatter(me, send_ref, recv_ref, held_ref, asem)
    if inside:
        shard = lax.axis_index("fsdp")
        rows = woo_ref.shape[0]
        extra_own[...] = extra_wide[...].astype(F32).T[0:rows, :].astype(BF)
        greet(me, greet_line())
        qkv_line = Line(lambda f: qw_ref.at[:, f], line_sem.at[0])
        wo_line = Line(lambda f: wo_ref.at[pl.ds(pl.multiple_of(f * rows, 16), rows)], line_sem.at[1])
        gu_line = Line(lambda f: gu_ref.at[:, :, :, f], line_sem.at[2])
        spreads = []

        def spread(own, width, place):
            def chunk(c):
                cols = pl.ds(pl.multiple_of(c * width, 128), width)
                return own.at[:, cols] if len(own.shape) == 2 else own.at[:, :, cols]

            at = len(spreads)
            spreads.append(Spread(me, chunk if width else lambda c: own, place, spread_sem.at[at], lsem.at[2 + at]))

        spread(query_own, nq, qw_ref.at[me, shard, :, pl.ds(0, nq)])
        spread(key_own, nk, qw_ref.at[me, shard, :, pl.ds(nq, nk)])
        spread(value_own, nk, qw_ref.at[me, shard, :, pl.ds(nq + nk, nk)])
        spread(extra_own, 0, qw_ref.at[me, shard, :, pl.ds(nqkv, 128)])
        spread(gate_own, gate_own.shape[2] // 4, gu_ref.at[0, :, me, shard])
        spread(up_own, gate_own.shape[2] // 4, gu_ref.at[1, :, me, shard])
        place_wo = pltpu.make_async_copy(woo_ref, wo_line.region(shard), lsem.at[1])
        for one in spreads[:4]:
            one.start()
        place_wo.start()
        xg.start()
        for one in spreads[4:]:
            one.start()
        for one in spreads[:4]:
            one.got()
        qkv_line.start()
        place_wo.wait()
        xs_ref[pl.ds(pl.multiple_of(me * toks, toks), toks), :] = x_ref[...]
        qkv_line.step(0)
        qkv_line.step(1)
        wo_line.start()
        for one in spreads[4:]:
            one.got()
        gu_line.start()
        xg.got_one()
        xg.got_two()
        qkv_line.step(2)
        wo_line.step(0)
        qkv_line.land()
        wo_line.step(1)
        xg.got_three()
        gg.start()
        for s in range(4):
            for f in range(8):
                wqkv_ref[s * 8 * rows + f * rows: s * 8 * rows + (f + 1) * rows, :] = qw_ref[s, f]
    else:
        greet(me, 0)
        xg.start()
        xs_ref[pl.ds(pl.multiple_of(me * toks, toks), toks), :] = x_ref[...]
        xg.got_one()
        xg.got_two()
        xg.got_three()
        gg.start()
    ext = wqkv_ref[:, nqkv:]
    ext_ref[...] = ext
    gain_ref[...] = ext.astype(F32).T[experts:experts + 2, :]
    gain1 = gain_ref[0:1, :]
    cols_ref[...] = jnp.zeros_like(cols_ref)

    @pl.loop(0, 4)
    def _(block):
        rows = pl.ds(pl.multiple_of(block * toks, toks), toks)
        xf = xs_ref[rows, :].astype(F32)
        n1_ref[rows, :] = (xf * rms_factor(xf) * gain1).astype(BF)
        proj = dot(n1_ref[rows, :], wqkv_ref[:, 0:nqkv]).astype(BF)
        qkv_ref[rows, :] = proj

    saves = load([(n1_ref, n1_out), (qkv_ref, qkv_out)], vsem)
    if inside:
        wo_line.step(2)
        gu_line.step(0)
        wo_line.land()
        saves += load([(wqkv_ref, wqkv_out), (wo_ref, wo_out)], vsem, 3)

    @pl.loop(0, 4)
    def _(turn):
        step = 3 - turn
        block = partner(me, step)
        rows = pl.ds(pl.multiple_of(block * toks, toks), toks)

        for b in range(4):

            @pl.when(block == b)
            def _(b=b):
                upto = b * toks
                qrows = slice(upto, upto + toks)
                inside = lanes((toks, toks)) <= lax.broadcasted_iota(jnp.int32, (toks, toks), 0)
                for h in range(nq // HEAD_DIM):
                    g = h // group
                    q = qkv_ref[qrows, h * HEAD_DIM:(h + 1) * HEAD_DIM] * SCALE
                    kc = slice(nq + g * HEAD_DIM, nq + (g + 1) * HEAD_DIM)
                    vc = slice(nq + nk + g * HEAD_DIM, nq + nk + (g + 1) * HEAD_DIM)
                    near = jnp.where(inside, dot_t(q, qkv_ref[qrows, kc]), -1e30)
                    top = jnp.max(near, axis=-1, keepdims=True)
                    if b:
                        far = dot_t(q, qkv_ref[0:upto, kc])
                        top = jnp.maximum(top, jnp.max(far, axis=-1, keepdims=True))
                    near = jnp.exp(near - top)
                    total = jnp.sum(near, axis=-1, keepdims=True)
                    if b:
                        far = jnp.exp(far - top)
                        total = total + jnp.sum(far, axis=-1, keepdims=True)
                    inv = 1.0 / total
                    res = dot((near * inv).astype(BF), qkv_ref[qrows, vc])
                    if b:
                        res = res + dot((far * inv).astype(BF), qkv_ref[0:upto, vc])
                    attn_ref[qrows, h * HEAD_DIM:(h + 1) * HEAD_DIM] = res.astype(BF)
                    cols_ref[qrows, h:h + 1] = top + jnp.log(total)

        send_ref[step] = dot(attn_ref[rows, :], wo_ref[...]).astype(BF)

        ao.start(step)

    saves += load([(attn_ref, attn_out)], vsem, 2)
    ao.onward()
    gg.got_one()
    gg.got_two()
    lse_ref[...] = cols_ref[...].T[0:8, :]
    if inside:
        gu_line.step(1)
    mixed = x_ref[...].astype(F32) + ao.total()
    if inside:
        gu_line.step(2)
    mixed_ref[...] = mixed
    n2 = (mixed * rms_factor(mixed) * gain_ref[1:2, :]).astype(BF)
    n2_ref[:, 0:d] = n2
    logits = dot(n2, ext_ref[...])
    expert = lax.broadcasted_iota(jnp.int32, (128, toks), 0)
    hit = (expert == named_ref[0:1, :]) | (expert == named_ref[1:2, :])
    named = jnp.where(hit, 1.0, 0.0).T > 0.0
    top = jnp.max(jnp.where(named, logits, -1e30), axis=-1, keepdims=True)
    weight = jnp.where(named, jnp.exp(jnp.minimum(logits - top, 0.0)), 0.0)
    gates = weight / jnp.sum(weight, axis=-1, keepdims=True)
    gate_ref[...] = gates
    n2_ref[:, d:] = pack_two(gates, experts)
    gg.got_three()
    gg.finish()
    xg.finish()
    keep.wait()
    for copy in saves:
        copy.wait()
    ao.finish()
    if inside:
        gu_line.land()
        for line in (qkv_line, wo_line, gu_line):
            line.finish()
        for one in spreads:
            one.finish()


def front(nq, nk, experts, x, g, named, weights, inside):
    toks, d = x.shape
    length = 4 * toks
    nqkv = nq + 2 * nk
    sds = jax.ShapeDtypeStruct
    out_shape = [
        sds((length, d), BF), sds((length, nqkv), BF), sds((length, nq), BF), sds((8, length), F32),
        sds((toks, d), F32), sds((toks, d + 128), BF), sds((toks, 128), F32), sds((length, d), BF),
        sds((2, d), F32), sds((d, 128), BF),
    ]
    in_specs = [VM] * 5
    out_specs = [ANY] * 3 + [VM] * 4 + [ANY] + [VM] * 2
    scratch = [
        pltpu.VMEM((length, d), BF), pltpu.VMEM((length, nqkv), BF), pltpu.VMEM((length, nq), BF),
        pltpu.SemaphoreType.DMA((5,)),
    ]
    if inside:
        scratch += [
            pltpu.VMEM((d, nqkv + 128), BF), pltpu.VMEM((nq, d), BF), pltpu.VMEM((weights[0].shape[0], 128), BF)]
    scratch += [
        pltpu.VMEM((length, 128), F32), pltpu.VMEM((length, d), BF), pltpu.VMEM((4, toks, d), BF),
        pltpu.VMEM((3, toks, d), BF), pltpu.VMEM((2, toks // 2, d), BF),
        pltpu.SemaphoreType.DMA((2, 4)), pltpu.SemaphoreType.DMA((2, 4)), pltpu.SemaphoreType.DMA((2, 6)),
        pltpu.SemaphoreType.DMA((8,)),
    ]
    if inside:
        query, key, value, extra, gate, up, woo = weights
        rows, fc = query.shape[0], gate.shape[2] // 4
        in_specs = [VM] * 3 + [ANY] * 3 + [VM] + [ANY] * 3
        out_shape += [sds((d, nqkv + 128), BF), sds((nq, d), BF), sds((2, experts, 4, 8, rows, fc), BF)]
        out_specs += [ANY, ANY, ANY]
        scratch += [
            pltpu.VMEM((4, 8, rows, nqkv + 128), BF), pltpu.SemaphoreType.DMA((6, 2, 4)),
            pltpu.SemaphoreType.DMA((3, 2, 10)),
        ]
    return pl.pallas_call(
        functools.partial(front_kernel, nq, nk, experts, inside),
        name="front",
        out_shape=out_shape,
        in_specs=in_specs,
        out_specs=out_specs,
        scratch_shapes=scratch,
        compiler_params=pltpu.CompilerParams(collective_id=1, has_side_effects=True, vmem_limit_bytes=60 * MIB),
        cost_estimate=pl.CostEstimate(flops=20 * 10**9, bytes_accessed=60 * 10**6, transcendentals=4 * 10**6),
    )(x, g, named, *weights)


def hidden_kernel(experts, shards, *refs):
    (n2o_ref, gs_hbm, gu_hbm, wd_hbm, gwd_ref, wd_out, n2_out, hg_out, hid_out, pre_out,
     n2_ref, gs_ref, gu_ref, wd_ref, pre_ref, hid_ref, hg_ref, grad_ref, nsem, lsem, ssem) = refs[:21]
    me = lax.axis_index("seq")
    toks, de = n2o_ref.shape
    d = de - 128
    length, ff = hg_ref.shape
    fc = ff // experts
    load_gu = load(
        [(gu_hbm.at[m, e], gu_ref.at[:, pl.ds((2 * e + m) * fc, fc)]) for e in range(experts) for m in range(2)], lsem, 6)
    (load_gs,) = load([(gs_hbm, gs_ref)], lsem, 1)
    if shards:
        (wsem,) = refs[21:]
        wd_line = Line(lambda f: wd_ref.at[:, f], wsem)
        (load_wd,) = load([(wd_hbm, wd_ref.at[:, lax.axis_index("fsdp")])], lsem, 2)
        greet(me, greet_line())
        load_wd.wait()
        wd_line.start()
    else:
        (load_wd,) = load([(wd_hbm, wd_ref)], lsem, 2)
        greet(me, 0)
        load_wd.wait()
    ng = Gather(me, n2o_ref, n2_ref, nsem)
    ng.start()
    for copy in load_gu:
        copy.wait()

    def gate_of(rows, e):
        packed = n2_ref[rows, d:].astype(F32)
        lane = lanes(packed.shape)
        return jnp.sum(jnp.where((lane == e) | (lane == e + experts), packed, 0.0), axis=-1, keepdims=True)

    def saves(step):
        rows = pl.ds(pl.multiple_of(partner(me, step) * toks, toks), toks)
        return [
            pltpu.make_async_copy(a.at[rows], b.at[rows], ssem.at[i, step])
            for i, (a, b) in enumerate(((hg_ref, hg_out), (hid_ref, hid_out), (pre_ref, pre_out), (n2_ref, n2_out)))
        ]

    @pl.loop(0, 4)
    def _(step):
        block = partner(me, step)
        rows = pl.ds(pl.multiple_of(block * toks, toks), toks)

        @pl.when(step == 0)
        def _():
            n2_ref[rows, :] = n2o_ref[...]

        @pl.when(step == 1)
        def _():
            if shards:
                wd_line.step(0)
            ng.got_one()

        @pl.when(step == 2)
        def _():
            ng.got_two()
            if shards:
                wd_line.step(1)

        @pl.when(step == 3)
        def _():
            ng.got_three()
            if shards:
                wd_line.step(2)

        @pl.loop(0, experts)
        def _(e):
            cols = pl.ds(pl.multiple_of(e * 2 * fc, 2 * fc), 2 * fc)
            hcols = pl.ds(pl.multiple_of(e * fc, fc), fc)
            pre = dot(n2_ref[rows, 0:d], gu_ref[:, cols])
            gp, up = pre[:, 0:fc], pre[:, fc:]
            sig = 1.0 / (1.0 + jnp.exp(-gp))
            act = gp * sig
            hid = (act * up).astype(BF)
            hid_ref[rows, hcols] = hid
            hg_ref[rows, hcols] = (gate_of(rows, e) * hid.astype(F32)).astype(BF)
            pre_ref[rows, pl.ds(pl.multiple_of(e * 2 * fc, fc), fc)] = up * sig * (1.0 + gp * (1.0 - sig))
            pre_ref[rows, pl.ds(pl.multiple_of(e * 2 * fc + fc, fc), fc)] = act

        for copy in saves(step):
            copy.start()

    load_gs.wait()
    if shards:
        low, wide = fc // shards, 2 * fc
        parts = d // wide

        @pl.loop(0, experts - 1)
        def _(e):
            cols = pl.ds(pl.multiple_of(e * fc, fc), fc)
            grad = t_dot(hg_ref[:, cols], gs_ref[...]).astype(BF)
            for f in range(shards):
                for c in range(parts):
                    at = pl.ds(pl.multiple_of((e * parts + c) * low, 16), low)
                    grad_ref[f, at, :] = grad[f * low:(f + 1) * low, c * wide:(c + 1) * wide]

        wd_line.land()
    else:

        @pl.loop(0, experts)
        def _(e):
            cols = pl.ds(pl.multiple_of(e * fc, fc), fc)
            grad_ref[cols, :] = t_dot(hg_ref[:, cols], gs_ref[...]).astype(BF)

    last = load([(grad_ref, gwd_ref), (wd_ref, wd_out)], lsem, 3)
    for step in range(4):
        for copy in saves(step):
            copy.wait()
    for copy in last:
        copy.wait()
    ng.finish()
    if shards:
        wd_line.finish()


def hidden(experts, shards, n2o, gs, gu, wd):
    toks, de = n2o.shape
    d = de - 128
    length = 4 * toks
    fc = gu.shape[3]
    ff = experts * fc
    sds = jax.ShapeDtypeStruct
    dma = pltpu.SemaphoreType.DMA
    whole = (experts, shards, fc // shards, d) if shards else (experts, fc, d)
    grad = (shards, (ff - fc) * d // (2 * fc) // shards, 2 * fc) if shards else (ff, d)
    return pl.pallas_call(
        functools.partial(hidden_kernel, experts, shards),
        name="hidden",
        out_shape=[
            sds(grad, BF), sds(whole, BF), sds((length, de), BF), sds((length, ff), BF), sds((length, ff), BF),
            sds((length, 2 * ff), F32),
        ],
        in_specs=[VM] + [ANY] * 3,
        out_specs=[ANY] * 6,
        scratch_shapes=[
            pltpu.VMEM((length, de), BF), pltpu.VMEM((length, d), BF), pltpu.VMEM((d, 2 * ff), BF),
            pltpu.VMEM(whole, BF), pltpu.VMEM((length, 2 * ff), F32), pltpu.VMEM((length, ff), BF),
            pltpu.VMEM((length, ff), BF), pltpu.VMEM(grad, BF),
            dma((2, 4)), dma((6 + 2 * experts,)), dma((4, 4)),
        ] + ([dma((2, 10))] if shards else []),
        compiler_params=pltpu.CompilerParams(collective_id=2, has_side_effects=True, vmem_limit_bytes=60 * MIB),
        cost_estimate=pl.CostEstimate(flops=20 * 10**9, bytes_accessed=50 * 10**6, transcendentals=4 * 10**6),
    )(n2o, gs, gu, wd)


def moe_kernel(experts, shards, n2_hbm, gs_hbm, gu_hbm, wd_hbm, hid_hbm, pre_hbm, hg_hbm, ggu_ref, dn2_ref, part_ref,
               n2_ref, gs_ref, gu_ref, wd_ref, pre_ref, hid_ref, dpre_ref, grad_ref, hg_ref, dsem, lsem, bsem):
    me = lax.axis_index("seq")
    length, d = gs_ref.shape
    toks = length // 4
    ff = hid_ref.shape[1]
    fc = ff // experts
    (load_wd,) = load([(wd_hbm, wd_ref)], lsem, 0)

    def blocks(step):
        rows = pl.ds(pl.multiple_of(partner(me, step) * toks, toks), toks)
        return [
            pltpu.make_async_copy(a.at[rows], b.at[rows], bsem.at[i, step])
            for i, (a, b) in enumerate(((n2_hbm, n2_ref), (gs_hbm, gs_ref), (hid_hbm, hid_ref), (pre_hbm, pre_ref)))
        ]

    for copy in blocks(3):
        copy.start()
    load_gu = load(
        [(gu_hbm.at[m, e], gu_ref.at[:, pl.ds((2 * e + m) * fc, fc)]) for e in range(experts) for m in range(2)], lsem, 6)
    for step in (2, 1, 0):
        for copy in blocks(step):
            copy.start()
    (load_hg,) = load([(hg_hbm.at[:, pl.ds(ff - fc, fc)], hg_ref)], lsem, 5)
    greet(me, 0)
    ns = Scatter(me, dn2_ref, part_ref, None, dsem, experts, "early")
    load_wd.wait()

    @pl.loop(0, 4)
    def _(turn):
        step = 3 - turn
        rows = pl.ds(pl.multiple_of(partner(me, step) * toks, toks), toks)
        for copy in blocks(step):
            copy.wait()

        def one_expert(e, dgate):
            hcols = pl.ds(pl.multiple_of(e * fc, fc), fc)
            left = pl.ds(pl.multiple_of(e * 2 * fc, fc), fc)
            right = pl.ds(pl.multiple_of(e * 2 * fc + fc, fc), fc)
            packed = n2_ref[rows, d:].astype(F32)
            lane = lanes(packed.shape)
            gate = jnp.sum(jnp.where((lane == e) | (lane == e + experts), packed, 0.0), axis=-1, keepdims=True)
            dh0 = dot_t(gs_ref[rows, :], wd_ref[e].reshape(fc, d))
            dh = gate * dh0
            dpre_ref[rows, left] = (dh * pre_ref[rows, left]).astype(BF)
            dpre_ref[rows, right] = (dh * pre_ref[rows, right]).astype(BF)
            sums = jnp.sum(hid_ref[rows, hcols].astype(F32) * dh0, axis=-1, keepdims=True)
            return dgate + jnp.where(lane == e, sums, 0.0)

        dgate = lax.fori_loop(0, experts, one_expert, jnp.zeros((toks, 128), F32), unroll=True)
        dn2_ref[step, :, d:] = pack_two(dgate, experts)

        @pl.when(turn == 0)
        def _():
            for copy in load_gu:
                copy.wait()

        tile = 512

        @pl.loop(0, d // tile)
        def _(t):
            cols = pl.ds(pl.multiple_of(t * tile, tile), tile)
            dn2_ref[step, :, cols] = dot_t(dpre_ref[rows, :], gu_ref[cols, :]).astype(BF)

        ns.start(step)

    if shards:
        rows, wide = d // 4 // shards, 2 * fc

        def save(s):
            part = pl.ds(pl.multiple_of(s * experts * rows, 16), experts * rows)
            return pltpu.make_async_copy(grad_ref.at[:, part], ggu_ref.at[:, part], lsem.at[1 + s])

        low, parts = fc // shards, d // wide
        base = 4 * experts * rows
        load_hg.wait()
        grad = t_dot(hg_ref[...], gs_ref[...]).astype(BF)
        for f in range(shards):
            for c in range(parts):
                at = base + c * low
                grad_ref[f, at:at + low, :] = grad[f * low:(f + 1) * low, c * wide:(c + 1) * wide]
        rest_part = pl.ds(base, parts * low)
        (save_last,) = load([(grad_ref.at[:, rest_part], ggu_ref.at[:, rest_part])], lsem, 0)

        @pl.loop(0, 4)
        def _(s):
            cols = pl.ds(pl.multiple_of(s * (d // 4), 128), d // 4)
            grad = t_dot(n2_ref[:, cols], dpre_ref[...]).astype(BF)
            for f in range(shards):
                for e in range(experts):
                    at = pl.ds(pl.multiple_of((s * experts + e) * rows, 16), rows)
                    grad_ref[f, at, :] = grad[f * rows:(f + 1) * rows, e * wide:(e + 1) * wide]
            save(s).start()

        for s in range(4):
            save(s).wait()
        save_last.wait()
    else:
        load_hg.wait()

        @pl.loop(0, d // 256)
        def _(t):
            cols = pl.ds(pl.multiple_of(t * 256, 256), 256)
            grad_ref[cols, :] = t_dot(n2_ref[:, cols], dpre_ref[...]).astype(BF)

        (save_ggu,) = load([(grad_ref, ggu_ref)], lsem, 1)
        save_ggu.wait()
    for copy in ns.early:
        copy.wait_recv()
    ns.finish()


def moe(experts, shards, n2, gs, gu, wd, hid, pre, hg):
    length, de = n2.shape
    d = de - 128
    toks = length // 4
    fc = gu.shape[3]
    ff = experts * fc
    sds = jax.ShapeDtypeStruct
    dma = pltpu.SemaphoreType.DMA
    grad = (shards, (2 * ff + fc) * d // (2 * fc) // shards, 2 * fc) if shards else (d, 2 * ff)
    return pl.pallas_call(
        functools.partial(moe_kernel, experts, shards),
        name="moe",
        out_shape=[sds(grad, BF), sds((4, toks, de), BF), sds((3, toks, de), BF)],
        in_specs=[ANY] * 7,
        out_specs=[ANY, VM, ANY],
        scratch_shapes=[
            pltpu.VMEM((length, de), BF), pltpu.VMEM((length, d), BF), pltpu.VMEM((d, 2 * ff), BF),
            pltpu.VMEM(wd.shape, BF), pltpu.VMEM((length, 2 * ff), F32), pltpu.VMEM((length, ff), BF),
            pltpu.VMEM((length, 2 * ff), BF), pltpu.VMEM(grad, BF), pltpu.VMEM((length, fc), BF),
            dma((2, 6)), dma((6 + 2 * experts,)), dma((4, 4)),
        ],
        compiler_params=pltpu.CompilerParams(collective_id=4, has_side_effects=True, vmem_limit_bytes=60 * MIB),
        cost_estimate=pl.CostEstimate(flops=40 * 10**9, bytes_accessed=60 * 10**6, transcendentals=10**6),
    )(n2, gs, gu, wd, hid, pre, hg)


def rest_kernel(nq, nk, experts, shards, *refs):
    x_ref, g_ref, mixed_ref, gate_ref, n2o_ref, gain_ref, ext_ref = refs[:7]
    n1_hbm, qkv_hbm, attn_hbm, lse_hbm, wqkv_hbm, wo_hbm, dn2_hbm, part_hbm, hg_hbm, wd_hbm = refs[7:17]
    out_ref, gin_ref, refs = refs[17], refs[18], refs[19:]
    if shards:
        gq_ref, gk_ref, gv_ref, gr_ref, gwo_ref = refs[:5]
        refs = refs[5:]
    else:
        gqkv_ref, gwo_ref = refs[:2]
        refs = refs[2:]
    (n1_ref, qkv_ref, attn_ref, lse_ref, wqkv_ref, wo_ref, dn2_ref, nrecv_ref, hg_ref, wd_ref,
     dmixed_ref, dproj_ref, dattn_ref, dqkv_ref, dk_ref, dv_ref, outp_ref, grouter_ref,
     nheld_ref, send_ref, recv_ref, held_ref, orecv_ref, oheld_ref, nsem, psem, dsem, osem, lsem) = refs[:29]
    me = lax.axis_index("seq")
    toks, d = x_ref.shape
    group = nq // nk
    nqkv = nq + 2 * nk
    own = pl.ds(pl.multiple_of(me * toks, toks), toks)
    upper, lower = pl.ds(0, toks // 2), pl.ds(toks // 2, toks // 2)
    early = load([
        (dn2_hbm.at[pl.ds(0, 3)], dn2_ref), (part_hbm.at[2], nrecv_ref.at[2]),
        (part_hbm.at[0, upper], nrecv_ref.at[0, upper]), (part_hbm.at[1, lower], nrecv_ref.at[1, lower]),
    ], lsem)
    next_loads = load([(hg_hbm, hg_ref), (wd_hbm, wd_ref)], lsem, 4)
    late_loads = load([
        (wo_hbm, wo_ref), (attn_hbm, attn_ref), (qkv_hbm, qkv_ref), (lse_hbm, lse_ref), (wqkv_hbm, wqkv_ref),
        (n1_hbm, n1_ref),
    ], lsem, 6)
    if shards:
        wmine, wcross, wbelow, wabove, qmine, qcross, qbelow, qabove, fin_ref, cut_ref, land_ref, wsem, qsem, ssem = refs[29:]
        wc = Collect(wmine, wcross, wbelow, wabove, wsem)
        qc = Collect(qmine, qcross, qbelow, qabove, qsem)
        greet(me, greet_line())
    else:
        greet(me, 0)
    ns = Scatter(me, dn2_ref, nrecv_ref, nheld_ref, nsem, experts, "late")
    os = Scatter(me, outp_ref, orecv_ref, oheld_ref, osem)
    ds = Scatter(me, send_ref, recv_ref, held_ref, dsem)
    for copy in early:
        copy.wait()
    ns.onward()
    for copy in next_loads:
        copy.wait()

    @pl.loop(0, 4)
    def _(step):
        rows = pl.ds(pl.multiple_of(partner(me, step) * toks, toks), toks)
        outp_ref[step] = dot(hg_ref[rows, :], wd_ref[...]).astype(BF)

    total = ns.total()
    os.start(3)
    both = total[:, d:]
    lane = lanes(both.shape)
    dgate = jnp.where(lane < experts, both + pltpu.roll(both, 128 - experts, 1), 0.0)
    gates = gate_ref[...]
    dlog = (gates * (dgate - jnp.sum(gates * dgate, axis=-1, keepdims=True))).astype(BF)
    dn = (total[:, 0:d] + dot_t(dlog, ext_ref[...])) * gain_ref[1:2, :]
    mixed = mixed_ref[...]
    r2 = rms_factor(mixed)
    dmixed = (
        g_ref[...].astype(F32) + r2 * dn - mixed * (r2 * r2 * r2) * jnp.mean(dn * mixed, axis=-1, keepdims=True))
    dmixed_ref[...] = dmixed
    dproj_ref[own, :] = dmixed.astype(BF)
    pg = Gather(me, dproj_ref.at[own], dproj_ref, psem)
    pg.start()
    grouter_ref[...] = pack_two(t_dot(n2o_ref[:, 0:d], dlog), experts)
    for copy in late_loads:
        copy.wait()

    dk_ref[...] = jnp.zeros_like(dk_ref)
    dv_ref[...] = jnp.zeros_like(dv_ref)

    @pl.loop(0, 4)
    def _(step):
        block = partner(me, step)
        rows = pl.ds(pl.multiple_of(block * toks, toks), toks)

        @pl.when(step == 1)
        def _():
            pg.got_one()

        @pl.when(step == 2)
        def _():
            pg.got_two()

        @pl.when(step == 3)
        def _():
            pg.got_three()

            os.start(1)
            os.start(2)
            if shards:
                low = nq // shards
                grad = t_dot(attn_ref[...], dproj_ref[...]).astype(BF)
                for f in range(shards):
                    wmine[f // 2, f % 2] = grad[f * low:(f + 1) * low]
                wc.start()

        dattn_ref[rows, :] = dot_t(dproj_ref[rows, :], wo_ref[...]).astype(BF)
        for b in range(4):

            @pl.when(block == b)
            def _(b=b):
                upto = b * toks
                qrows = slice(upto, upto + toks)
                inside = lax.broadcasted_iota(jnp.int32, (toks, toks), 0) <= lanes((toks, toks))
                for h in range(nq // HEAD_DIM):
                    g = h // group
                    hc = slice(h * HEAD_DIM, (h + 1) * HEAD_DIM)
                    gc = slice(g * HEAD_DIM, (g + 1) * HEAD_DIM)
                    q = qkv_ref[qrows, hc] * SCALE
                    da = dattn_ref[qrows, hc]
                    lse = lse_ref[h:h + 1, qrows]
                    parts = ([slice(0, upto)] if b else []) + [qrows]
                    probs, dprobs = [], []
                    delta = 0.0
                    for krows in parts:
                        k = qkv_ref[krows, nq + g * HEAD_DIM: nq + (g + 1) * HEAD_DIM]
                        v = qkv_ref[krows, nq + nk + g * HEAD_DIM: nq + nk + (g + 1) * HEAD_DIM]
                        p = jnp.exp(dot_t(k, q) - lse)
                        if krows is qrows:
                            p = jnp.where(inside, p, 0.0)
                        dp = dot_t(v, da)
                        delta = delta + jnp.sum(p * dp, axis=0, keepdims=True)
                        probs.append(p)
                        dprobs.append(dp)
                    dq = 0.0
                    for krows, p, dp in zip(parts, probs, dprobs):
                        k = qkv_ref[krows, nq + g * HEAD_DIM: nq + (g + 1) * HEAD_DIM]
                        dsc = (p * (dp - delta)).astype(BF)
                        dq = dq + t_dot(k, dsc)
                        dk_ref[krows, gc] += dot(dsc, q)
                        dv_ref[krows, gc] += dot(p.astype(BF), da)
                    dqkv_ref[qrows, hc] = (dq.T * SCALE).astype(BF)

    dqkv_ref[:, nq:nq + nk] = dk_ref[...].astype(BF)
    dqkv_ref[:, nq + nk:] = dv_ref[...].astype(BF)

    os.onward()
    if shards:
        part = d // 4 // shards

        @pl.loop(0, 4)
        def _(s):
            cols = pl.ds(pl.multiple_of(s * (d // 4), 128), d // 4)
            at = pl.ds(pl.multiple_of(s * part, 16), part)
            grad = t_dot(n1_ref[:, cols], dqkv_ref[...]).astype(BF)
            for f in range(shards):
                qmine[f // 2, f % 2, at, 0:nqkv] = grad[f * part:(f + 1) * part, :]
                of = pl.ds(pl.multiple_of(s * (d // 4) + f * part, 16), part)
                qmine[f // 2, f % 2, at, nqkv:] = grouter_ref[of, :]

        qc.start()
        wc.combine()

    @pl.loop(0, 4)
    def _(turn):
        step = 3 - turn
        block = partner(me, step)
        rows = pl.ds(pl.multiple_of(block * toks, toks), toks)
        send_ref[step] = dot_t(dqkv_ref[rows, :], wqkv_ref[:, 0:nqkv]).astype(BF)
        ds.start(step)

    if shards:
        qc.combine()
        wc.step(0)
        qc.step(0)
        ds.onward()
        wc.step(1)
        qc.step(1)
        wc.step(2)
        qc.step(2)
        qc.total(fin_ref)
        for s in range(4):
            cut_ref[s] = fin_ref[s * part:(s + 1) * part, :].astype(BF)
        spread = Spread(me, lambda c: cut_ref.at[c], land_ref.at[me], ssem, lsem.at[12])
        spread.start()
        wc.total(gwo_ref)
    else:
        ds.onward()

        @pl.loop(0, d // 256)
        def _(t):
            cols = pl.ds(pl.multiple_of(t * 256, 256), 256)
            gqkv_ref[cols, 0:nqkv] = t_dot(n1_ref[:, cols], dqkv_ref[...]).astype(BF)

        gqkv_ref[:, nqkv:] = grouter_ref[...]

        @pl.loop(0, nq // 128)
        def _(t):
            cols = pl.ds(pl.multiple_of(t * 128, 128), 128)
            gwo_ref[cols, :] = t_dot(attn_ref[:, cols], dproj_ref[...]).astype(BF)

    out_ref[...] = (mixed_ref[...] + os.total()).astype(BF)
    dn = ds.total() * gain_ref[0:1, :]
    xf = x_ref[...].astype(F32)
    r1 = rms_factor(xf)
    gin_ref[...] = (
        dmixed_ref[...] + r1 * dn - xf * (r1 * r1 * r1) * jnp.mean(dn * xf, axis=-1, keepdims=True)).astype(BF)
    if shards:
        spread.got()
        router = 0.0
        for s in range(4):
            piece = land_ref[s].astype(F32)
            gq_ref[:, s * nq:(s + 1) * nq] = piece[:, 0:nq]
            gk_ref[:, s * nk:(s + 1) * nk] = piece[:, nq:nq + nk]
            gv_ref[:, s * nk:(s + 1) * nk] = piece[:, nq + nk:nqkv]
            router = router + piece[:, nqkv:]
        gr_ref[...] = router
        spread.finish()
        wc.finish()
        qc.finish()
    pg.finish()
    ns.finish()
    os.finish()
    ds.finish()


def rest(nq, nk, experts, shards, rows, *args):
    toks, d = args[0].shape
    length = 4 * toks
    nqkv = nq + 2 * nk
    wide = nqkv + 128
    sds = jax.ShapeDtypeStruct
    dma = pltpu.SemaphoreType.DMA
    if shards:
        grads = [sds((rows, 4 * nq), F32), sds((rows, 4 * nk), F32), sds((rows, 4 * nk), F32), sds((rows, 128), F32),
                 sds((rows, d), F32)]
        more = [pltpu.VMEM((4, 2, rows, d), BF)] + [pltpu.VMEM((4, rows, d), BF)] * 3
        more += [pltpu.VMEM((4, 2, 4 * rows, wide), BF)] + [pltpu.VMEM((4, 4 * rows, wide), BF)] * 3
        more += [pltpu.VMEM((4 * rows, wide), F32)] + [pltpu.VMEM((4, rows, wide), BF)] * 2
        more += [dma((2, 12)), dma((2, 12)), dma((2, 4))]
    else:
        grads = [sds((d, wide), BF), sds((nq, d), BF)]
        more = []
    half = pltpu.VMEM((2, toks // 2, d), BF)
    blocks, three = pltpu.VMEM((4, toks, d), BF), pltpu.VMEM((3, toks, d), BF)
    return pl.pallas_call(
        functools.partial(rest_kernel, nq, nk, experts, shards),
        name="rest",
        out_shape=[sds((toks, d), BF), sds((toks, d), BF)] + grads,
        in_specs=[VM] * 7 + [ANY] * 10,
        out_specs=[VM] * (2 + len(grads)),
        scratch_shapes=[
            pltpu.VMEM((length, d), BF), pltpu.VMEM((length, nqkv), BF), pltpu.VMEM((length, nq), BF),
            pltpu.VMEM((8, length), F32), pltpu.VMEM((d, wide), BF), pltpu.VMEM((nq, d), BF),
            pltpu.VMEM((3, toks, d + 128), BF), pltpu.VMEM((3, toks, d + 128), BF), pltpu.VMEM(args[15].shape, BF),
            pltpu.VMEM(args[16].shape, BF),
            pltpu.VMEM((toks, d), F32), pltpu.VMEM((length, d), BF), pltpu.VMEM((length, nq), BF),
            pltpu.VMEM((length, nqkv), BF), pltpu.VMEM((length, nk), F32), pltpu.VMEM((length, nk), F32),
            blocks, pltpu.VMEM((d, 128), BF),
            pltpu.VMEM((2, toks // 2, d + 128), BF), blocks, three, half, three, half,
            dma((2, 6)), dma((2, 4)), dma((2, 6)), dma((2, 6)), dma((13,)),
        ] + more,
        compiler_params=pltpu.CompilerParams(collective_id=3, has_side_effects=True, vmem_limit_bytes=63 * MIB),
        cost_estimate=pl.CostEstimate(flops=60 * 10**9, bytes_accessed=80 * 10**6, transcendentals=4 * 10**6),
    )(*args)


def swap_kernel(own_ref, land_ref, ssem, lsem):
    me = lax.axis_index("seq")
    size = land_ref.shape[1]
    greet(me, 0)
    spread = Spread(me, lambda c: own_ref.at[pl.ds(pl.multiple_of(c * size, 16), size)], land_ref.at[me], ssem, lsem.at[0])
    spread.start()
    spread.got()
    spread.finish()


def swap(own, size):
    return pl.pallas_call(
        swap_kernel,
        name="swap",
        out_shape=jax.ShapeDtypeStruct((4, size, own.shape[1]), BF),
        in_specs=[ANY],
        out_specs=ANY,
        scratch_shapes=[pltpu.SemaphoreType.DMA((2, 4)), pltpu.SemaphoreType.DMA((1,))],
        compiler_params=pltpu.CompilerParams(collective_id=5, has_side_effects=True, vmem_limit_bytes=60 * MIB),
    )(own)


def finish_kernel(gu_ref, low_ref, last_ref, out_in, gin_in, gq_ref, gk_ref, gv_ref, gr_ref, gwo_ref, wq_ref, wk_ref, wv_ref,
                  extra_ref, gate_ref, up_ref,
                  out_ref, gin_ref, gone_ref, q_ref, k_ref, v_ref, o_ref, gtwo_ref, r_ref, ggate_ref, gup_ref, gdown_ref):
    for source, target in (
        (out_in, out_ref), (gin_in, gin_ref), (gq_ref, q_ref), (gk_ref, k_ref), (gv_ref, v_ref), (gwo_ref, o_ref)
    ):
        target[...] = source[...]
    experts, rows, _ = gate_ref.shape
    fc = gu_ref.shape[2] // 2
    low, d = gdown_ref.shape[1:]

    def inner(a, b):
        return jnp.sum(a[...].astype(F32) * b[...], axis=-1, keepdims=True)

    extra = extra_ref[...].astype(F32).T[0:rows, :]

    def row(column):
        return jnp.broadcast_to(column, (rows, 128)).T[0:1, :]

    gain = extra[:, experts:experts + 1]
    gone_ref[...] = row((inner(wq_ref, gq_ref) + inner(wk_ref, gk_ref) + inner(wv_ref, gv_ref)) / gain)
    both = gr_ref[...]
    both = both + pltpu.roll(both, 128 - experts, 1)
    r_ref[...] = both.T[0:experts, :]
    router = both[:, 0:experts]
    sums = jnp.sum(extra[:, 0:experts] * router, axis=-1, keepdims=True)
    for e in range(experts):
        for s in range(4):
            piece = gu_ref[s, e * rows:(e + 1) * rows, :].astype(F32)
            ggate_ref[e, :, s * fc:(s + 1) * fc] = piece[:, 0:fc]
            gup_ref[e, :, s * fc:(s + 1) * fc] = piece[:, fc:]
        sums = sums + inner(gate_ref.at[e], ggate_ref.at[e]) + inner(up_ref.at[e], gup_ref.at[e])
    gtwo_ref[...] = row(sums / extra[:, experts + 1:experts + 2])
    parts = d // (2 * fc)
    for e in range(experts):
        source, base = (low_ref, e * parts * low) if e < experts - 1 else (last_ref, 4 * experts * rows)
        for c in range(parts):
            at = base + c * low
            gdown_ref[e, :, c * 2 * fc:(c + 1) * 2 * fc] = source[at:at + low, :].astype(F32)


def finish(*args):
    gu, low, last, out, gin, gq, gk, gv, gr, gwo, wq, wk, wv, extra, gate, up = args
    sds = jax.ShapeDtypeStruct
    rows = gq.shape[0]
    column = sds((1, rows), F32)
    experts = gate.shape[0]
    return pl.pallas_call(
        finish_kernel,
        name="finish",
        out_shape=[
            sds(out.shape, BF), sds(gin.shape, BF), column, sds(gq.shape, F32), sds(gk.shape, F32), sds(gv.shape, F32),
            sds(gwo.shape, F32), column, sds((experts, rows), F32), sds(gate.shape, F32), sds(gate.shape, F32),
            sds((experts, low.size // (experts - 1) // gwo.shape[1], gwo.shape[1]), F32),
        ],
        in_specs=[VM] * 16,
        out_specs=[VM] * 12,
        compiler_params=pltpu.CompilerParams(vmem_limit_bytes=56 * MIB),
        cost_estimate=pl.CostEstimate(flops=10**6, bytes_accessed=12 * 10**6, transcendentals=0),
    )(*args)


def shards(x, cot, routes, gain_attn, w_query, w_key, w_value, w_out, gain_ffn, router, w_gate, w_up, w_down):
    n_seq = lax.axis_size("seq")
    n_fsdp = lax.axis_size("fsdp")
    rows, d = w_query.shape
    experts, ff_rows, _ = w_down.shape
    ff = w_gate.shape[2]
    fc = ff // n_seq

    nq, nk = w_query.shape[1] // n_seq, w_key.shape[1] // n_seq
    nqkv = nq + 2 * nk
    inside = n_seq == 4 and n_fsdp == 8 and rows % 16 == 0 and ff_rows % 16 == 0 and rows <= 128

    extra = jnp.concatenate([router.T, gain_attn[None], gain_ffn[None]], axis=0)
    extra = jnp.pad(extra, ((0, 128 - 2 - experts), (0, max(128 - rows, 0))))
    named = routes[0].T
    if inside:
        (n1, proj, attn, lse, mixed, n2o, gates, gs, gains, ext, wqkv, wo, gu) = front(
            nq, nk, experts, x[0], cot[0], named, (w_query, w_key, w_value, extra, w_gate, w_up, w_out), True)
        gu = gu.reshape(2, experts, d, fc)
        wd = w_down
    else:
        qkv = jnp.concatenate(
            [w_query.reshape(rows, n_seq, -1), w_key.reshape(rows, n_seq, -1), w_value.reshape(rows, n_seq, -1),
             jnp.broadcast_to(extra.T[:rows, None], (rows, n_seq, 128))], axis=2,
        ).transpose(1, 0, 2)
        gu = jnp.stack([w_gate, w_up]).reshape(2, experts, rows, n_seq, fc).transpose(3, 2, 0, 1, 4)
        gu = gu.reshape(n_seq, rows, 2 * experts * fc)
        qkv = lax.all_to_all(qkv, "seq", split_axis=0, concat_axis=0, tiled=True)
        gu = lax.all_to_all(gu, "seq", split_axis=0, concat_axis=0, tiled=True)
        do = jnp.concatenate([w_down.reshape(experts * ff_rows, d), w_out], axis=0)
        wqkv = lax.all_gather(qkv, "fsdp", axis=1).reshape(d, -1)
        do = lax.all_gather(do, "fsdp", axis=0)
        wo = do[:, experts * ff_rows:].reshape(-1, d)
        wd = do[:, : experts * ff_rows].reshape(n_fsdp, experts, ff_rows, d).transpose(1, 0, 2, 3)
        wd = wd.reshape(experts, -1, d)
        gu = lax.all_gather(gu, "fsdp", axis=1).reshape(d, 2, experts, fc).transpose(1, 2, 0, 3)
        (n1, proj, attn, lse, mixed, n2o, gates, gs, gains, ext) = front(
            nq, nk, experts, x[0], cot[0], named, (wqkv, wo), False)

    packed = n_fsdp if inside else 0
    gwd, wd, n2, hg, hid, pre = hidden(experts, packed, n2o, gs, gu, wd)
    if inside:
        gwd = lax.psum_scatter(gwd, "fsdp", scatter_dimension=0, tiled=True)[0]
    else:
        gwd = gwd.reshape(experts, n_fsdp, ff_rows, d).transpose(1, 0, 2, 3).reshape(-1, d)
        gwd = lax.psum_scatter(gwd, "fsdp", scatter_dimension=0, tiled=True).reshape(experts, ff_rows, d)
    ggu, dn2, part = moe(experts, packed, n2, gs, gu, wd, hid, pre, hg)
    if inside:
        ggu, gwd = lax.optimization_barrier((ggu, gwd))
        ggu = lax.psum_scatter(ggu, "fsdp", scatter_dimension=0, tiled=True)[0]
    else:
        ggu = ggu.reshape(n_seq, n_fsdp, rows, experts, 2 * fc).transpose(1, 0, 3, 2, 4)
        ggu = lax.psum_scatter(ggu, "fsdp", scatter_dimension=0, tiled=True).reshape(n_seq, experts * rows, 2 * fc)
    output, gin, *tail = rest(
        nq, nk, experts, packed, rows, x[0], cot[0], mixed, gates, n2o, gains, ext, n1, proj, attn, lse, wqkv, wo, dn2,
        part, hg, wd.reshape(-1, d))
    ggu, tail = lax.optimization_barrier((ggu, tail))
    if inside:
        g_query, g_key, g_value, g_router, gwo = tail
        output, gin, one, g_query, g_key, g_value, gwo, two, g_router, g_gate, g_up, gwd = finish(
            swap(ggu, experts * rows), gwd, ggu, output, gin, g_query, g_key, g_value, g_router, gwo, w_query, w_key, w_value,
            extra, w_gate, w_up)
        return (
            output[None], gin[None], one[0], g_query, g_key, g_value, gwo, two[0], g_router.T, g_gate, g_up, gwd,
        )
    else:
        ggu = lax.all_to_all(ggu, "seq", split_axis=0, concat_axis=0, tiled=True)
        gqkv, gwo = tail
        gwo = lax.psum_scatter(gwo, "fsdp", scatter_dimension=0, tiled=True)
        gqkv = gqkv.reshape(n_seq, n_fsdp, rows, -1).transpose(1, 0, 2, 3).reshape(n_fsdp * n_seq * rows, -1)
        gqkv = lax.psum_scatter(gqkv, "fsdp", scatter_dimension=0, tiled=True).reshape(n_seq, rows, -1)
        gqkv = lax.all_to_all(gqkv, "seq", split_axis=0, concat_axis=0, tiled=True)
        gqkv = gqkv.astype(F32)
        g_query = gqkv[:, :, :nq].transpose(1, 0, 2).reshape(rows, -1)
        g_key = gqkv[:, :, nq: nq + nk].transpose(1, 0, 2).reshape(rows, -1)
        g_value = gqkv[:, :, nq + nk: nqkv].transpose(1, 0, 2).reshape(rows, -1)
        g_router = jnp.sum(gqkv[:, :, nqkv: nqkv + experts] + gqkv[:, :, nqkv + experts: nqkv + 2 * experts], axis=0)
    ggu = ggu.astype(F32).reshape(n_seq, experts, rows, 2, fc).transpose(3, 1, 2, 0, 4).reshape(2, experts, rows, ff)
    g_gate, g_up = ggu[0], ggu[1]
    g_gain_one = (
        jnp.sum(w_query.astype(F32) * g_query, axis=1) + jnp.sum(w_key.astype(F32) * g_key, axis=1)
        + jnp.sum(w_value.astype(F32) * g_value, axis=1)
    ) / gain_attn.astype(F32)
    g_gain_two = (
        jnp.sum(w_gate.astype(F32) * g_gate + w_up.astype(F32) * g_up, axis=(0, 2))
        + jnp.sum(router.astype(F32) * g_router, axis=1)
    ) / gain_ffn.astype(F32)
    return (
        output[None], gin[None], g_gain_one, g_query, g_key, g_value, gwo.astype(F32), g_gain_two, g_router,
        g_gate, g_up, gwd.astype(F32),
    )


def solution(mesh):
    tok = P("fsdp", "seq", None)
    vec = P(("seq", "fsdp"))
    mat = P(("seq", "fsdp"), None)
    exp = P(None, ("seq", "fsdp"), None)
    return jax.shard_map(
        shards,
        mesh=mesh,
        in_specs=(tok, tok, tok, vec, mat, mat, mat, mat, vec, mat, exp, exp, exp),
        out_specs=(tok, tok, vec, mat, mat, mat, mat, vec, mat, exp, exp, exp),
        check_vma=False,
    )
```

```python
import functools

import jax
import jax.numpy as jnp
from jax import lax
from jax.experimental import pallas as pl
from jax.experimental.pallas import tpu as pltpu
from jax.sharding import PartitionSpec as P

HEAD_DIM = 64
EPS = 1e-06
SCALE = HEAD_DIM ** (-0.5)
BF = jnp.bfloat16
F32 = jnp.float32
MESH = pl.DeviceIdType.MESH
ANY = pl.BlockSpec(memory_space=pl.ANY)
VM = pl.BlockSpec(memory_space=pltpu.VMEM)
MIB = 2**20


def dot(a, b):
    return jnp.dot(a, b, preferred_element_type=F32)


def dot_t(a, b):
    return lax.dot_general(a, b, (((1,), (1,)), ((), ())), preferred_element_type=F32)


def t_dot(a, b):
    return lax.dot_general(a, b, (((0,), (0,)), ((), ())), preferred_element_type=F32)


def rms_factor(rows):
    return lax.rsqrt(jnp.mean(rows * rows, axis=-1, keepdims=True) + EPS)


def partner(me, step):
    return ((me // 2 + step // 2) % 2) * 2 + (me % 2 + step % 2) % 2


def send(src, dst, sems, slot, peer):
    return pltpu.make_async_remote_copy(
        src_ref=src, dst_ref=dst, send_sem=sems.at[0, slot], recv_sem=sems.at[1, slot],
        device_id={"seq": peer}, device_id_type=MESH,
    )


def greet(me, others):
    barrier = pltpu.get_barrier_semaphore()
    for step in (1, 2, 3):
        pl.semaphore_signal(barrier, inc=1, device_id={"seq": partner(me, step)}, device_id_type=MESH)
    pl.semaphore_wait(barrier, 3 + others)


class Gather:
    def __init__(self, me, own, buf, sems, base=0):
        rows = own.shape[0]
        half = rows // 2
        one, two = partner(me, 1), partner(me, 2)

        def part(owner, start, size):
            return buf.at[pl.ds(pl.multiple_of(owner * rows + start, half), size)]

        mine = part(me, 0, rows)
        self.first = send(own, mine, sems, base, one)
        self.second = send(own, mine, sems, base + 1, two)
        onward = part(one, 0, half)
        self.third = send(onward, onward, sems, base + 2, two)
        onward = part(two, half, half)
        self.fourth = send(onward, onward, sems, base + 3, one)

    def start(self):
        self.first.start()
        self.second.start()

    def got_one(self):
        self.first.wait_recv()
        self.third.start()

    def got_two(self):
        self.second.wait_recv()
        self.fourth.start()

    def got_three(self):
        self.third.wait_recv()
        self.fourth.wait_recv()

    def finish(self):
        for copy in (self.first, self.second, self.third, self.fourth):
            copy.wait_send()


class Scatter:
    def __init__(self, me, parts, got, held, sems, extra=0, kind="whole"):
        half = parts.shape[1] // 2
        one, two = partner(me, 1), partner(me, 2)
        self.top, self.low = pl.ds(0, half), pl.ds(half, half)
        self.parts, self.got, self.held, self.extra = parts, got, held, extra

        def copy(slot, step, rows, peer, src=None):
            return send(parts.at[step, rows] if src is None else src, got.at[step - 1, rows], sems, slot, peer)

        self.early = self.late = ()
        if kind != "late":
            self.far_top = copy(0, 3, self.top, one)
            self.far_low = copy(1, 3, self.low, two)
            self.one_top = copy(2, 1, self.top, one)
            self.two_low = copy(3, 2, self.low, two)
            self.early = (self.far_top, self.far_low, self.one_top, self.two_low)
        if kind != "early":
            self.one_low = copy(4, 1, self.low, one, held.at[0])
            self.two_top = copy(5, 2, self.top, two, held.at[1])
            self.late = (self.one_low, self.two_top)

    def start(self, step):
        @pl.when(step == 3)
        def _():
            self.far_top.start()
            self.far_low.start()

        pl.when(step == 2)(self.two_low.start)
        pl.when(step == 1)(self.one_top.start)

    def onward(self):
        for slot, step, rows, arrived, copy in ((0, 1, self.low, 1, self.one_low), (1, 2, self.top, 0, self.two_top)):
            if self.early:
                self.early[arrived].wait_recv()
            both = self.parts[step, rows, :].astype(F32) + self.got[2, rows, :].astype(F32)
            self.held[slot] = both.astype(BF)
            if self.extra:
                tail = both[:, -128:]
                whole = tail + pltpu.roll(tail, 128 - self.extra, 1)
                self.held[slot, :, -128:] = pack_two(jnp.where(lanes(tail.shape) < self.extra, whole, 0.0), self.extra)
            copy.start()

    def arrive(self):
        for copy in self.early[2:] + self.late:
            copy.wait_recv()

    def total(self):
        self.arrive()
        return self.parts[0].astype(F32) + self.got[0].astype(F32) + self.got[1].astype(F32)

    def finish(self):
        for copy in self.early + self.late:
            copy.wait_send()


def lanes(shape):
    return lax.broadcasted_iota(jnp.int32, shape, len(shape) - 1)


def pack_two(value, experts):
    high = value.astype(BF).astype(F32)
    low = value - high
    return jnp.where(lanes(value.shape) < experts, high, pltpu.roll(low, experts, 1)).astype(BF)


class Line:
    def __init__(self, region, sems):
        me = lax.axis_index("fsdp")
        self.last = lax.axis_size("fsdp") // 2 - 1
        self.z, self.core = me // 2, me % 2
        self.region, self.sems = region, sems

    def copy(self, slot, plane, core, target):
        part = self.region(plane * 2 + core)
        return pltpu.make_async_remote_copy(
            src_ref=part, dst_ref=part, send_sem=self.sems.at[0, slot], recv_sem=self.sems.at[1, slot],
            device_id={"fsdp": target}, device_id_type=MESH,
        )

    def up(self, hop):
        return self.copy(hop, self.z - hop, self.core, (self.z + 1) * 2 + self.core)

    def from_below(self, hop):
        return self.copy(hop, self.z - 1 - hop, self.core, self.z * 2 + self.core)

    def down(self, hop):
        return self.copy(3 + hop, self.z + hop, self.core, (self.z - 1) * 2 + self.core)

    def from_above(self, hop):
        return self.copy(3 + hop, self.z + 1 + hop, self.core, self.z * 2 + self.core)

    def across(self, plane):
        return self.copy(6 + plane, plane, self.core, self.z * 2 + 1 - self.core)

    def from_across(self, plane):
        return self.copy(6 + plane, plane, 1 - self.core, self.z * 2 + self.core)

    def start(self):
        pl.when(self.z < self.last)(lambda: self.up(0).start())
        pl.when(self.z > 0)(lambda: self.down(0).start())
        self.across(self.z).start()

    def step(self, hop):
        @pl.when(self.z > hop)
        def _():
            self.from_below(hop).wait_recv()
            if hop < 2:
                pl.when(self.z < self.last)(lambda: self.up(hop + 1).start())
            self.across(self.z - 1 - hop).start()

        @pl.when(self.z + hop < self.last)
        def _():
            self.from_above(hop).wait_recv()
            if hop < 2:
                pl.when(self.z > 0)(lambda: self.down(hop + 1).start())
            self.across(self.z + 1 + hop).start()

    def land(self):
        for plane in range(4):
            self.from_across(plane).wait_recv()

    def finish(self):
        for hop in range(3):
            pl.when((self.z >= hop) & (self.z < self.last))(lambda hop=hop: self.up(hop).wait_send())
            pl.when((self.z + hop <= self.last) & (self.z > 0))(lambda hop=hop: self.down(hop).wait_send())
        for plane in range(4):
            self.across(plane).wait_send()


class Collect:
    def __init__(self, mine, cross, below, above, sems):
        me = lax.axis_index("fsdp")
        self.z, self.core = me // 2, me % 2
        self.mine, self.cross, self.below, self.above, self.sems = mine, cross, below, above, sems

    def copy(self, slot, src, dst, target):
        return pltpu.make_async_remote_copy(
            src_ref=src, dst_ref=dst, send_sem=self.sems.at[0, slot], recv_sem=self.sems.at[1, slot],
            device_id={"fsdp": target}, device_id_type=MESH,
        )

    def over(self, plane):
        return self.copy(plane, self.mine.at[plane, 1 - self.core], self.cross.at[plane], self.z * 2 + 1 - self.core)

    def up(self, plane, src):
        return self.copy(4 + plane, src.at[plane], self.below.at[plane], (self.z + 1) * 2 + self.core)

    def down(self, plane, src):
        return self.copy(8 + plane, src.at[plane], self.above.at[plane], (self.z - 1) * 2 + self.core)

    def start(self):
        for plane in range(4):
            self.over(plane).start()

    def combine(self):
        for plane in (3, 0, 2, 1):
            self.over(plane).wait_recv()
            both = self.mine[plane, self.core].astype(F32) + self.cross[plane].astype(F32)
            self.cross[plane] = both.astype(BF)

            if plane == 3:
                pl.when(self.z == 0)(self.up(3, self.cross).start)
            if plane == 0:
                pl.when(self.z == 3)(self.down(0, self.cross).start)

    def step(self, turn):
        high, low = 3 - turn, turn
        z = self.z

        if turn < 2:

            @pl.when(z == 0)
            def _():
                self.up(high, self.cross).wait_send()
                self.up(high - 1, self.cross).start()

            @pl.when(z == 3)
            def _():
                self.down(low, self.cross).wait_send()
                self.down(low + 1, self.cross).start()

        @pl.when((z > 0) & (z <= high))
        def _():
            self.up(high, self.below).wait_recv()

        @pl.when((z > 0) & (z < high))
        def _():
            self.below[high] = (self.below[high].astype(F32) + self.cross[high].astype(F32)).astype(BF)
            self.up(high, self.below).start()

        @pl.when((z < 3) & (z >= low))
        def _():
            self.down(low, self.above).wait_recv()

        @pl.when((z < 3) & (z > low))
        def _():
            self.above[low] = (self.above[low].astype(F32) + self.cross[low].astype(F32)).astype(BF)
            self.down(low, self.above).start()

    def total(self, out):
        z = self.z
        out[...] = self.cross[z].astype(F32)

        @pl.when(z > 0)
        def _():
            out[...] += self.below[z].astype(F32)

        @pl.when(z < 3)
        def _():
            out[...] += self.above[z].astype(F32)

    def finish(self):
        z = self.z
        for plane in range(4):
            self.over(plane).wait_send()
            pl.when((z > 0) & (z < 3) & (z < plane))(self.up(plane, self.below).wait_send)
            pl.when((z > 0) & (z < 3) & (z > plane))(self.down(plane, self.above).wait_send)
        pl.when(z == 0)(self.up(1, self.cross).wait_send)
        pl.when(z == 3)(self.down(2, self.cross).wait_send)


def load(pairs, sems, first=0):
    copies = [pltpu.make_async_copy(a, b, sems.at[first + i]) for i, (a, b) in enumerate(pairs)]
    for copy in copies:
        copy.start()
    return copies


def greet_line():
    me = lax.axis_index("fsdp")
    last = lax.axis_size("fsdp") // 2 - 1
    z, core = me // 2, me % 2
    barrier = pltpu.get_barrier_semaphore()

    @pl.when(z < last)
    def _():
        pl.semaphore_signal(barrier, inc=1, device_id={"fsdp": me + 2}, device_id_type=MESH)

    @pl.when(z > 0)
    def _():
        pl.semaphore_signal(barrier, inc=1, device_id={"fsdp": me - 2}, device_id_type=MESH)

    pl.semaphore_signal(barrier, inc=1, device_id={"fsdp": z * 2 + 1 - core}, device_id_type=MESH)
    return 1 + jnp.minimum(z, 1) + jnp.minimum(last - z, 1)


class Spread:
    def __init__(self, me, chunk, place, sems, local):
        self.copies = [send(chunk(partner(me, step)), place, sems, step, partner(me, step)) for step in (3, 2, 1)]
        self.local = pltpu.make_async_copy(chunk(me), place, local)

    def start(self):
        self.local.start()
        for copy in self.copies:
            copy.start()

    def got(self):
        self.local.wait()
        for copy in self.copies:
            copy.wait_recv()

    def finish(self):
        for copy in self.copies:
            copy.wait_send()


def front_kernel(nq, nk, experts, inside, *refs):
    if inside:
        (x_ref, g_ref, named_ref, query_own, key_own, value_own, extra_wide, gate_own, up_own, woo_ref,
         n1_out, qkv_out, attn_out, lse_ref, mixed_ref, n2_ref, gate_ref, gs_ref, gain_ref, ext_ref, wqkv_out, wo_out,
         gu_ref, n1_ref, qkv_ref, attn_ref, vsem, wqkv_ref, wo_ref, extra_own,
         cols_ref, xs_ref, send_ref, recv_ref, held_ref, xsem, gsem, asem, lsem, qw_ref, spread_sem, line_sem) = refs
    else:
        (x_ref, g_ref, named_ref, wqkv_ref, wo_ref,
         n1_out, qkv_out, attn_out, lse_ref, mixed_ref, n2_ref, gate_ref, gs_ref, gain_ref, ext_ref,
         n1_ref, qkv_ref, attn_ref, vsem,
         cols_ref, xs_ref, send_ref, recv_ref, held_ref, xsem, gsem, asem, lsem) = refs
    me = lax.axis_index("seq")
    toks, d = x_ref.shape
    group = nq // nk
    nqkv = nq + 2 * nk
    xg = Gather(me, x_ref, xs_ref, xsem)
    gg = Gather(me, g_ref, gs_ref, gsem)
    keep = pltpu.make_async_copy(g_ref, gs_ref.at[pl.ds(pl.multiple_of(me * toks, toks), toks)], lsem.at[0])
    keep.start()
    ao = Scatter(me, send_ref, recv_ref, held_ref, asem)
    if inside:
        shard = lax.axis_index("fsdp")
        rows = woo_ref.shape[0]
        extra_own[...] = extra_wide[...].astype(F32).T[0:rows, :].astype(BF)
        greet(me, greet_line())
        qkv_line = Line(lambda f: qw_ref.at[:, f], line_sem.at[0])
        wo_line = Line(lambda f: wo_ref.at[pl.ds(pl.multiple_of(f * rows, 16), rows)], line_sem.at[1])
        gu_line = Line(lambda f: gu_ref.at[:, :, :, f], line_sem.at[2])
        spreads = []

        def spread(own, width, place):
            def chunk(c):
                cols = pl.ds(pl.multiple_of(c * width, 128), width)
                return own.at[:, cols] if len(own.shape) == 2 else own.at[:, :, cols]

            at = len(spreads)
            spreads.append(Spread(me, chunk if width else lambda c: own, place, spread_sem.at[at], lsem.at[2 + at]))

        spread(query_own, nq, qw_ref.at[me, shard, :, pl.ds(0, nq)])
        spread(key_own, nk, qw_ref.at[me, shard, :, pl.ds(nq, nk)])
        spread(value_own, nk, qw_ref.at[me, shard, :, pl.ds(nq + nk, nk)])
        spread(extra_own, 0, qw_ref.at[me, shard, :, pl.ds(nqkv, 128)])
        spread(gate_own, gate_own.shape[2] // 4, gu_ref.at[0, :, me, shard])
        spread(up_own, gate_own.shape[2] // 4, gu_ref.at[1, :, me, shard])
        place_wo = pltpu.make_async_copy(woo_ref, wo_line.region(shard), lsem.at[1])
        for one in spreads[:4]:
            one.start()
        place_wo.start()
        xg.start()
        for one in spreads[4:]:
            one.start()
        for one in spreads[:4]:
            one.got()
        qkv_line.start()
        place_wo.wait()
        xs_ref[pl.ds(pl.multiple_of(me * toks, toks), toks), :] = x_ref[...]
        qkv_line.step(0)
        qkv_line.step(1)
        wo_line.start()
        xg.got_one()
        xg.got_two()
        qkv_line.step(2)
        for one in spreads[4:]:
            one.got()
        gu_line.start()
        wo_line.step(0)
        qkv_line.land()
        wo_line.step(1)
        xg.got_three()
        gg.start()
        for s in range(4):
            for f in range(8):
                wqkv_ref[s * 8 * rows + f * rows: s * 8 * rows + (f + 1) * rows, :] = qw_ref[s, f]
    else:
        greet(me, 0)
        xg.start()
        xs_ref[pl.ds(pl.multiple_of(me * toks, toks), toks), :] = x_ref[...]
        xg.got_one()
        xg.got_two()
        xg.got_three()
        gg.start()
    ext = wqkv_ref[:, nqkv:]
    ext_ref[...] = ext
    gain_ref[...] = ext.astype(F32).T[experts:experts + 2, :]
    gain1 = gain_ref[0:1, :]
    cols_ref[...] = jnp.zeros_like(cols_ref)

    @pl.loop(0, 4)
    def _(block):
        rows = pl.ds(pl.multiple_of(block * toks, toks), toks)
        xf = xs_ref[rows, :].astype(F32)
        n1_ref[rows, :] = (xf * rms_factor(xf) * gain1).astype(BF)
        proj = dot(n1_ref[rows, :], wqkv_ref[:, 0:nqkv]).astype(BF)
        qkv_ref[rows, :] = proj

    saves = load([(n1_ref, n1_out), (qkv_ref, qkv_out)], vsem)
    if inside:
        wo_line.step(2)
        gu_line.step(0)
        wo_line.land()
        saves += load([(wqkv_ref, wqkv_out), (wo_ref, wo_out)], vsem, 3)

    @pl.loop(0, 4)
    def _(turn):
        step = 3 - turn
        block = partner(me, step)
        rows = pl.ds(pl.multiple_of(block * toks, toks), toks)

        for b in range(4):

            @pl.when(block == b)
            def _(b=b):
                upto = b * toks
                qrows = slice(upto, upto + toks)
                inside = lanes((toks, toks)) <= lax.broadcasted_iota(jnp.int32, (toks, toks), 0)
                for h in range(nq // HEAD_DIM):
                    g = h // group
                    q = qkv_ref[qrows, h * HEAD_DIM:(h + 1) * HEAD_DIM] * SCALE
                    kc = slice(nq + g * HEAD_DIM, nq + (g + 1) * HEAD_DIM)
                    vc = slice(nq + nk + g * HEAD_DIM, nq + nk + (g + 1) * HEAD_DIM)
                    near = jnp.where(inside, dot_t(q, qkv_ref[qrows, kc]), -1e30)
                    top = jnp.max(near, axis=-1, keepdims=True)
                    if b:
                        far = dot_t(q, qkv_ref[0:upto, kc])
                        top = jnp.maximum(top, jnp.max(far, axis=-1, keepdims=True))
                    near = jnp.exp(near - top)
                    total = jnp.sum(near, axis=-1, keepdims=True)
                    if b:
                        far = jnp.exp(far - top)
                        total = total + jnp.sum(far, axis=-1, keepdims=True)
                    inv = 1.0 / total
                    res = dot((near * inv).astype(BF), qkv_ref[qrows, vc])
                    if b:
                        res = res + dot((far * inv).astype(BF), qkv_ref[0:upto, vc])
                    attn_ref[qrows, h * HEAD_DIM:(h + 1) * HEAD_DIM] = res.astype(BF)
                    cols_ref[qrows, h:h + 1] = top + jnp.log(total)

        send_ref[step] = dot(attn_ref[rows, :], wo_ref[...]).astype(BF)

        ao.start(step)

    saves += load([(attn_ref, attn_out)], vsem, 2)
    ao.onward()
    gg.got_one()
    gg.got_two()
    lse_ref[...] = cols_ref[...].T[0:8, :]
    if inside:
        gu_line.step(1)
    mixed = x_ref[...].astype(F32) + ao.total()
    if inside:
        gu_line.step(2)
    mixed_ref[...] = mixed
    n2 = (mixed * rms_factor(mixed) * gain_ref[1:2, :]).astype(BF)
    n2_ref[:, 0:d] = n2
    logits = dot(n2, ext_ref[...])
    expert = lax.broadcasted_iota(jnp.int32, (128, toks), 0)
    hit = (expert == named_ref[0:1, :]) | (expert == named_ref[1:2, :])
    named = jnp.where(hit, 1.0, 0.0).T > 0.0
    top = jnp.max(jnp.where(named, logits, -1e30), axis=-1, keepdims=True)
    weight = jnp.where(named, jnp.exp(jnp.minimum(logits - top, 0.0)), 0.0)
    gates = weight / jnp.sum(weight, axis=-1, keepdims=True)
    gate_ref[...] = gates
    n2_ref[:, d:] = pack_two(gates, experts)
    gg.got_three()
    gg.finish()
    xg.finish()
    keep.wait()
    for copy in saves:
        copy.wait()
    ao.finish()
    if inside:
        gu_line.land()
        for line in (qkv_line, wo_line, gu_line):
            line.finish()
        for one in spreads:
            one.finish()


def front(nq, nk, experts, x, g, named, weights, inside):
    toks, d = x.shape
    length = 4 * toks
    nqkv = nq + 2 * nk
    sds = jax.ShapeDtypeStruct
    out_shape = [
        sds((length, d), BF), sds((length, nqkv), BF), sds((length, nq), BF), sds((8, length), F32),
        sds((toks, d), F32), sds((toks, d + 128), BF), sds((toks, 128), F32), sds((length, d), BF),
        sds((2, d), F32), sds((d, 128), BF),
    ]
    in_specs = [VM] * 5
    out_specs = [ANY] * 3 + [VM] * 4 + [ANY] + [VM] * 2
    scratch = [
        pltpu.VMEM((length, d), BF), pltpu.VMEM((length, nqkv), BF), pltpu.VMEM((length, nq), BF),
        pltpu.SemaphoreType.DMA((5,)),
    ]
    if inside:
        scratch += [
            pltpu.VMEM((d, nqkv + 128), BF), pltpu.VMEM((nq, d), BF), pltpu.VMEM((weights[0].shape[0], 128), BF)]
    scratch += [
        pltpu.VMEM((length, 128), F32), pltpu.VMEM((length, d), BF), pltpu.VMEM((4, toks, d), BF),
        pltpu.VMEM((3, toks, d), BF), pltpu.VMEM((2, toks // 2, d), BF),
        pltpu.SemaphoreType.DMA((2, 4)), pltpu.SemaphoreType.DMA((2, 4)), pltpu.SemaphoreType.DMA((2, 6)),
        pltpu.SemaphoreType.DMA((8,)),
    ]
    if inside:
        query, key, value, extra, gate, up, woo = weights
        rows, fc = query.shape[0], gate.shape[2] // 4
        in_specs = [VM] * 3 + [ANY] * 3 + [VM] + [ANY] * 3
        out_shape += [sds((d, nqkv + 128), BF), sds((nq, d), BF), sds((2, experts, 4, 8, rows, fc), BF)]
        out_specs += [ANY, ANY, ANY]
        scratch += [
            pltpu.VMEM((4, 8, rows, nqkv + 128), BF), pltpu.SemaphoreType.DMA((6, 2, 4)),
            pltpu.SemaphoreType.DMA((3, 2, 10)),
        ]
    return pl.pallas_call(
        functools.partial(front_kernel, nq, nk, experts, inside),
        name="front",
        out_shape=out_shape,
        in_specs=in_specs,
        out_specs=out_specs,
        scratch_shapes=scratch,
        compiler_params=pltpu.CompilerParams(collective_id=1, has_side_effects=True, vmem_limit_bytes=60 * MIB),
        cost_estimate=pl.CostEstimate(flops=20 * 10**9, bytes_accessed=60 * 10**6, transcendentals=4 * 10**6),
    )(x, g, named, *weights)


def hidden_kernel(experts, shards, *refs):
    (n2o_ref, gs_hbm, gu_hbm, wd_hbm, gwd_ref, wd_out, n2_out, hg_out, hid_out, pre_out,
     n2_ref, gs_ref, gu_ref, wd_ref, pre_ref, hid_ref, hg_ref, grad_ref, nsem, lsem, ssem) = refs[:21]
    me = lax.axis_index("seq")
    toks, de = n2o_ref.shape
    d = de - 128
    length, ff = hg_ref.shape
    fc = ff // experts
    load_gu = load(
        [(gu_hbm.at[m, e], gu_ref.at[:, pl.ds((2 * e + m) * fc, fc)]) for e in range(experts) for m in range(2)], lsem, 6)
    (load_gs,) = load([(gs_hbm, gs_ref)], lsem, 1)
    if shards:
        (wsem,) = refs[21:]
        wd_line = Line(lambda f: wd_ref.at[:, f], wsem)
        (load_wd,) = load([(wd_hbm, wd_ref.at[:, lax.axis_index("fsdp")])], lsem, 2)
        greet(me, greet_line())
        load_wd.wait()
        wd_line.start()
    else:
        (load_wd,) = load([(wd_hbm, wd_ref)], lsem, 2)
        greet(me, 0)
        load_wd.wait()
    ng = Gather(me, n2o_ref, n2_ref, nsem)
    ng.start()
    for copy in load_gu:
        copy.wait()

    def gate_of(rows, e):
        packed = n2_ref[rows, d:].astype(F32)
        lane = lanes(packed.shape)
        return jnp.sum(jnp.where((lane == e) | (lane == e + experts), packed, 0.0), axis=-1, keepdims=True)

    def saves(step):
        rows = pl.ds(pl.multiple_of(partner(me, step) * toks, toks), toks)
        return [
            pltpu.make_async_copy(a.at[rows], b.at[rows], ssem.at[i, step])
            for i, (a, b) in enumerate(((hg_ref, hg_out), (hid_ref, hid_out), (pre_ref, pre_out), (n2_ref, n2_out)))
        ]

    @pl.loop(0, 4)
    def _(step):
        block = partner(me, step)
        rows = pl.ds(pl.multiple_of(block * toks, toks), toks)

        @pl.when(step == 0)
        def _():
            n2_ref[rows, :] = n2o_ref[...]

        @pl.when(step == 1)
        def _():
            if shards:
                wd_line.step(0)
            ng.got_one()

        @pl.when(step == 2)
        def _():
            ng.got_two()
            if shards:
                wd_line.step(1)

        @pl.when(step == 3)
        def _():
            ng.got_three()
            if shards:
                wd_line.step(2)

        @pl.loop(0, experts)
        def _(e):
            cols = pl.ds(pl.multiple_of(e * 2 * fc, 2 * fc), 2 * fc)
            hcols = pl.ds(pl.multiple_of(e * fc, fc), fc)
            pre = dot(n2_ref[rows, 0:d], gu_ref[:, cols])
            gp, up = pre[:, 0:fc], pre[:, fc:]
            sig = 1.0 / (1.0 + jnp.exp(-gp))
            act = gp * sig
            hid = (act * up).astype(BF)
            hid_ref[rows, hcols] = hid
            hg_ref[rows, hcols] = (gate_of(rows, e) * hid.astype(F32)).astype(BF)
            pre_ref[rows, pl.ds(pl.multiple_of(e * 2 * fc, fc), fc)] = up * sig * (1.0 + gp * (1.0 - sig))
            pre_ref[rows, pl.ds(pl.multiple_of(e * 2 * fc + fc, fc), fc)] = act

        for copy in saves(step):
            copy.start()

    load_gs.wait()
    if shards:
        low, wide = fc // shards, 2 * fc
        parts = d // wide

        @pl.loop(0, experts - 1)
        def _(e):
            cols = pl.ds(pl.multiple_of(e * fc, fc), fc)
            grad = t_dot(hg_ref[:, cols], gs_ref[...]).astype(BF)
            for f in range(shards):
                for c in range(parts):
                    at = pl.ds(pl.multiple_of((e * parts + c) * low, 16), low)
                    grad_ref[f, at, :] = grad[f * low:(f + 1) * low, c * wide:(c + 1) * wide]

        wd_line.land()
    else:

        @pl.loop(0, experts)
        def _(e):
            cols = pl.ds(pl.multiple_of(e * fc, fc), fc)
            grad_ref[cols, :] = t_dot(hg_ref[:, cols], gs_ref[...]).astype(BF)

    last = load([(grad_ref, gwd_ref), (wd_ref, wd_out)], lsem, 3)
    for step in range(4):
        for copy in saves(step):
            copy.wait()
    for copy in last:
        copy.wait()
    ng.finish()
    if shards:
        wd_line.finish()


def hidden(experts, shards, n2o, gs, gu, wd):
    toks, de = n2o.shape
    d = de - 128
    length = 4 * toks
    fc = gu.shape[3]
    ff = experts * fc
    sds = jax.ShapeDtypeStruct
    dma = pltpu.SemaphoreType.DMA
    whole = (experts, shards, fc // shards, d) if shards else (experts, fc, d)
    grad = (shards, (ff - fc) * d // (2 * fc) // shards, 2 * fc) if shards else (ff, d)
    return pl.pallas_call(
        functools.partial(hidden_kernel, experts, shards),
        name="hidden",
        out_shape=[
            sds(grad, BF), sds(whole, BF), sds((length, de), BF), sds((length, ff), BF), sds((length, ff), BF),
            sds((length, 2 * ff), F32),
        ],
        in_specs=[VM] + [ANY] * 3,
        out_specs=[ANY] * 6,
        scratch_shapes=[
            pltpu.VMEM((length, de), BF), pltpu.VMEM((length, d), BF), pltpu.VMEM((d, 2 * ff), BF),
            pltpu.VMEM(whole, BF), pltpu.VMEM((length, 2 * ff), F32), pltpu.VMEM((length, ff), BF),
            pltpu.VMEM((length, ff), BF), pltpu.VMEM(grad, BF),
            dma((2, 4)), dma((6 + 2 * experts,)), dma((4, 4)),
        ] + ([dma((2, 10))] if shards else []),
        compiler_params=pltpu.CompilerParams(collective_id=2, has_side_effects=True, vmem_limit_bytes=60 * MIB),
        cost_estimate=pl.CostEstimate(flops=20 * 10**9, bytes_accessed=50 * 10**6, transcendentals=4 * 10**6),
    )(n2o, gs, gu, wd)


def moe_kernel(experts, shards, n2_hbm, gs_hbm, gu_hbm, wd_hbm, hid_hbm, pre_hbm, hg_hbm, ggu_ref, dn2_out, part_ref,
               dn2_ref, outsem, n2_ref, gs_ref, gu_ref, wd_ref, pre_ref, hid_ref, dpre_ref, grad_ref, hg_ref, dsem, lsem, bsem):
    me = lax.axis_index("seq")
    length, d = gs_ref.shape
    toks = length // 4
    ff = hid_ref.shape[1]
    fc = ff // experts
    (load_wd,) = load([(wd_hbm, wd_ref)], lsem, 0)

    def blocks(step):
        rows = pl.ds(pl.multiple_of(partner(me, step) * toks, toks), toks)
        return [
            pltpu.make_async_copy(a.at[rows], b.at[rows], bsem.at[i, step])
            for i, (a, b) in enumerate(((n2_hbm, n2_ref), (gs_hbm, gs_ref), (hid_hbm, hid_ref), (pre_hbm, pre_ref)))
        ]

    for copy in blocks(3):
        copy.start()
    load_gu = load(
        [(gu_hbm.at[m, e], gu_ref.at[:, pl.ds((2 * e + m) * fc, fc)]) for e in range(experts) for m in range(2)], lsem, 6)
    for step in (2, 1, 0):
        for copy in blocks(step):
            copy.start()
    (load_hg,) = load([(hg_hbm.at[:, pl.ds(ff - fc, fc)], hg_ref)], lsem, 5)
    greet(me, 0)
    ns = Scatter(me, dn2_ref, part_ref, None, dsem, experts, "early")
    load_wd.wait()

    @pl.loop(0, 4)
    def _(turn):
        step = 3 - turn
        rows = pl.ds(pl.multiple_of(partner(me, step) * toks, toks), toks)
        for copy in blocks(step):
            copy.wait()

        def one_expert(e, dgate):
            hcols = pl.ds(pl.multiple_of(e * fc, fc), fc)
            left = pl.ds(pl.multiple_of(e * 2 * fc, fc), fc)
            right = pl.ds(pl.multiple_of(e * 2 * fc + fc, fc), fc)
            packed = n2_ref[rows, d:].astype(F32)
            lane = lanes(packed.shape)
            gate = jnp.sum(jnp.where((lane == e) | (lane == e + experts), packed, 0.0), axis=-1, keepdims=True)
            dh0 = dot_t(gs_ref[rows, :], wd_ref[e].reshape(fc, d))
            dh = gate * dh0
            dpre_ref[rows, left] = (dh * pre_ref[rows, left]).astype(BF)
            dpre_ref[rows, right] = (dh * pre_ref[rows, right]).astype(BF)
            sums = jnp.sum(hid_ref[rows, hcols].astype(F32) * dh0, axis=-1, keepdims=True)
            return dgate + jnp.where(lane == e, sums, 0.0)

        dgate = lax.fori_loop(0, experts, one_expert, jnp.zeros((toks, 128), F32), unroll=True)
        dn2_ref[step, :, d:] = pack_two(dgate, experts)

        @pl.when(turn == 0)
        def _():
            for copy in load_gu:
                copy.wait()

        tile = 512

        @pl.loop(0, d // tile)
        def _(t):
            cols = pl.ds(pl.multiple_of(t * tile, tile), tile)
            dn2_ref[step, :, cols] = dot_t(dpre_ref[rows, :], gu_ref[cols, :]).astype(BF)

        ns.start(step)
        pltpu.make_async_copy(dn2_ref.at[step], dn2_out.at[step], outsem.at[step]).start()

    if shards:
        rows, wide = d // 4 // shards, 2 * fc

        def save(s):
            part = pl.ds(pl.multiple_of(s * experts * rows, 16), experts * rows)
            return pltpu.make_async_copy(grad_ref.at[:, part], ggu_ref.at[:, part], lsem.at[1 + s])

        low, parts = fc // shards, d // wide
        base = 4 * experts * rows
        load_hg.wait()
        grad = t_dot(hg_ref[...], gs_ref[...]).astype(BF)
        for f in range(shards):
            for c in range(parts):
                at = base + c * low
                grad_ref[f, at:at + low, :] = grad[f * low:(f + 1) * low, c * wide:(c + 1) * wide]
        rest_part = pl.ds(base, parts * low)
        (save_last,) = load([(grad_ref.at[:, rest_part], ggu_ref.at[:, rest_part])], lsem, 0)

        @pl.loop(0, 4)
        def _(s):
            cols = pl.ds(pl.multiple_of(s * (d // 4), 128), d // 4)
            grad = t_dot(n2_ref[:, cols], dpre_ref[...]).astype(BF)
            for f in range(shards):
                for e in range(experts):
                    at = pl.ds(pl.multiple_of((s * experts + e) * rows, 16), rows)
                    grad_ref[f, at, :] = grad[f * rows:(f + 1) * rows, e * wide:(e + 1) * wide]
            save(s).start()

        for s in range(4):
            save(s).wait()
        save_last.wait()
    else:
        load_hg.wait()

        @pl.loop(0, d // 256)
        def _(t):
            cols = pl.ds(pl.multiple_of(t * 256, 256), 256)
            grad_ref[cols, :] = t_dot(n2_ref[:, cols], dpre_ref[...]).astype(BF)

        (save_ggu,) = load([(grad_ref, ggu_ref)], lsem, 1)
        save_ggu.wait()
    for step in range(4):
        pltpu.make_async_copy(dn2_ref.at[step], dn2_out.at[step], outsem.at[step]).wait()
    for copy in ns.early:
        copy.wait_recv()
    ns.finish()


def moe(experts, shards, n2, gs, gu, wd, hid, pre, hg):
    length, de = n2.shape
    d = de - 128
    toks = length // 4
    fc = gu.shape[3]
    ff = experts * fc
    sds = jax.ShapeDtypeStruct
    dma = pltpu.SemaphoreType.DMA
    grad = (shards, (2 * ff + fc) * d // (2 * fc) // shards, 2 * fc) if shards else (d, 2 * ff)
    return pl.pallas_call(
        functools.partial(moe_kernel, experts, shards),
        name="moe",
        out_shape=[sds(grad, BF), sds((4, toks, de), BF), sds((3, toks, de), BF)],
        in_specs=[ANY] * 7,
        out_specs=[ANY] * 3,
        scratch_shapes=[
            pltpu.VMEM((4, toks, de), BF), dma((4,)),
            pltpu.VMEM((length, de), BF), pltpu.VMEM((length, d), BF), pltpu.VMEM((d, 2 * ff), BF),
            pltpu.VMEM(wd.shape, BF), pltpu.VMEM((length, 2 * ff), F32), pltpu.VMEM((length, ff), BF),
            pltpu.VMEM((length, 2 * ff), BF), pltpu.VMEM(grad, BF), pltpu.VMEM((length, fc), BF),
            dma((2, 6)), dma((6 + 2 * experts,)), dma((4, 4)),
        ],
        compiler_params=pltpu.CompilerParams(collective_id=4, has_side_effects=True, vmem_limit_bytes=60 * MIB),
        cost_estimate=pl.CostEstimate(flops=40 * 10**9, bytes_accessed=60 * 10**6, transcendentals=10**6),
    )(n2, gs, gu, wd, hid, pre, hg)


def rest_kernel(nq, nk, experts, shards, *refs):
    x_ref, g_ref, mixed_ref, gate_ref, n2o_ref, gain_ref, ext_ref = refs[:7]
    n1_hbm, qkv_hbm, attn_hbm, lse_hbm, wqkv_hbm, wo_hbm, dn2_hbm, part_hbm, hg_hbm, wd_hbm = refs[7:17]
    out_ref, gin_ref, refs = refs[17], refs[18], refs[19:]
    if shards:
        gq_ref, gk_ref, gv_ref, gr_ref, gwo_ref = refs[:5]
        refs = refs[5:]
    else:
        gqkv_ref, gwo_ref = refs[:2]
        refs = refs[2:]
    (n1_ref, qkv_ref, attn_ref, lse_ref, wqkv_ref, wo_ref, dn2_ref, nrecv_ref, hg_ref, wd_ref,
     dmixed_ref, dproj_ref, dattn_ref, dqkv_ref, dk_ref, dv_ref, outp_ref, grouter_ref,
     nheld_ref, send_ref, recv_ref, held_ref, orecv_ref, oheld_ref, nsem, psem, dsem, osem, lsem) = refs[:29]
    me = lax.axis_index("seq")
    toks, d = x_ref.shape
    group = nq // nk
    nqkv = nq + 2 * nk
    own = pl.ds(pl.multiple_of(me * toks, toks), toks)
    upper, lower = pl.ds(0, toks // 2), pl.ds(toks // 2, toks // 2)
    early = load([
        (dn2_hbm.at[pl.ds(0, 3)], dn2_ref), (part_hbm.at[2], nrecv_ref.at[2]),
        (part_hbm.at[0, upper], nrecv_ref.at[0, upper]), (part_hbm.at[1, lower], nrecv_ref.at[1, lower]),
    ], lsem)
    next_loads = load([(hg_hbm, hg_ref), (wd_hbm, wd_ref)], lsem, 4)
    late_loads = load([
        (wo_hbm, wo_ref), (attn_hbm, attn_ref), (qkv_hbm, qkv_ref), (lse_hbm, lse_ref), (wqkv_hbm, wqkv_ref),
        (n1_hbm, n1_ref),
    ], lsem, 6)
    if shards:
        wmine, wcross, wbelow, wabove, qmine, qcross, qbelow, qabove, fin_ref, cut_ref, land_ref, wsem, qsem, ssem = refs[29:]
        wc = Collect(wmine, wcross, wbelow, wabove, wsem)
        qc = Collect(qmine, qcross, qbelow, qabove, qsem)
        greet(me, greet_line())
    else:
        greet(me, 0)
    ns = Scatter(me, dn2_ref, nrecv_ref, nheld_ref, nsem, experts, "late")
    os = Scatter(me, outp_ref, orecv_ref, oheld_ref, osem)
    ds = Scatter(me, send_ref, recv_ref, held_ref, dsem)
    for copy in early:
        copy.wait()
    ns.onward()
    for copy in next_loads:
        copy.wait()

    @pl.loop(0, 4)
    def _(step):
        rows = pl.ds(pl.multiple_of(partner(me, step) * toks, toks), toks)
        outp_ref[step] = dot(hg_ref[rows, :], wd_ref[...]).astype(BF)

    total = ns.total()
    os.start(3)
    both = total[:, d:]
    lane = lanes(both.shape)
    dgate = jnp.where(lane < experts, both + pltpu.roll(both, 128 - experts, 1), 0.0)
    gates = gate_ref[...]
    dlog = (gates * (dgate - jnp.sum(gates * dgate, axis=-1, keepdims=True))).astype(BF)
    dn = (total[:, 0:d] + dot_t(dlog, ext_ref[...])) * gain_ref[1:2, :]
    mixed = mixed_ref[...]
    r2 = rms_factor(mixed)
    dmixed = (
        g_ref[...].astype(F32) + r2 * dn - mixed * (r2 * r2 * r2) * jnp.mean(dn * mixed, axis=-1, keepdims=True))
    dmixed_ref[...] = dmixed
    dproj_ref[own, :] = dmixed.astype(BF)
    pg = Gather(me, dproj_ref.at[own], dproj_ref, psem)
    pg.start()
    grouter_ref[...] = pack_two(t_dot(n2o_ref[:, 0:d], dlog), experts)
    for copy in late_loads:
        copy.wait()

    dk_ref[...] = jnp.zeros_like(dk_ref)
    dv_ref[...] = jnp.zeros_like(dv_ref)

    @pl.loop(0, 4)
    def _(step):
        block = partner(me, step)
        rows = pl.ds(pl.multiple_of(block * toks, toks), toks)

        @pl.when(step == 1)
        def _():
            pg.got_one()

        @pl.when(step == 2)
        def _():
            pg.got_two()

        @pl.when(step == 3)
        def _():
            pg.got_three()

            os.start(1)
            os.start(2)
            if shards:
                low = nq // shards
                grad = t_dot(attn_ref[...], dproj_ref[...]).astype(BF)
                for f in range(shards):
                    wmine[f // 2, f % 2] = grad[f * low:(f + 1) * low]
                wc.start()

        dattn_ref[rows, :] = dot_t(dproj_ref[rows, :], wo_ref[...]).astype(BF)
        for b in range(4):

            @pl.when(block == b)
            def _(b=b):
                upto = b * toks
                qrows = slice(upto, upto + toks)
                inside = lax.broadcasted_iota(jnp.int32, (toks, toks), 0) <= lanes((toks, toks))
                for h in range(nq // HEAD_DIM):
                    g = h // group
                    hc = slice(h * HEAD_DIM, (h + 1) * HEAD_DIM)
                    gc = slice(g * HEAD_DIM, (g + 1) * HEAD_DIM)
                    q = qkv_ref[qrows, hc] * SCALE
                    da = dattn_ref[qrows, hc]
                    lse = lse_ref[h:h + 1, qrows]
                    parts = ([slice(0, upto)] if b else []) + [qrows]
                    probs, dprobs = [], []
                    delta = 0.0
                    for krows in parts:
                        k = qkv_ref[krows, nq + g * HEAD_DIM: nq + (g + 1) * HEAD_DIM]
                        v = qkv_ref[krows, nq + nk + g * HEAD_DIM: nq + nk + (g + 1) * HEAD_DIM]
                        p = jnp.exp(dot_t(k, q) - lse)
                        if krows is qrows:
                            p = jnp.where(inside, p, 0.0)
                        dp = dot_t(v, da)
                        delta = delta + jnp.sum(p * dp, axis=0, keepdims=True)
                        probs.append(p)
                        dprobs.append(dp)
                    dq = 0.0
                    for krows, p, dp in zip(parts, probs, dprobs):
                        k = qkv_ref[krows, nq + g * HEAD_DIM: nq + (g + 1) * HEAD_DIM]
                        dsc = (p * (dp - delta)).astype(BF)
                        dq = dq + t_dot(k, dsc)
                        dk_ref[krows, gc] += dot(dsc, q)
                        dv_ref[krows, gc] += dot(p.astype(BF), da)
                    dqkv_ref[qrows, hc] = (dq.T * SCALE).astype(BF)

    dqkv_ref[:, nq:nq + nk] = dk_ref[...].astype(BF)
    dqkv_ref[:, nq + nk:] = dv_ref[...].astype(BF)

    os.onward()
    if shards:
        part = d // 4 // shards

        @pl.loop(0, 4)
        def _(s):
            cols = pl.ds(pl.multiple_of(s * (d // 4), 128), d // 4)
            at = pl.ds(pl.multiple_of(s * part, 16), part)
            grad = t_dot(n1_ref[:, cols], dqkv_ref[...]).astype(BF)
            for f in range(shards):
                qmine[f // 2, f % 2, at, 0:nqkv] = grad[f * part:(f + 1) * part, :]
                of = pl.ds(pl.multiple_of(s * (d // 4) + f * part, 16), part)
                qmine[f // 2, f % 2, at, nqkv:] = grouter_ref[of, :]

        qc.start()
        wc.combine()

    @pl.loop(0, 4)
    def _(turn):
        step = 3 - turn
        block = partner(me, step)
        rows = pl.ds(pl.multiple_of(block * toks, toks), toks)
        send_ref[step] = dot_t(dqkv_ref[rows, :], wqkv_ref[:, 0:nqkv]).astype(BF)
        ds.start(step)

    if shards:
        qc.combine()
        wc.step(0)
        qc.step(0)
        ds.onward()
        wc.step(1)
        qc.step(1)
        wc.step(2)
        qc.step(2)
        qc.total(fin_ref)
        for s in range(4):
            cut_ref[s] = fin_ref[s * part:(s + 1) * part, :].astype(BF)
        spread = Spread(me, lambda c: cut_ref.at[c], land_ref.at[me], ssem, lsem.at[12])
        spread.start()
        wc.total(gwo_ref)
    else:
        ds.onward()

        @pl.loop(0, d // 256)
        def _(t):
            cols = pl.ds(pl.multiple_of(t * 256, 256), 256)
            gqkv_ref[cols, 0:nqkv] = t_dot(n1_ref[:, cols], dqkv_ref[...]).astype(BF)

        gqkv_ref[:, nqkv:] = grouter_ref[...]

        @pl.loop(0, nq // 128)
        def _(t):
            cols = pl.ds(pl.multiple_of(t * 128, 128), 128)
            gwo_ref[cols, :] = t_dot(attn_ref[:, cols], dproj_ref[...]).astype(BF)

    out_ref[...] = (mixed_ref[...] + os.total()).astype(BF)
    dn = ds.total() * gain_ref[0:1, :]
    xf = x_ref[...].astype(F32)
    r1 = rms_factor(xf)
    gin_ref[...] = (
        dmixed_ref[...] + r1 * dn - xf * (r1 * r1 * r1) * jnp.mean(dn * xf, axis=-1, keepdims=True)).astype(BF)
    if shards:
        spread.got()
        router = 0.0
        for s in range(4):
            piece = land_ref[s].astype(F32)
            gq_ref[:, s * nq:(s + 1) * nq] = piece[:, 0:nq]
            gk_ref[:, s * nk:(s + 1) * nk] = piece[:, nq:nq + nk]
            gv_ref[:, s * nk:(s + 1) * nk] = piece[:, nq + nk:nqkv]
            router = router + piece[:, nqkv:]
        gr_ref[...] = router
        spread.finish()
        wc.finish()
        qc.finish()
    pg.finish()
    ns.finish()
    os.finish()
    ds.finish()


def rest(nq, nk, experts, shards, rows, *args):
    toks, d = args[0].shape
    length = 4 * toks
    nqkv = nq + 2 * nk
    wide = nqkv + 128
    sds = jax.ShapeDtypeStruct
    dma = pltpu.SemaphoreType.DMA
    if shards:
        grads = [sds((rows, 4 * nq), F32), sds((rows, 4 * nk), F32), sds((rows, 4 * nk), F32), sds((rows, 128), F32),
                 sds((rows, d), F32)]
        more = [pltpu.VMEM((4, 2, rows, d), BF)] + [pltpu.VMEM((4, rows, d), BF)] * 3
        more += [pltpu.VMEM((4, 2, 4 * rows, wide), BF)] + [pltpu.VMEM((4, 4 * rows, wide), BF)] * 3
        more += [pltpu.VMEM((4 * rows, wide), F32)] + [pltpu.VMEM((4, rows, wide), BF)] * 2
        more += [dma((2, 12)), dma((2, 12)), dma((2, 4))]
    else:
        grads = [sds((d, wide), BF), sds((nq, d), BF)]
        more = []
    half = pltpu.VMEM((2, toks // 2, d), BF)
    blocks, three = pltpu.VMEM((4, toks, d), BF), pltpu.VMEM((3, toks, d), BF)
    return pl.pallas_call(
        functools.partial(rest_kernel, nq, nk, experts, shards),
        name="rest",
        out_shape=[sds((toks, d), BF), sds((toks, d), BF)] + grads,
        in_specs=[VM] * 7 + [ANY] * 10,
        out_specs=[VM] * (2 + len(grads)),
        scratch_shapes=[
            pltpu.VMEM((length, d), BF), pltpu.VMEM((length, nqkv), BF), pltpu.VMEM((length, nq), BF),
            pltpu.VMEM((8, length), F32), pltpu.VMEM((d, wide), BF), pltpu.VMEM((nq, d), BF),
            pltpu.VMEM((3, toks, d + 128), BF), pltpu.VMEM((3, toks, d + 128), BF), pltpu.VMEM(args[15].shape, BF),
            pltpu.VMEM(args[16].shape, BF),
            pltpu.VMEM((toks, d), F32), pltpu.VMEM((length, d), BF), pltpu.VMEM((length, nq), BF),
            pltpu.VMEM((length, nqkv), BF), pltpu.VMEM((length, nk), F32), pltpu.VMEM((length, nk), F32),
            blocks, pltpu.VMEM((d, 128), BF),
            pltpu.VMEM((2, toks // 2, d + 128), BF), blocks, three, half, three, half,
            dma((2, 6)), dma((2, 4)), dma((2, 6)), dma((2, 6)), dma((13,)),
        ] + more,
        compiler_params=pltpu.CompilerParams(collective_id=3, has_side_effects=True, vmem_limit_bytes=63 * MIB),
        cost_estimate=pl.CostEstimate(flops=60 * 10**9, bytes_accessed=80 * 10**6, transcendentals=4 * 10**6),
    )(*args)


def swap_kernel(own_ref, land_ref, ssem, lsem):
    me = lax.axis_index("seq")
    size = land_ref.shape[1]
    greet(me, 0)
    spread = Spread(me, lambda c: own_ref.at[pl.ds(pl.multiple_of(c * size, 16), size)], land_ref.at[me], ssem, lsem.at[0])
    spread.start()
    spread.got()
    spread.finish()


def swap(own, size):
    return pl.pallas_call(
        swap_kernel,
        name="swap",
        out_shape=jax.ShapeDtypeStruct((4, size, own.shape[1]), BF),
        in_specs=[ANY],
        out_specs=ANY,
        scratch_shapes=[pltpu.SemaphoreType.DMA((2, 4)), pltpu.SemaphoreType.DMA((1,))],
        compiler_params=pltpu.CompilerParams(collective_id=5, has_side_effects=True, vmem_limit_bytes=60 * MIB),
    )(own)


def finish_kernel(gu_ref, low_ref, last_ref, out_in, gin_in, gq_ref, gk_ref, gv_ref, gr_ref, gwo_ref, wq_ref, wk_ref, wv_ref,
                  extra_ref, gate_ref, up_ref,
                  out_ref, gin_ref, gone_ref, q_ref, k_ref, v_ref, o_ref, gtwo_ref, r_ref, ggate_ref, gup_ref, gdown_ref):
    for source, target in (
        (out_in, out_ref), (gin_in, gin_ref), (gq_ref, q_ref), (gk_ref, k_ref), (gv_ref, v_ref), (gwo_ref, o_ref)
    ):
        target[...] = source[...]
    experts, rows, _ = gate_ref.shape
    fc = gu_ref.shape[2] // 2
    low, d = gdown_ref.shape[1:]

    def inner(a, b):
        return jnp.sum(a[...].astype(F32) * b[...], axis=-1, keepdims=True)

    extra = extra_ref[...].astype(F32).T[0:rows, :]

    def row(column):
        return jnp.broadcast_to(column, (rows, 128)).T[0:1, :]

    gain = extra[:, experts:experts + 1]
    gone_ref[...] = row((inner(wq_ref, gq_ref) + inner(wk_ref, gk_ref) + inner(wv_ref, gv_ref)) / gain)
    both = gr_ref[...]
    both = both + pltpu.roll(both, 128 - experts, 1)
    r_ref[...] = both.T[0:experts, :]
    router = both[:, 0:experts]
    sums = jnp.sum(extra[:, 0:experts] * router, axis=-1, keepdims=True)
    for e in range(experts):
        for s in range(4):
            piece = gu_ref[s, e * rows:(e + 1) * rows, :].astype(F32)
            ggate_ref[e, :, s * fc:(s + 1) * fc] = piece[:, 0:fc]
            gup_ref[e, :, s * fc:(s + 1) * fc] = piece[:, fc:]
        sums = sums + inner(gate_ref.at[e], ggate_ref.at[e]) + inner(up_ref.at[e], gup_ref.at[e])
    gtwo_ref[...] = row(sums / extra[:, experts + 1:experts + 2])
    parts = d // (2 * fc)
    for e in range(experts):
        source, base = (low_ref, e * parts * low) if e < experts - 1 else (last_ref, 4 * experts * rows)
        for c in range(parts):
            at = base + c * low
            gdown_ref[e, :, c * 2 * fc:(c + 1) * 2 * fc] = source[at:at + low, :].astype(F32)


def finish(*args):
    gu, low, last, out, gin, gq, gk, gv, gr, gwo, wq, wk, wv, extra, gate, up = args
    sds = jax.ShapeDtypeStruct
    rows = gq.shape[0]
    column = sds((1, rows), F32)
    experts = gate.shape[0]
    return pl.pallas_call(
        finish_kernel,
        name="finish",
        out_shape=[
            sds(out.shape, BF), sds(gin.shape, BF), column, sds(gq.shape, F32), sds(gk.shape, F32), sds(gv.shape, F32),
            sds(gwo.shape, F32), column, sds((experts, rows), F32), sds(gate.shape, F32), sds(gate.shape, F32),
            sds((experts, low.size // (experts - 1) // gwo.shape[1], gwo.shape[1]), F32),
        ],
        in_specs=[VM] * 16,
        out_specs=[VM] * 12,
        compiler_params=pltpu.CompilerParams(vmem_limit_bytes=56 * MIB),
        cost_estimate=pl.CostEstimate(flops=10**6, bytes_accessed=12 * 10**6, transcendentals=0),
    )(*args)


def shards(x, cot, routes, gain_attn, w_query, w_key, w_value, w_out, gain_ffn, router, w_gate, w_up, w_down):
    n_seq = lax.axis_size("seq")
    n_fsdp = lax.axis_size("fsdp")
    rows, d = w_query.shape
    experts, ff_rows, _ = w_down.shape
    ff = w_gate.shape[2]
    fc = ff // n_seq

    nq, nk = w_query.shape[1] // n_seq, w_key.shape[1] // n_seq
    nqkv = nq + 2 * nk
    inside = n_seq == 4 and n_fsdp == 8 and rows % 16 == 0 and ff_rows % 16 == 0 and rows <= 128

    extra = jnp.concatenate([router.T, gain_attn[None], gain_ffn[None]], axis=0)
    extra = jnp.pad(extra, ((0, 128 - 2 - experts), (0, max(128 - rows, 0))))
    named = routes[0].T
    if inside:
        (n1, proj, attn, lse, mixed, n2o, gates, gs, gains, ext, wqkv, wo, gu) = front(
            nq, nk, experts, x[0], cot[0], named, (w_query, w_key, w_value, extra, w_gate, w_up, w_out), True)
        gu = gu.reshape(2, experts, d, fc)
        wd = w_down
    else:
        qkv = jnp.concatenate(
            [w_query.reshape(rows, n_seq, -1), w_key.reshape(rows, n_seq, -1), w_value.reshape(rows, n_seq, -1),
             jnp.broadcast_to(extra.T[:rows, None], (rows, n_seq, 128))], axis=2,
        ).transpose(1, 0, 2)
        gu = jnp.stack([w_gate, w_up]).reshape(2, experts, rows, n_seq, fc).transpose(3, 2, 0, 1, 4)
        gu = gu.reshape(n_seq, rows, 2 * experts * fc)
        qkv = lax.all_to_all(qkv, "seq", split_axis=0, concat_axis=0, tiled=True)
        gu = lax.all_to_all(gu, "seq", split_axis=0, concat_axis=0, tiled=True)
        do = jnp.concatenate([w_down.reshape(experts * ff_rows, d), w_out], axis=0)
        wqkv = lax.all_gather(qkv, "fsdp", axis=1).reshape(d, -1)
        do = lax.all_gather(do, "fsdp", axis=0)
        wo = do[:, experts * ff_rows:].reshape(-1, d)
        wd = do[:, : experts * ff_rows].reshape(n_fsdp, experts, ff_rows, d).transpose(1, 0, 2, 3)
        wd = wd.reshape(experts, -1, d)
        gu = lax.all_gather(gu, "fsdp", axis=1).reshape(d, 2, experts, fc).transpose(1, 2, 0, 3)
        (n1, proj, attn, lse, mixed, n2o, gates, gs, gains, ext) = front(
            nq, nk, experts, x[0], cot[0], named, (wqkv, wo), False)

    packed = n_fsdp if inside else 0
    gwd, wd, n2, hg, hid, pre = hidden(experts, packed, n2o, gs, gu, wd)
    if inside:
        gwd = lax.psum_scatter(gwd, "fsdp", scatter_dimension=0, tiled=True)[0]
    else:
        gwd = gwd.reshape(experts, n_fsdp, ff_rows, d).transpose(1, 0, 2, 3).reshape(-1, d)
        gwd = lax.psum_scatter(gwd, "fsdp", scatter_dimension=0, tiled=True).reshape(experts, ff_rows, d)
    ggu, dn2, part = moe(experts, packed, n2, gs, gu, wd, hid, pre, hg)
    if inside:
        ggu, gwd = lax.optimization_barrier((ggu, gwd))
        ggu = lax.psum_scatter(ggu, "fsdp", scatter_dimension=0, tiled=True)[0]
    else:
        ggu = ggu.reshape(n_seq, n_fsdp, rows, experts, 2 * fc).transpose(1, 0, 3, 2, 4)
        ggu = lax.psum_scatter(ggu, "fsdp", scatter_dimension=0, tiled=True).reshape(n_seq, experts * rows, 2 * fc)
    output, gin, *tail = rest(
        nq, nk, experts, packed, rows, x[0], cot[0], mixed, gates, n2o, gains, ext, n1, proj, attn, lse, wqkv, wo, dn2,
        part, hg, wd.reshape(-1, d))
    ggu, tail = lax.optimization_barrier((ggu, tail))
    if inside:
        g_query, g_key, g_value, g_router, gwo = tail
        output, gin, one, g_query, g_key, g_value, gwo, two, g_router, g_gate, g_up, gwd = finish(
            swap(ggu, experts * rows), gwd, ggu, output, gin, g_query, g_key, g_value, g_router, gwo, w_query, w_key, w_value,
            extra, w_gate, w_up)
        return (
            output[None], gin[None], one[0], g_query, g_key, g_value, gwo, two[0], g_router.T, g_gate, g_up, gwd,
        )
    else:
        ggu = lax.all_to_all(ggu, "seq", split_axis=0, concat_axis=0, tiled=True)
        gqkv, gwo = tail
        gwo = lax.psum_scatter(gwo, "fsdp", scatter_dimension=0, tiled=True)
        gqkv = gqkv.reshape(n_seq, n_fsdp, rows, -1).transpose(1, 0, 2, 3).reshape(n_fsdp * n_seq * rows, -1)
        gqkv = lax.psum_scatter(gqkv, "fsdp", scatter_dimension=0, tiled=True).reshape(n_seq, rows, -1)
        gqkv = lax.all_to_all(gqkv, "seq", split_axis=0, concat_axis=0, tiled=True)
        gqkv = gqkv.astype(F32)
        g_query = gqkv[:, :, :nq].transpose(1, 0, 2).reshape(rows, -1)
        g_key = gqkv[:, :, nq: nq + nk].transpose(1, 0, 2).reshape(rows, -1)
        g_value = gqkv[:, :, nq + nk: nqkv].transpose(1, 0, 2).reshape(rows, -1)
        g_router = jnp.sum(gqkv[:, :, nqkv: nqkv + experts] + gqkv[:, :, nqkv + experts: nqkv + 2 * experts], axis=0)
    ggu = ggu.astype(F32).reshape(n_seq, experts, rows, 2, fc).transpose(3, 1, 2, 0, 4).reshape(2, experts, rows, ff)
    g_gate, g_up = ggu[0], ggu[1]
    g_gain_one = (
        jnp.sum(w_query.astype(F32) * g_query, axis=1) + jnp.sum(w_key.astype(F32) * g_key, axis=1)
        + jnp.sum(w_value.astype(F32) * g_value, axis=1)
    ) / gain_attn.astype(F32)
    g_gain_two = (
        jnp.sum(w_gate.astype(F32) * g_gate + w_up.astype(F32) * g_up, axis=(0, 2))
        + jnp.sum(router.astype(F32) * g_router, axis=1)
    ) / gain_ffn.astype(F32)
    return (
        output[None], gin[None], g_gain_one, g_query, g_key, g_value, gwo.astype(F32), g_gain_two, g_router,
        g_gate, g_up, gwd.astype(F32),
    )


def solution(mesh):
    tok = P("fsdp", "seq", None)
    vec = P(("seq", "fsdp"))
    mat = P(("seq", "fsdp"), None)
    exp = P(None, ("seq", "fsdp"), None)
    return jax.shard_map(
        shards,
        mesh=mesh,
        in_specs=(tok, tok, tok, vec, mat, mat, mat, mat, vec, mat, exp, exp, exp),
        out_specs=(tok, tok, vec, mat, mat, mat, mat, vec, mat, exp, exp, exp),
        check_vma=False,
    )
```
